32 devices in a mesh: head: 2 (over x), seq: 16 (over z, y, core).
Axes of the slice: x: 2, y: 2, z: 4, core: 2. Of those that a mesh axis runs over, the one named last changes fastest.
Arguments:
- tokens: bfloat16 [16384, 4096], P('seq')
- qkv_weight: bfloat16 [4096, 1536], P('seq', 'head'), may hold values from -0.09375 to 0.09375
- out_weight: bfloat16 [512, 4096], P('head', 'seq'), may hold values from -0.25 to 0.25
- centroids: float32 [4, 64, 128], P('head', 'seq'), may hold values from -6 to 6
- clusters: int32 [4, 128], P('head', 'seq'), may hold values from 0 to 63, as said below
- slots: int32 [4, 128], P('head', 'seq'), may hold values from 0 to 1, as said below
Outputs:
- output: bfloat16 [4096, 16384], P('head', 'seq')
- new_centroids: float32 [4, 64, 128], P('head', 'seq')
The draws below stay inside these ranges and needn't reach their ends.
Inputs may be any that keep to these rules, and one draw needn't show every extreme that they name: `clusters`: for each head at most 2 tiles name one cluster, and in each head every cluster of some owner holds 2 tiles; the owner of cluster c is the index c // 4 of seq. A tile of head h from the index s of seq names an owner o with s + o - h divisible by 2. The tiles of one index of seq, over the 2 heads of one index of head, name pairwise different owners. Tiles of one head naming the same cluster have different slots.
All inputs are finite; a program needn't handle non-finite values.
Results may differ from the reference program's by a relative error of at most 0.017.
Values may be sent and summed in bfloat16 or wider, within the bound.
No kernel may reach another device: no remote copies, remote signals or barrier semaphores. Data moves between devices by JAX's collectives and lax.ppermute only.
A program may use at most 128 MiB of HBM per device.

```python
import math
import jax
import jax.numpy as jnp
from jax import lax

D = 4096
HEAD_WIDTH = 128
HEAD_DEV = 2
TILE = 128
CAP = 2
TOK_DEV = 1024
HEADS = 4
CLUS_DEV = 4
CLUSTERS = 64
TOKENS = 16384
NT = 128
N_HEAD = 2
N_SEQ = 16


def routing_tables(key):
    key = jax.random.fold_in(key, 11)
    first_key, second_key, third_key, fourth_key = jax.random.split(key, 4)
    members = N_SEQ // HEAD_DEV
    tiles_dev = TOK_DEV // TILE
    local_head = jnp.arange(HEADS, dtype=jnp.int32) % HEAD_DEV
    source = jnp.arange(N_SEQ, dtype=jnp.int32)
    full_owner = jax.random.randint(first_key, (HEADS,), 0, N_SEQ)
    full_owner = jnp.where(jnp.arange(HEADS, dtype=jnp.int32) == 0, N_SEQ - 1, full_owner).astype(jnp.int32)
    residue = (local_head[:, None] - source[None, :]) % HEAD_DEV
    ranking = jax.random.randint(second_key, (HEADS, N_SEQ, members), 0, 1 << 20) * members + jnp.arange(members, dtype=jnp.int32)
    holds_full = residue == (full_owner % HEAD_DEV)[:, None]
    is_full = holds_full[:, :, None] & (jnp.arange(members, dtype=jnp.int32)[None, None, :] == (full_owner // HEAD_DEV)[:, None, None])
    ranking = jnp.where(is_full, 1 << 30, ranking)
    unused, chosen = lax.top_k(ranking, tiles_dev)
    shuffle = jnp.argsort(jax.random.randint(third_key, (HEADS, N_SEQ, tiles_dev), 0, 1 << 20) * tiles_dev + jnp.arange(tiles_dev, dtype=jnp.int32), axis=-1)
    chosen = jnp.take_along_axis(chosen, shuffle, axis=-1)
    owner = residue[:, :, None] + HEAD_DEV * chosen
    sigma = jnp.argsort(jax.random.randint(fourth_key, (HEADS, N_SEQ, members), 0, 1 << 20) * members + jnp.arange(members, dtype=jnp.int32), axis=-1)
    source_rank = (source // HEAD_DEV)[None, :, None]
    flat_index = (owner * members + source_rank).reshape(HEADS, N_SEQ * tiles_dev)
    placed = jnp.take_along_axis(sigma.reshape(HEADS, N_SEQ * members), flat_index, axis=1)
    cluster_ids = owner.reshape(HEADS, N_SEQ * tiles_dev) * CLUS_DEV + placed // CAP
    slot_ids = placed % CAP
    return (cluster_ids.astype(jnp.int32), slot_ids.astype(jnp.int32))


def draw_clusters(key, part):
    return routing_tables(key)[0]


def draw_slots(key, part):
    return routing_tables(key)[1]


def draw_tokens(key, part):
    key = jax.random.fold_in(key, 5)
    first_key, second_key, third_key, fourth_key = jax.random.split(key, 4)
    noise = jax.random.normal(first_key, (TOKENS, D), jnp.float32)
    common = jax.random.normal(second_key, (TOKENS // TILE, D), jnp.float32)
    row_scale = jnp.exp(jax.random.uniform(third_key, (TOKENS, 1), jnp.float32) * math.log(10.0))
    column_scale = jnp.exp(jax.random.uniform(fourth_key, (1, D), jnp.float32) * math.log(10.0))
    values = (noise + jnp.repeat(common, TILE, axis=0)) * row_scale * column_scale
    return values.astype(jnp.bfloat16)


def block_scale(stream_key, dims, shards, least, largest):
    loudness = 1.0
    for dim, shards_of in shards:
        draws = jax.random.uniform(jax.random.fold_in(jax.random.fold_in(stream_key, 6), dim), (shards_of,), jnp.float32, least / len(shards), largest / len(shards))
        loudness = loudness * jnp.repeat(jnp.exp(draws), dims[dim] // shards_of).reshape((-1,) + (1,) * (len(dims) - 1 - dim))
    return loudness


def scatter_about(stream_key, extent, deviation, most, pieces=(), held_as=jnp.bfloat16):
    level = block_scale(stream_key, extent, pieces, -0.22, 0.18) if pieces else 1.0
    result = jax.random.normal(stream_key, extent, jnp.float32) * deviation * level
    return jnp.minimum(jnp.maximum(result, -most), most).astype(held_as)


def setup_inputs(seed: int = 0) -> dict:
    streams_of = jax.random.split(jax.random.key(seed), 7)
    return {
        "tokens": draw_tokens(jax.random.fold_in(streams_of[6], 71), 0),
        "qkv_weight": scatter_about(streams_of[1], (D, HEADS * 3 * HEAD_WIDTH), D ** -0.5, 0.09375, ((0, 16), (1, 2))),
        "out_weight": scatter_about(streams_of[2], (HEADS * HEAD_WIDTH, D), (HEADS * HEAD_WIDTH) ** -0.5, 0.25, ((0, 2), (1, 16))),
        "centroids": scatter_about(streams_of[3], (HEADS, CLUSTERS, HEAD_WIDTH), 1.0, 6.0, ((0, 2), (1, 16)), jnp.float32),
        "clusters": draw_clusters(jax.random.fold_in(streams_of[6], 71), 0),
        "slots": draw_slots(jax.random.fold_in(streams_of[6], 71), 0),
    }


LOGIT_SCALE = 8.0
KEEP_RATE = 0.75

def unit_rows(values, epsilon):
    return values * lax.rsqrt(lax.optimization_barrier(jnp.mean(values * values, axis=-1, keepdims=True)) + epsilon)

def cluster_attention(normalized_query, normalized_key, value_matrix, token_live, position):
    attention_logits = LOGIT_SCALE / HEAD_WIDTH * jnp.einsum('tra,tla->trl', normalized_query.astype(jnp.float32), normalized_key.astype(jnp.float32))
    span_rows = normalized_query.shape[1]
    diagonal = jnp.arange(span_rows)[:, None] == jnp.arange(span_rows)[None, :]
    allowed = (token_live[:, None, :] > 0) & (position[:, None, :] <= position[:, :, None]) | diagonal[None]
    exp_scores = jnp.where(allowed, jnp.exp(attention_logits), 0.0)
    attention_probs = (exp_scores / lax.optimization_barrier(jnp.sum(exp_scores, axis=-1, keepdims=True))).astype(jnp.bfloat16)
    return jnp.einsum('xjs,xsv->xjv', attention_probs.astype(jnp.float32), value_matrix.astype(jnp.float32)).astype(jnp.bfloat16)

def update_centroids(centroid_rows, key_float, token_live, tiles_held):
    key_sums = lax.optimization_barrier(jnp.sum(key_float * token_live[:, :, None], axis=1))
    counts = tiles_held * TILE
    means = key_sums / jnp.maximum(counts, 1.0)[:, None]
    return centroid_rows + (1.0 - KEEP_RATE) * jnp.where(counts[:, None] > 0, means - centroid_rows, 0.0)

def head_pass(packed):
    qkv_head, cluster_ids, slot_ids, centroid_rows = packed
    slot_index = (cluster_ids * CAP + slot_ids).astype(jnp.int32)
    total_slots = CLUSTERS * CAP
    buffer = jnp.zeros((total_slots, TILE, 3, HEAD_WIDTH), jnp.bfloat16).at[slot_index].set(qkv_head)
    occupied = jnp.zeros((total_slots,), jnp.float32).at[slot_index].set(1.0)
    tile_of = jnp.zeros((total_slots,), jnp.int32).at[slot_index].set(jnp.arange(NT, dtype=jnp.int32))
    cluster_grouped_rows = buffer.reshape(CLUSTERS, CAP * TILE, 3, HEAD_WIDTH)
    token_live = jnp.repeat(occupied.reshape(CLUSTERS, CAP), TILE, axis=1)
    position = (tile_of.reshape(CLUSTERS, CAP, 1) * TILE + jnp.arange(TILE, dtype=jnp.int32)[None, None, :]).reshape(CLUSTERS, CAP * TILE)
    normalized_query = unit_rows(cluster_grouped_rows[:, :, 0].astype(jnp.float32), 1e-06).astype(jnp.bfloat16)
    key_float = unit_rows(cluster_grouped_rows[:, :, 1].astype(jnp.float32), 1e-06)
    normalized_key = key_float.astype(jnp.bfloat16)
    attended = cluster_attention(normalized_query, normalized_key, cluster_grouped_rows[:, :, 2], token_live, position)
    gathered_back = attended.reshape(total_slots, TILE, HEAD_WIDTH)[slot_index]
    tiles_held = lax.optimization_barrier(jnp.sum(occupied.reshape(CLUSTERS, CAP), axis=1))
    new_rows = update_centroids(centroid_rows, key_float, token_live, tiles_held)
    return (gathered_back, new_rows)

def add_group(running, packed):
    group_attention, group_weight = packed
    partial_value = jnp.dot(group_weight.T, group_attention.T, preferred_element_type=jnp.float32).astype(jnp.bfloat16)
    partial_value = lax.optimization_barrier(partial_value)
    return (running + partial_value.astype(jnp.float32), None)

def reference(tokens, qkv_weight, out_weight, centroids, clusters, slots):
    normed = unit_rows(tokens.astype(jnp.float32), 1e-05).astype(jnp.bfloat16)
    projected = jnp.dot(normed, qkv_weight, preferred_element_type=jnp.float32).astype(jnp.bfloat16)
    per_head = projected.reshape(NT, TILE, HEADS, 3, HEAD_WIDTH).transpose(2, 0, 1, 3, 4)
    attended, new_centroids = lax.map(head_pass, (per_head, clusters, slots, centroids))
    attention = attended.transpose(1, 2, 0, 3).reshape(TOKENS, HEADS * HEAD_WIDTH)
    group_width = HEADS * HEAD_WIDTH // N_HEAD
    grouped_attention = attention.reshape(TOKENS, N_HEAD, group_width).transpose(1, 0, 2)
    grouped_weight = out_weight.reshape(N_HEAD, group_width, D)
    running, unused = lax.scan(add_group, jnp.zeros((D, TOKENS), jnp.float32), (grouped_attention, grouped_weight))
    return (running.astype(jnp.bfloat16), new_centroids)
```

```python
import functools

import jax
import jax.numpy as jnp
from jax import lax
from jax.experimental import pallas as pl
from jax.experimental.pallas import tpu as pltpu
from jax.sharding import PartitionSpec as P

LOGIT_SCALE = 8.0
KEEP_RATE = 0.75
VMEM_BYTES = 40 * 1024 * 1024
LABEL_ROWS = 16
NT_DIMS = (((1,), (1,)), ((), ()))
TN_DIMS = (((0,), (0,)), ((), ()))
tie = lax.optimization_barrier


def params(axes=1):
    return pltpu.CompilerParams(
        vmem_limit_bytes=VMEM_BYTES, dimension_semantics=("arbitrary",) * axes
    )


def cost(flops, moved, exps=0):
    return pl.CostEstimate(flops=flops, bytes_accessed=moved, transcendentals=exps)


def whole_block(shape):
    zeros = (0,) * len(shape)
    return pl.BlockSpec(shape, lambda *_: zeros)


def norm_kernel(x_ref, out_ref):
    x = x_ref[...].astype(jnp.float32)
    scale = lax.rsqrt(jnp.mean(x * x, axis=-1, keepdims=True) + 1e-05)
    out_ref[...] = (x * scale).astype(out_ref.dtype)


def norm_rows(tokens):
    rows, width = tokens.shape
    step = min(128, rows)
    return pl.pallas_call(
        norm_kernel,
        out_shape=jax.ShapeDtypeStruct(tokens.shape, jnp.bfloat16),
        grid=(rows // step,),
        in_specs=[pl.BlockSpec((step, width), lambda i: (i, 0))],
        out_specs=pl.BlockSpec((step, width), lambda i: (i, 0)),
        compiler_params=params(),
        cost_estimate=cost(4 * rows * width, 4 * rows * width),
        name="norm_rows",
    )(tokens)


def early_kernel(n_early, n_late, place_ref, x_ref, *refs):
    weights, (acc_ref, rest_ref) = refs[: 2 * n_early], refs[2 * n_early :]
    depth, half = weights[0].shape

    def columns(i):
        return x_ref[:, pl.ds(pl.multiple_of(place_ref[i] * depth, depth), depth)]

    for part in range(2):
        total = None
        for i in range(n_early):
            term = jnp.dot(
                columns(i), weights[2 * i + part][...], preferred_element_type=jnp.float32
            )
            total = term if total is None else total + term
        acc_ref[:, part * half : (part + 1) * half] = total
    for i in range(n_late):
        rest_ref[:, i * depth : (i + 1) * depth] = columns(n_early + i)


def early_projection(normed, places, early, n_late):
    rows, width = normed.shape
    depth, half = early[0][0].shape
    n_early = len(early)
    step = 256
    flat = [part for pair in early for part in pair]
    return pl.pallas_call(
        functools.partial(early_kernel, n_early, n_late),
        out_shape=(
            jax.ShapeDtypeStruct((rows, 2 * half), jnp.float32),
            jax.ShapeDtypeStruct((rows, n_late * depth), jnp.bfloat16),
        ),
        grid_spec=pltpu.PrefetchScalarGridSpec(
            num_scalar_prefetch=1,
            grid=(rows // step,),
            in_specs=[pl.BlockSpec((step, width), lambda i, _: (i, 0))]
            + [whole_block((depth, half))] * (2 * n_early),
            out_specs=(
                pl.BlockSpec((step, 2 * half), lambda i, _: (i, 0)),
                pl.BlockSpec((step, n_late * depth), lambda i, _: (i, 0)),
            ),
        ),
        compiler_params=params(),
        cost_estimate=cost(
            4 * rows * n_early * depth * half, 2 * rows * width + 8 * rows * half
        ),
        name="early_projection",
    )(places, normed, *flat)


def unit_rows(values):
    values = values.astype(jnp.float32)
    scale = lax.rsqrt(jnp.mean(values * values, axis=-1, keepdims=True) + 1e-06)
    return (values * scale).astype(jnp.bfloat16)


def late_kernel(n_late, heads, tiles, tile_rows, owner_ref, later_ref, acc_ref, rest_ref, *refs):
    weights, (qkv_ref, out_ref) = refs[: 2 * n_late], refs[2 * n_late :]
    depth, half = weights[0].shape
    head_dim = out_ref.shape[2] // 2
    step = pl.program_id(0)
    tiles_step = acc_ref.shape[0] // tile_rows

    if out_ref.shape[0] > heads * tiles:

        @pl.when(step == 0)
        def _():
            out_ref[...] = jnp.zeros_like(out_ref)

    for part in range(2):
        total = acc_ref[:, part * half : (part + 1) * half]
        for i in range(n_late):
            total += jnp.dot(
                rest_ref[:, i * depth : (i + 1) * depth],
                weights[2 * i + part][...],
                preferred_element_type=jnp.float32,
            )
        projected = total.astype(jnp.bfloat16)
        for local in range(heads // 2):
            head = part * (heads // 2) + local
            base = local * 3 * head_dim
            query = unit_rows(projected[:, base : base + head_dim])
            key = unit_rows(projected[:, base + head_dim : base + 2 * head_dim])
            value = projected[:, base + 2 * head_dim : base + 3 * head_dim]
            at = head * 3 * head_dim
            qkv_ref[:, at : at + head_dim] = query
            qkv_ref[:, at + head_dim : at + 2 * head_dim] = key
            qkv_ref[:, at + 2 * head_dim : at + 3 * head_dim] = value
            for t in range(tiles_step):
                index = head * tiles + step * tiles_step + t
                owner = owner_ref[index]
                span = slice(t * tile_rows, (t + 1) * tile_rows)
                out_ref[owner, :, :head_dim] = key[span]
                out_ref[owner, :, head_dim:] = jnp.where(
                    later_ref[index] > 0, query[span], value[span]
                )


def late_projection(acc, rest, late, owners, later, n_owners, heads, tiles):
    rows, cols = acc.shape
    depth, half = late[0][0].shape
    n_late = len(late)
    tile_rows = rows // tiles
    head_dim = cols // (3 * heads)
    step = 2 * tile_rows
    flat = [part for pair in late for part in pair]
    return pl.pallas_call(
        functools.partial(late_kernel, n_late, heads, tiles, tile_rows),
        out_shape=(
            jax.ShapeDtypeStruct((rows, cols), jnp.bfloat16),
            jax.ShapeDtypeStruct((n_owners, tile_rows, 2 * head_dim), jnp.bfloat16),
        ),
        grid_spec=pltpu.PrefetchScalarGridSpec(
            num_scalar_prefetch=2,
            grid=(rows // step,),
            in_specs=[
                pl.BlockSpec((step, cols), lambda i, *_: (i, 0)),
                pl.BlockSpec((step, n_late * depth), lambda i, *_: (i, 0)),
            ]
            + [whole_block((depth, half))] * (2 * n_late),
            out_specs=(
                pl.BlockSpec((step, cols), lambda i, *_: (i, 0)),
                whole_block((n_owners, tile_rows, 2 * head_dim)),
            ),
        ),
        compiler_params=params(),
        cost_estimate=cost(4 * rows * n_late * depth * half, 9 * rows * cols),
        name="late_projection",
    )(owners, later, acc, rest, *flat)


def inner_kernel(heads, qkv_ref, sums_ref, mass_ref):
    rows = qkv_ref.shape[0]
    head_dim = qkv_ref.shape[1] // (3 * heads)
    allowed = lax.broadcasted_iota(jnp.int32, (rows, rows), 1) <= lax.broadcasted_iota(
        jnp.int32, (rows, rows), 0
    )
    ones = jnp.ones((rows, head_dim), jnp.bfloat16)
    for head in range(heads):
        at = head * 3 * head_dim
        query = qkv_ref[:, at : at + head_dim]
        key = qkv_ref[:, at + head_dim : at + 2 * head_dim]
        value = qkv_ref[:, at + 2 * head_dim : at + 3 * head_dim]
        scores = lax.dot_general(query, key, NT_DIMS, preferred_element_type=jnp.float32)
        weights = jnp.where(allowed, jnp.exp(scores * (LOGIT_SCALE / head_dim)), 0.0)
        weights = weights.astype(jnp.bfloat16)
        span = slice(head * head_dim, (head + 1) * head_dim)
        sums_ref[:, span] = jnp.dot(weights, value, preferred_element_type=jnp.float32)
        mass_ref[:, span] = jnp.dot(weights, ones, preferred_element_type=jnp.float32)


def inner_attention(qkv, heads, tiles):
    rows, cols = qkv.shape
    tile_rows = rows // tiles
    out = jax.ShapeDtypeStruct((rows, cols // 3), jnp.float32)
    return pl.pallas_call(
        functools.partial(inner_kernel, heads),
        out_shape=(out, out),
        grid=(tiles,),
        in_specs=[pl.BlockSpec((tile_rows, cols), lambda i: (i, 0))],
        out_specs=(pl.BlockSpec((tile_rows, cols // 3), lambda i: (i, 0)),) * 2,
        compiler_params=params(),
        cost_estimate=cost(
            2 * rows * tile_rows * cols, 5 * rows * cols, rows * tile_rows * heads
        ),
        name="inner_attention",
    )(qkv)


def owner_kernel(first_ref, second_ref, held_ref, in_ref, cent_ref, out_ref, new_ref):
    tile_rows = in_ref.shape[1]
    head_dim = in_ref.shape[2] // 2
    out_ref[...] = jnp.zeros_like(out_ref)
    ones = jnp.ones((LABEL_ROWS, tile_rows), jnp.bfloat16)
    line = lax.broadcasted_iota(jnp.int32, (LABEL_ROWS, tile_rows), 0)
    for c in range(cent_ref.shape[0]):
        first, second, held = first_ref[c], second_ref[c], held_ref[c]
        key = in_ref[first, :, :head_dim]

        @pl.when(held > 1)
        def _():
            value = in_ref[first, :, head_dim:]
            query = in_ref[second, :, head_dim:]
            scores = lax.dot_general(query, key, NT_DIMS, preferred_element_type=jnp.float32)
            weights = jnp.exp(scores * (LOGIT_SCALE / head_dim)).astype(jnp.bfloat16)
            out_ref[second, :tile_rows, :] = jnp.dot(
                weights, value, preferred_element_type=jnp.float32
            ).astype(jnp.bfloat16)
            mass = lax.dot_general(ones, weights, NT_DIMS, preferred_element_type=jnp.float32)
            high = mass.astype(jnp.bfloat16).astype(jnp.float32)
            out_ref[second, tile_rows:, :] = jnp.where(
                line == 0, high, jnp.where(line == 1, mass - high, 0.0)
            ).astype(jnp.bfloat16)

        other = in_ref[second, :, :head_dim]
        first_sum = jnp.sum(key.astype(jnp.float32), axis=0, keepdims=True)
        other_sum = jnp.sum(other.astype(jnp.float32), axis=0, keepdims=True)
        key_sum = jnp.where(held > 1, first_sum + other_sum, first_sum)
        count = jnp.maximum(held, 1).astype(jnp.float32) * tile_rows
        old = cent_ref[c : c + 1, :]
        moved = old + (1.0 - KEEP_RATE) * (key_sum / count - old)
        new_ref[c : c + 1, :] = jnp.where(held > 0, moved, old)


def owner_attention(incoming, centroid_rows, first, second, held):
    n, tile_rows, width = incoming.shape
    head_dim = width // 2
    returning = (n, tile_rows + LABEL_ROWS, head_dim)
    return pl.pallas_call(
        owner_kernel,
        out_shape=(
            jax.ShapeDtypeStruct(returning, jnp.bfloat16),
            jax.ShapeDtypeStruct(centroid_rows.shape, jnp.float32),
        ),
        grid_spec=pltpu.PrefetchScalarGridSpec(
            num_scalar_prefetch=3,
            grid=(1,),
            in_specs=[whole_block(incoming.shape), whole_block(centroid_rows.shape)],
            out_specs=(whole_block(returning), whole_block(centroid_rows.shape)),
        ),
        compiler_params=params(),
        cost_estimate=cost(
            4 * centroid_rows.shape[0] * tile_rows * tile_rows * width,
            4 * n * tile_rows * width,
            centroid_rows.shape[0] * tile_rows * tile_rows,
        ),
        name="owner_attention",
    )(first, second, held, incoming, centroid_rows)


def merge_kernel(heads, tiles, owner_ref, later_ref, sums_ref, mass_ref, back_ref, out_ref):
    tile_rows = sums_ref.shape[0]
    head_dim = sums_ref.shape[1] // heads
    step = pl.program_id(0)
    pick = (lax.broadcasted_iota(jnp.int32, (LABEL_ROWS, head_dim), 0) < 2).astype(jnp.bfloat16)
    for head in range(heads):
        index = head * tiles + step
        owner, later = owner_ref[index], later_ref[index] > 0
        span = slice(head * head_dim, (head + 1) * head_dim)
        sums = sums_ref[:, span]
        mass = mass_ref[:, span]
        far_mass = lax.dot_general(
            back_ref[owner, tile_rows:, :], pick, TN_DIMS, preferred_element_type=jnp.float32
        )
        far_sums = back_ref[owner, :tile_rows, :].astype(jnp.float32)
        sums = jnp.where(later, sums + far_sums, sums)
        mass = jnp.where(later, mass + far_mass, mass)
        out_ref[:, span] = (sums / mass).astype(out_ref.dtype)


def merge_attention(sums, mass, back, owners, later, heads, tiles):
    rows, cols = sums.shape
    tile_rows = rows // tiles
    block = pl.BlockSpec((tile_rows, cols), lambda i, *_: (i, 0))
    return pl.pallas_call(
        functools.partial(merge_kernel, heads, tiles),
        out_shape=jax.ShapeDtypeStruct((rows, cols), jnp.bfloat16),
        grid_spec=pltpu.PrefetchScalarGridSpec(
            num_scalar_prefetch=2,
            grid=(tiles,),
            in_specs=[block, block, whole_block(back.shape)],
            out_specs=block,
        ),
        compiler_params=params(),
        cost_estimate=cost(8 * rows * cols, 12 * rows * cols),
        name="merge_attention",
    )(owners, later, sums, mass, back)


def output_kernel(place_ref, weight_ref, *refs):
    parts, out_ref = refs[:-1], refs[-1]
    total, at = None, 0
    for part in parts:
        width = part.shape[1]
        term = lax.dot_general(
            weight_ref[0, :, at : at + width],
            part[...],
            NT_DIMS,
            preferred_element_type=jnp.float32,
        )
        total = term if total is None else total + term
        at += width
    out_ref[...] = total.astype(out_ref.dtype)


def output_projection(weight_blocks, places, parts):
    n, features, depth = weight_blocks.shape
    rows = parts[0].shape[0]
    return pl.pallas_call(
        output_kernel,
        out_shape=jax.ShapeDtypeStruct((n * features, rows), jnp.bfloat16),
        grid_spec=pltpu.PrefetchScalarGridSpec(
            num_scalar_prefetch=1,
            grid=(n,),
            in_specs=[pl.BlockSpec((1, features, depth), lambda i, _: (i, 0, 0))]
            + [whole_block(part.shape) for part in parts],
            out_specs=pl.BlockSpec((features, rows), lambda i, place: (place[i], 0)),
        ),
        compiler_params=params(),
        cost_estimate=cost(
            2 * n * features * depth * rows, 2 * n * features * (rows + depth)
        ),
        name="output_projection",
    )(places, weight_blocks, *parts)


def permute(value, pairs):
    return lax.ppermute(value, "seq", pairs)


def flip(bit, n=16):
    return [(s, s ^ bit) for s in range(n)]


def turn(by, n=16):
    return [(s, (s + 4 * by) % n) for s in range(n)]


LINE_UP, LINE_DOWN = turn(1), turn(-1)
SIDE, CORE = flip(2), flip(1)


def gather_weights(weight):
    half = weight.shape[1] // 2
    own = tie((weight[:, :half], weight[:, half:]))
    lines, sides, far = [[o] for o in own], [[], []], [[], []]

    def hop(p, last=False):
        moves = []
        if not last:
            moves.append((lines[p], lines[p][-1], LINE_UP))
        if not last or p == 0:
            moves.append((sides[p], lines[p][-1], SIDE))
        else:
            moves.append((sides[p], sides[p][0], LINE_DOWN))
        moves.append((far[p], lines[p][-1], CORE))
        if sides[p]:
            moves.append((far[p], sides[p][-1], CORE))
        results = tie(tuple(permute(value, pairs) for _, value, pairs in moves))
        for (group, _, _), value in zip(moves, results):
            group.append(value)

    for k in range(4):
        for p in range(2):
            hop(p, last=k == 3)
    for p in range(2):
        far[p].append(permute(sides[p][3], CORE))

    early = [
        tuple(lines[p][k] for p in range(2)) for k in range(4)
    ] + [
        tuple(sides[p][k] for p in range(2)) for k in range(3)
    ] + [tuple(far[p][k] for p in range(2)) for k in range(5)]
    late = [tuple(sides[p][3] for p in range(2))] + [
        tuple(far[p][k] for p in range(2)) for k in range(5, 8)
    ]
    return early, late


def weight_places(me):
    line, side, core = me // 4, me // 2 % 2, me % 2

    def at(back, other_side, other_core):
        where = jnp.mod(line - back, 4) * 4
        where += (1 - side if other_side else side) * 2
        return where + (1 - core if other_core else core)

    early = [at(k, 0, 0) for k in range(4)] + [at(k, 1, 0) for k in range(3)]
    early += [at(0, 0, 1), at(1, 0, 1), at(0, 1, 1), at(2, 0, 1), at(1, 1, 1)]
    late = [at(3, 1, 0), at(3, 0, 1), at(2, 1, 1), at(3, 1, 1)]
    return jnp.stack(early + late).astype(jnp.int32)


def gather_labels(labels):
    gathered = labels[None]
    for bit in (1, 2, 4, 8):
        gathered = jnp.concatenate([gathered, permute(gathered, flip(bit))], axis=0)
    return gathered


def gather_out_weight(weight, me, group):
    mine = weight.T
    across = permute(mine, flip(8))
    inside = me // 8 == group
    keep = jnp.where(inside, mine, across)
    give = jnp.where(inside, across, mine)
    got = lax.ppermute(give, "head", [(0, 1), (1, 0)])
    blocks = jnp.concatenate([keep, got], axis=1)[None]
    for bit in (4, 2, 1):
        blocks = jnp.concatenate([blocks, permute(blocks, flip(bit))], axis=0)
    order = jnp.arange(8, dtype=jnp.int32)
    places = (me % 8) ^ (order % 2 * 4) ^ (order // 2 % 2 * 2) ^ (order // 4)
    return blocks, places.astype(jnp.int32)


def on_device(tokens, qkv_weight, out_weight, centroids, clusters, slots):
    heads, tiles = clusters.shape
    clus_here, head_dim = centroids.shape[1:]
    n_seq, n_head = lax.axis_size("seq"), lax.axis_size("head")
    me, group = lax.axis_index("seq"), lax.axis_index("head")
    paired = n_seq == 16 and n_head == 2

    if paired:
        early, late = gather_weights(qkv_weight)
        places = weight_places(me)
        labels = gather_labels(clusters)
        sources = me ^ jnp.arange(n_seq, dtype=jnp.int32)
    else:
        full = lax.all_gather(qkv_weight, "seq", axis=0, tiled=True)
        depth, half = full.shape[0] // 16, full.shape[1] // 2
        blocks = [
            (full[i * depth : (i + 1) * depth, :half], full[i * depth : (i + 1) * depth, half:])
            for i in range(16)
        ]
        early, late = blocks[:12], blocks[12:]
        places = jnp.arange(16, dtype=jnp.int32)
        labels = lax.all_gather(clusters, "seq", axis=0)
        sources = jnp.arange(n_seq, dtype=jnp.int32)

    numbers = (sources[:, None] * tiles + jnp.arange(tiles, dtype=jnp.int32)).reshape(-1)
    labels = labels.transpose(1, 0, 2).reshape(heads, -1)
    own_numbers = me * tiles + jnp.arange(tiles, dtype=jnp.int32)
    earlier = (labels[:, None, :] == clusters[:, :, None]) & (
        numbers[None, None, :] < own_numbers[None, :, None]
    )
    later = jnp.any(earlier, axis=2).astype(jnp.int32).reshape(-1)
    owners = (clusters // clus_here).reshape(-1)
    owned = me * clus_here + jnp.arange(clus_here, dtype=jnp.int32)
    member = labels[:, None, :] == owned[None, :, None]
    held = jnp.sum(member.astype(jnp.int32), axis=2).reshape(-1)
    total = n_seq * tiles
    first = jnp.min(jnp.where(member, numbers[None, None, :], total - 1), axis=2).reshape(-1)
    second = jnp.max(jnp.where(member, numbers[None, None, :], 0), axis=2).reshape(-1)
    first, second = first // tiles, second // tiles

    normed = norm_rows(tokens)
    acc, rest = early_projection(normed, places, early, len(late))
    qkv, outgoing = late_projection(acc, rest, late, owners, later, n_seq, heads, tiles)
    incoming = lax.all_to_all(outgoing, "seq", split_axis=0, concat_axis=0, tiled=True)
    sums, mass = inner_attention(qkv, heads, tiles)
    returning, new_rows = owner_attention(
        incoming, centroids.reshape(heads * clus_here, head_dim), first, second, held
    )
    back = lax.all_to_all(returning, "seq", split_axis=0, concat_axis=0, tiled=True)
    attention = merge_attention(sums, mass, back, owners, later, heads, tiles)

    if paired:
        weight_blocks, feature_places = gather_out_weight(out_weight, me, group)
        parts = [attention, lax.ppermute(attention, "head", [(0, 1), (1, 0)])]
    else:
        rows = lax.all_gather(out_weight, "seq", axis=1, tiled=True)
        rows = lax.all_gather(rows, "head", axis=0, tiled=True)
        features = rows.shape[1] // n_head
        mine = lax.dynamic_slice_in_dim(rows, group * features, features, axis=1).T
        weight_blocks = mine.reshape(-1, min(256, features), mine.shape[1])
        feature_places = jnp.arange(weight_blocks.shape[0], dtype=jnp.int32)
        parts = [lax.all_gather(attention, "head", axis=1, tiled=True)]
    summed = output_projection(weight_blocks, feature_places, parts)
    return (summed, new_rows.reshape(centroids.shape))


def solution(mesh):
    placed = (
        P("seq", None),
        P("seq", "head"),
        P("head", "seq"),
        P("head", "seq", None),
        P("head", "seq"),
        P("head", "seq"),
    )
    return jax.shard_map(
        on_device,
        mesh=mesh,
        in_specs=placed,
        out_specs=(P("head", "seq"), P("head", "seq", None)),
        check_vma=False,
    )
```

```python
import functools

import jax
import jax.numpy as jnp
from jax import lax
from jax.experimental import pallas as pl
from jax.experimental.pallas import tpu as pltpu
from jax.sharding import PartitionSpec as P

LOGIT_SCALE = 8.0
KEEP_RATE = 0.75
VMEM_BYTES = 16 * 1024 * 1024
LABEL_ROWS = 16
NT_DIMS = (((1,), (1,)), ((), ()))
TN_DIMS = (((0,), (0,)), ((), ()))
tie = lax.optimization_barrier


def params(axes=1):
    return pltpu.CompilerParams(
        vmem_limit_bytes=VMEM_BYTES, dimension_semantics=("arbitrary",) * axes
    )


def cost(flops, moved, exps=0):
    return pl.CostEstimate(flops=flops, bytes_accessed=moved, transcendentals=exps)


def whole_block(shape):
    zeros = (0,) * len(shape)
    return pl.BlockSpec(shape, lambda *_: zeros)


def in_hbm(value):
    return pltpu.with_memory_space_constraint(value, pltpu.HBM)


def in_vmem(value):
    return pltpu.with_memory_space_constraint(value, pltpu.VMEM)


W_PLACE = in_vmem
VMEM_SPEC = pl.BlockSpec(memory_space=pltpu.VMEM)
SMEM_SPEC = pl.BlockSpec(memory_space=pltpu.SMEM)
W_SPEC = VMEM_SPEC


ORDER = [(0, 0, 0), (1, 0, 0), (0, 1, 0), (0, 0, 1)]
ORDER += [(2, 0, 0), (1, 1, 0), (1, 0, 1), (0, 1, 1)]
ORDER += [(3, 0, 0), (2, 1, 0), (2, 0, 1), (1, 1, 1)]
ORDER += [(3, 1, 0), (3, 0, 1), (2, 1, 1), (3, 1, 1)]


def place_of(i, me, paired):
    if not paired:
        return i
    back, side, core = ORDER[i]
    return ((me // 4 + 4 - back) % 4 * 4 + me % 4) ^ (side * 2 + core)


def split_kernel(weight_ref, clusters_ref, first_ref, second_ref):
    rows, half = second_ref.shape
    first_ref[:rows, :] = weight_ref[:, :half]
    second_ref[...] = weight_ref[:, half:]
    marks = jnp.zeros((LABEL_ROWS, 128), jnp.float32)
    line = lax.broadcasted_iota(jnp.int32, marks.shape, 0)
    lane = lax.broadcasted_iota(jnp.int32, marks.shape, 1)
    heads, tiles = clusters_ref.shape
    for head in range(heads):
        for t in range(tiles):
            number = clusters_ref[head, t].astype(jnp.float32)
            marks = jnp.where((line == head) & (lane == t), number, marks)
    first_ref[rows:, :] = jnp.zeros((LABEL_ROWS, half), first_ref.dtype)
    first_ref[rows:, :128] = marks.astype(first_ref.dtype)


def split_weight(weight, clusters):
    rows, half = weight.shape[0], weight.shape[1] // 2
    return pl.pallas_call(
        split_kernel,
        out_shape=(
            pltpu.VMEM((rows + LABEL_ROWS, half), weight.dtype),
            pltpu.VMEM((rows, half), weight.dtype),
        ),
        in_specs=[VMEM_SPEC, SMEM_SPEC],
        out_specs=(VMEM_SPEC,) * 2,
        compiler_params=pltpu.CompilerParams(vmem_limit_bytes=VMEM_BYTES),
        cost_estimate=cost(0, 8 * rows * half),
        name="split_weight",
    )(weight, clusters)


def spread_marks(blocks, depth, start, total):
    for i, ref in enumerate(blocks):
        marks = ref[depth : depth + LABEL_ROWS, :128].astype(jnp.float32)
        shift = (start + i) * 8
        moved = pltpu.roll(marks, shift, 1) if shift else marks
        total = moved if total is None else total + moved
    return total


def early_kernel(n_early, n_late, paired, me_ref, x_ref, *refs):
    weights, (acc_ref, rest_ref, marks_ref) = refs[: 2 * n_early], refs[2 * n_early :]
    depth, half = weights[1].shape
    me = me_ref[0]

    @pl.when(pl.program_id(0) == 0)
    def _():
        marks_ref[...] = jnp.zeros_like(marks_ref)
        if paired:
            marks_ref[...] = spread_marks(weights[::2], depth, 0, None)

    def columns(i):
        at = place_of(i, me, paired) * depth
        return x_ref[:, pl.ds(pl.multiple_of(at, depth), depth)]

    square = None
    for at in range(0, x_ref.shape[1], 128):
        x = x_ref[:, at : at + 128].astype(jnp.float32)
        square = x * x if square is None else square + x * x
    mean = jnp.sum(square, axis=-1, keepdims=True) / x_ref.shape[1]
    scale = lax.rsqrt(mean + 1e-05)
    for part in range(2):
        total = None
        for i in range(n_early):
            term = jnp.dot(
                columns(i), weights[2 * i + part][:depth, :], preferred_element_type=jnp.float32
            )
            total = term if total is None else total + term
        acc_ref[:, part * half : (part + 1) * half] = jnp.where(scale > 0, total * scale, 0.0)
    for i in range(n_late):
        x = columns(n_early + i).astype(jnp.float32)
        rest_ref[:, i * depth : (i + 1) * depth] = (x * scale).astype(rest_ref.dtype)


def project_early(tokens, me, early, n_late, paired):
    rows, width = tokens.shape
    depth, half = early[0][1].shape
    n_early = len(early)
    step = min(256, rows)
    flat = [part for pair in early for part in pair]
    return pl.pallas_call(
        functools.partial(early_kernel, n_early, n_late, paired),
        out_shape=(
            pltpu.HBM((rows, 2 * half), jnp.float32),
            pltpu.HBM((rows, n_late * depth), jnp.bfloat16),
            pltpu.HBM((LABEL_ROWS, 128), jnp.float32),
        ),
        grid_spec=pltpu.PrefetchScalarGridSpec(
            num_scalar_prefetch=1,
            grid=(rows // step,),
            in_specs=[pl.BlockSpec((step, width), lambda i, _: (i, 0))] + [W_SPEC] * len(flat),
            out_specs=(
                pl.BlockSpec((step, 2 * half), lambda i, _: (i, 0)),
                pl.BlockSpec((step, n_late * depth), lambda i, _: (i, 0)),
                whole_block((LABEL_ROWS, 128)),
            ),
        ),
        compiler_params=pltpu.CompilerParams(vmem_limit_bytes=26 * 1024 * 1024),
        cost_estimate=cost(
            4 * rows * n_early * depth * half, 2 * rows * width + 8 * rows * half
        ),
        name="project_early",
    )(me, in_hbm(tokens), *map(W_PLACE, flat))


def unit_rows(values):
    values = values.astype(jnp.float32)
    scale = lax.rsqrt(jnp.mean(values * values, axis=-1, keepdims=True) + 1e-06)
    return (values * scale).astype(jnp.bfloat16)


def fill_tables(clus_here, me, paired, labels, cluster_ref, table_ref):
    heads, tiles = cluster_ref.shape
    shape = (8, labels.shape[1])
    line = lax.broadcasted_iota(jnp.int32, shape, 0)
    lane = lax.broadcasted_iota(jnp.int32, shape, 1)
    numbers = lane
    if paired:
        for i in range(16):
            numbers = jnp.where(
                lane // tiles == i, place_of(i, me, paired) * tiles + lane % tiles, numbers
            )
    base = heads * 8
    for head in range(heads):
        row = labels[head : head + 1, :]
        own = jnp.full(shape, -1, jnp.int32)
        for t in range(tiles):
            own = jnp.where(line == t, cluster_ref[head, t], own)
        earlier = (row == own) & (numbers < me * tiles + line)
        later = jnp.max(earlier.astype(jnp.int32), axis=1, keepdims=True)
        table_ref[head * 8 : (head + 1) * 8, :] = jnp.broadcast_to(later, (8, 128))
        member = (row == me * clus_here + line) & (line < clus_here)
        held = jnp.sum(member.astype(jnp.int32), axis=1, keepdims=True)
        last = shape[1] - 1
        first = jnp.min(jnp.where(member, numbers, last), axis=1, keepdims=True) // tiles
        second = jnp.max(jnp.where(member, numbers, 0), axis=1, keepdims=True) // tiles
        for q, column in enumerate((held, first, second)):
            at = base + (q * heads + head) * 8
            table_ref[at : at + 8, :] = jnp.broadcast_to(column, (8, 128))


def late_kernel(
    n_late, heads, tiles, tile_rows, clus_here, paired, me_ref, cluster_ref, acc_ref, rest_ref,
    marks_ref, *refs
):
    weights, (qkv_ref, out_ref, table_ref) = refs[: 2 * n_late], refs[2 * n_late :]
    depth, half = weights[1].shape
    head_dim = out_ref.shape[2] // 2
    step = pl.program_id(0)
    tiles_step = acc_ref.shape[0] // tile_rows

    @pl.when(step == 0)
    def _():
        labels = marks_ref[...]
        if paired:
            labels = spread_marks(weights[::2], depth, 16 - n_late, labels)
        labels = labels.astype(jnp.int32)
        fill_tables(clus_here, me_ref[0], paired, labels, cluster_ref, table_ref)
        if out_ref.shape[0] > heads * tiles:
            out_ref[...] = jnp.zeros_like(out_ref)

    for part in range(2):
        total = acc_ref[:, part * half : (part + 1) * half]
        for i in range(n_late):
            total += jnp.dot(
                rest_ref[:, i * depth : (i + 1) * depth],
                weights[2 * i + part][:depth, :],
                preferred_element_type=jnp.float32,
            )
        projected = total.astype(jnp.bfloat16)
        for local in range(heads // 2):
            head = part * (heads // 2) + local
            base = local * 3 * head_dim
            query = unit_rows(projected[:, base : base + head_dim])
            key = unit_rows(projected[:, base + head_dim : base + 2 * head_dim])
            value = projected[:, base + 2 * head_dim : base + 3 * head_dim]
            at = head * 3 * head_dim
            qkv_ref[:, at : at + head_dim] = query
            qkv_ref[:, at + head_dim : at + 2 * head_dim] = key
            qkv_ref[:, at + 2 * head_dim : at + 3 * head_dim] = value
            for t in range(tiles_step):
                tile = step * tiles_step + t
                owner = cluster_ref[head, tile] // clus_here
                later = table_ref[pl.ds(head * 8 + tile, 1), :]
                span = slice(t * tile_rows, (t + 1) * tile_rows)
                out_ref[owner, :, :head_dim] = key[span]
                out_ref[owner, :, head_dim:] = jnp.where(later > 0, query[span], value[span])


def project_late(me, clusters, clus_here, acc, rest, marks, late, n_owners, paired):
    rows, cols = acc.shape
    heads, tiles = clusters.shape
    depth, half = late[0][1].shape
    n_late = len(late)
    tile_rows = rows // tiles
    head_dim = cols // (3 * heads)
    step = 2 * tile_rows
    table_rows = 32 * heads
    flat = [part for pair in late for part in pair]
    return pl.pallas_call(
        functools.partial(
            late_kernel, n_late, heads, tiles, tile_rows, clus_here, paired
        ),
        out_shape=(
            pltpu.HBM((rows, cols), jnp.bfloat16),
            pltpu.HBM((n_owners, tile_rows, 2 * head_dim), jnp.bfloat16),
            pltpu.HBM((table_rows, 128), jnp.int32),
        ),
        grid_spec=pltpu.PrefetchScalarGridSpec(
            num_scalar_prefetch=2,
            grid=(rows // step,),
            in_specs=[
                pl.BlockSpec((step, cols), lambda i, *_: (i, 0)),
                pl.BlockSpec((step, n_late * depth), lambda i, *_: (i, 0)),
                whole_block(marks.shape),
            ]
            + [W_SPEC] * len(flat),
            out_specs=(
                pl.BlockSpec((step, cols), lambda i, *_: (i, 0)),
                whole_block((n_owners, tile_rows, 2 * head_dim)),
                whole_block((table_rows, 128)),
            ),
        ),
        compiler_params=params(),
        cost_estimate=cost(4 * rows * n_late * depth * half, 9 * rows * cols),
        name="project_late",
    )(me, clusters, in_hbm(acc), in_hbm(rest), in_hbm(marks), *map(W_PLACE, flat))


def inner_kernel(heads, qkv_ref, sums_ref, mass_ref):
    rows = qkv_ref.shape[0]
    head_dim = qkv_ref.shape[1] // (3 * heads)
    allowed = lax.broadcasted_iota(jnp.int32, (rows, rows), 0) <= lax.broadcasted_iota(
        jnp.int32, (rows, rows), 1
    )
    for head in range(heads):
        at = head * 3 * head_dim
        query = qkv_ref[:, at : at + head_dim]
        key = qkv_ref[:, at + head_dim : at + 2 * head_dim]
        value = qkv_ref[:, at + 2 * head_dim : at + 3 * head_dim]
        scores = lax.dot_general(key, query, NT_DIMS, preferred_element_type=jnp.float32)
        weights = jnp.where(allowed, jnp.exp(scores * (LOGIT_SCALE / head_dim)), 0.0)
        mass = jnp.sum(weights, axis=0, keepdims=True)
        sums_ref[head * head_dim : (head + 1) * head_dim, :] = lax.dot_general(
            value, weights.astype(jnp.bfloat16), TN_DIMS, preferred_element_type=jnp.float32
        )
        mass_ref[head * 8 : (head + 1) * 8, :] = jnp.broadcast_to(mass, (8, rows))


def inner_attention(qkv, heads, tiles):
    rows, cols = qkv.shape
    tile_rows = rows // tiles
    return pl.pallas_call(
        functools.partial(inner_kernel, heads),
        out_shape=(
            pltpu.HBM((cols // 3, rows), jnp.float32),
            pltpu.HBM((heads * 8, rows), jnp.float32),
        ),
        grid=(tiles,),
        in_specs=[pl.BlockSpec((tile_rows, cols), lambda i: (i, 0))],
        out_specs=(
            pl.BlockSpec((cols // 3, tile_rows), lambda i: (0, i)),
            pl.BlockSpec((heads * 8, tile_rows), lambda i: (0, i)),
        ),
        compiler_params=params(),
        cost_estimate=cost(
            2 * rows * tile_rows * cols, 5 * rows * cols, rows * tile_rows * heads
        ),
        name="inner_attention",
    )(in_hbm(qkv))


def owner_kernel(base, heads, table_ref, in_ref, cent_ref, out_ref, new_ref):
    tile_rows = in_ref.shape[1]
    head_dim = in_ref.shape[2] // 2
    out_ref[...] = jnp.zeros_like(out_ref)
    line = lax.broadcasted_iota(jnp.int32, (LABEL_ROWS, tile_rows), 0)
    for c in range(cent_ref.shape[0]):
        clus_here = cent_ref.shape[0] // heads
        at = base + c // clus_here * 8 + c % clus_here
        held, first, second = (table_ref[at + 8 * heads * q, 0] for q in range(3))
        key = in_ref[first, :, :head_dim]

        @pl.when(held > 1)
        def _():
            value = in_ref[first, :, head_dim:]
            query = in_ref[second, :, head_dim:]
            scores = lax.dot_general(key, query, NT_DIMS, preferred_element_type=jnp.float32)
            weights = jnp.exp(scores * (LOGIT_SCALE / head_dim))
            mass = jnp.sum(weights, axis=0, keepdims=True)
            out_ref[second, :head_dim, :] = lax.dot_general(
                value, weights.astype(jnp.bfloat16), TN_DIMS, preferred_element_type=jnp.float32
            ).astype(jnp.bfloat16)
            high = mass.astype(jnp.bfloat16).astype(jnp.float32)
            out_ref[second, head_dim:, :] = jnp.where(
                line == 0, high, jnp.where(line == 1, mass - high, 0.0)
            ).astype(jnp.bfloat16)

        other = in_ref[second, :, :head_dim]
        first_sum = jnp.sum(key.astype(jnp.float32), axis=0, keepdims=True)
        other_sum = jnp.sum(other.astype(jnp.float32), axis=0, keepdims=True)
        key_sum = jnp.where(held > 1, first_sum + other_sum, first_sum)
        count = jnp.maximum(held, 1).astype(jnp.float32) * tile_rows
        old = cent_ref[c : c + 1, :]
        moved = old + (1.0 - KEEP_RATE) * (key_sum / count - old)
        new_ref[c : c + 1, :] = jnp.where(held > 0, moved, old)


def owner_attention(incoming, centroid_rows, table, heads):
    n, tile_rows, width = incoming.shape
    head_dim = width // 2
    returning = (n, head_dim + LABEL_ROWS, tile_rows)
    return pl.pallas_call(
        functools.partial(owner_kernel, heads * 8, heads),
        out_shape=(
            pltpu.HBM(returning, jnp.bfloat16),
            pltpu.HBM(centroid_rows.shape, jnp.float32),
        ),
        grid=(1,),
        in_specs=[
            pl.BlockSpec(memory_space=pltpu.SMEM),
            whole_block(incoming.shape),
            whole_block(centroid_rows.shape),
        ],
        out_specs=(whole_block(returning), whole_block(centroid_rows.shape)),
        compiler_params=params(),
        cost_estimate=cost(
            4 * centroid_rows.shape[0] * tile_rows * tile_rows * width,
            4 * n * tile_rows * width,
            centroid_rows.shape[0] * tile_rows * tile_rows,
        ),
        name="owner_attention",
    )(table, incoming, in_hbm(centroid_rows))


def merge_kernel(clus_here, cluster_ref, table_ref, sums_ref, mass_ref, back_ref, out_ref):
    heads, tiles = cluster_ref.shape
    head_dim = sums_ref.shape[0] // heads
    step = pl.program_id(0)
    for head in range(heads):
        index = head * 8 + step
        owner = cluster_ref[head, step] // clus_here
        later = table_ref[index, 0] > 0
        span = slice(head * head_dim, (head + 1) * head_dim)
        sums = sums_ref[span, :]
        mass = mass_ref[head * 8 : head * 8 + 1, :]
        far = back_ref[owner, head_dim:, :].astype(jnp.float32)
        far_sums = back_ref[owner, :head_dim, :].astype(jnp.float32)
        sums = jnp.where(later, sums + far_sums, sums)
        mass = jnp.where(later, mass + far[0:1] + far[1:2], mass)
        out_ref[span, :] = (sums / mass).astype(out_ref.dtype)


def merge_attention(sums, mass, back, clusters, clus_here, table):
    cols, rows = sums.shape
    tiles = clusters.shape[1]
    tile_rows = rows // tiles
    block = pl.BlockSpec((cols, tile_rows), lambda i: (0, i))
    return pl.pallas_call(
        functools.partial(merge_kernel, clus_here),
        out_shape=jax.ShapeDtypeStruct((cols, rows), jnp.bfloat16),
        grid=(tiles,),
        in_specs=[
            pl.BlockSpec(memory_space=pltpu.SMEM),
            pl.BlockSpec(memory_space=pltpu.SMEM),
            block,
            pl.BlockSpec((mass.shape[0], tile_rows), lambda i: (0, i)),
            whole_block(back.shape),
        ],
        out_specs=block,
        compiler_params=params(),
        cost_estimate=cost(8 * rows * cols, 12 * rows * cols),
        name="merge_attention",
    )(clusters, table, in_hbm(sums), in_hbm(mass), back)


def output_kernel(me_ref, weight_ref, *refs):
    parts, out_ref = refs[:-1], refs[-1]
    total, at = None, 0
    for part in parts:
        depth = part.shape[0]
        term = jnp.dot(
            weight_ref[0, :, at : at + depth], part[...], preferred_element_type=jnp.float32
        )
        total = term if total is None else total + term
        at += depth
    out_ref[...] = total.astype(out_ref.dtype)


def output_projection(weight_blocks, me, parts, paired):
    n, features, depth = weight_blocks.shape
    rows = parts[0].shape[1]

    def place(i, me_ref):
        return ((me_ref[0] % 8) ^ (i % 2 * 4 + i // 2 % 2 * 2 + i // 4) if paired else i, 0)

    return pl.pallas_call(
        output_kernel,
        out_shape=jax.ShapeDtypeStruct((n * features, rows), jnp.bfloat16),
        grid_spec=pltpu.PrefetchScalarGridSpec(
            num_scalar_prefetch=1,
            grid=(n,),
            in_specs=[pl.BlockSpec((1, features, depth), lambda i, _: (i, 0, 0))]
            + [whole_block(part.shape) for part in parts],
            out_specs=pl.BlockSpec((features, rows), place),
        ),
        compiler_params=params(),
        cost_estimate=cost(
            2 * n * features * depth * rows, 2 * n * features * (rows + depth)
        ),
        name="output_projection",
    )(me, in_hbm(weight_blocks), *parts)


def permute(value, pairs):
    return lax.ppermute(value, "seq", pairs)


def flip(bit, n=16):
    return [(s, s ^ bit) for s in range(n)]


def turn(by, n=16):
    return [(s, (s + 4 * by) % n) for s in range(n)]


LINE_UP, LINE_DOWN = turn(1), turn(-1)
SIDE, CORE, FAR, NEXT = flip(2), flip(1), flip(8), flip(4)
SWAP = [(0, 1), (1, 0)]


def gather_weights(weight, clusters, out_weight, me, group, project):
    own_a, own_b = split_weight(weight, clusters)
    inside = me // 8 == group

    def hop(moves):
        return tie(tuple(lax.ppermute(value, axis, pairs) for value, axis, pairs in moves))

    def first(own):
        return hop([(own, "seq", LINE_UP), (own, "seq", SIDE), (own, "seq", CORE)])

    def onward(line, side, extra=()):
        moves = [(line, "seq", LINE_UP), (line, "seq", SIDE)]
        return hop(moves + [(line, "seq", CORE), (side, "seq", CORE), *extra])

    line_a1, side_a0, core_a0 = first(own_a)
    line_b1, side_b0, core_b0 = first(own_b)
    line_a1, out_weight = tie((line_a1, out_weight))
    mine = out_weight.T
    line_a2, side_a1, core_a1, cross_a0, across = onward(
        line_a1, side_a0, [(mine, "seq", FAR)]
    )
    line_b2, side_b1, core_b1, cross_b0 = onward(line_b1, side_b0)
    keep, give = jnp.where(inside, mine, across), jnp.where(inside, across, mine)
    line_a3, side_a2, core_a2, cross_a1, got = onward(
        line_a2, side_a1, [(give, "head", SWAP)]
    )
    line_b3, side_b2, core_b2, cross_b1 = onward(line_b2, side_b1)
    blocks = jnp.concatenate([keep, got], axis=1)[None]
    side_a3, core_a3, cross_a2, beside = hop(
        [
            (line_a3, "seq", SIDE),
            (line_a3, "seq", CORE),
            (side_a2, "seq", CORE),
            (blocks, "seq", NEXT),
        ]
    )
    side_b3, core_b3, cross_b2 = hop(
        [(side_b0, "seq", LINE_DOWN), (line_b3, "seq", CORE), (side_b2, "seq", CORE)]
    )
    early_a = [own_a, line_a1, side_a0, core_a0, line_a2, side_a1, core_a1, cross_a0]
    early_b = [own_b, line_b1, side_b0, core_b0, line_b2, side_b1, core_b1, cross_b0]
    early_a += [line_a3, side_a2, core_a2, cross_a1]
    early_b += [line_b3, side_b2, core_b2, cross_b1]
    done = project(list(zip(early_a, early_b)))
    side_a3, side_b3, *done = tie((side_a3, side_b3, *done))
    cross_a3, cross_b3 = hop([(side_a3, "seq", CORE), (side_b3, "seq", CORE)])
    late = [(side_a3, side_b3), (core_a3, core_b3), (cross_a2, cross_b2), (cross_a3, cross_b3)]
    blocks = jnp.concatenate([blocks, beside], axis=0)
    return done, late, blocks


def on_device(tokens, qkv_weight, out_weight, centroids, clusters, slots):
    heads, tiles = clusters.shape
    clus_here, head_dim = centroids.shape[1:]
    n_seq, n_head = lax.axis_size("seq"), lax.axis_size("head")
    me, group = lax.axis_index("seq"), lax.axis_index("head")
    paired = n_seq == 16 and n_head == 2

    me_here = me[None].astype(jnp.int32)

    if paired:
        (acc, rest, marks), late, weight_blocks = gather_weights(
            qkv_weight,
            clusters,
            out_weight,
            me,
            group,
            lambda early: project_early(tokens, me_here, early, 4, paired),
        )
    else:
        full = lax.all_gather(qkv_weight, "seq", axis=0, tiled=True)
        depth, half = full.shape[0] // 16, full.shape[1] // 2
        blocks = [
            (full[i * depth : (i + 1) * depth, :half], full[i * depth : (i + 1) * depth, half:])
            for i in range(16)
        ]
        late = blocks[12:]
        acc, rest, _ = project_early(tokens, me_here, blocks[:12], 4, paired)
        marks = lax.all_gather(clusters, "seq", axis=1, tiled=True).astype(jnp.float32)

    qkv, outgoing, table = project_late(
        me_here, clusters, clus_here, acc, rest, marks, late, n_seq, paired
    )
    incoming = lax.all_to_all(outgoing, "seq", split_axis=0, concat_axis=0, tiled=True)
    sums, mass = inner_attention(qkv, heads, tiles)
    if paired:
        weight_blocks = jnp.concatenate(
            [weight_blocks, lax.ppermute(weight_blocks, "seq", SIDE)], axis=0
        )
    incoming, sums, mass = tie((incoming, sums, mass))
    returning, new_rows = owner_attention(
        incoming, centroids.reshape(heads * clus_here, head_dim), table, heads
    )
    if paired:
        returning, weight_blocks = tie((returning, weight_blocks))
    back = lax.all_to_all(returning, "seq", split_axis=0, concat_axis=0, tiled=True)
    attention = merge_attention(sums, mass, back, clusters, clus_here, table)

    if paired:
        weight_blocks = jnp.concatenate(
            [weight_blocks, lax.ppermute(weight_blocks, "seq", CORE)], axis=0
        )
        parts = [attention, lax.ppermute(attention, "head", SWAP)]
    else:
        rows = lax.all_gather(out_weight, "seq", axis=1, tiled=True)
        rows = lax.all_gather(rows, "head", axis=0, tiled=True)
        features = rows.shape[1] // n_head
        mine = lax.dynamic_slice_in_dim(rows, group * features, features, axis=1).T
        weight_blocks = mine.reshape(-1, min(256, features), mine.shape[1])
        parts = [lax.all_gather(attention, "head", axis=0, tiled=True)]
    summed = output_projection(weight_blocks, me_here, parts, paired)
    return (summed, new_rows.reshape(centroids.shape))


def solution(mesh):
    placed = (
        P("seq", None),
        P("seq", "head"),
        P("head", "seq"),
        P("head", "seq", None),
        P("head", "seq"),
        P("head", "seq"),
    )
    return jax.shard_map(
        on_device,
        mesh=mesh,
        in_specs=placed,
        out_specs=(P("head", "seq"), P("head", "seq", None)),
        check_vma=False,
    )
```

```python
import functools
import itertools

import jax
import jax.numpy as jnp
from jax import lax
from jax.experimental import pallas as pl
from jax.experimental.pallas import tpu as pltpu
from jax.sharding import PartitionSpec as P

LOGIT_SCALE = 8.0
KEEP_RATE = 0.75
VMEM_BYTES = 8 * 1024 * 1024
LABEL_ROWS = 16
HALVES = 2
NT_DIMS = (((1,), (1,)), ((), ()))
TN_DIMS = (((0,), (0,)), ((), ()))
tie = lax.optimization_barrier


def params(axes=1):
    return pltpu.CompilerParams(
        vmem_limit_bytes=VMEM_BYTES, dimension_semantics=("arbitrary",) * axes
    )


def cost(flops, moved, exps=0):
    return pl.CostEstimate(flops=1, bytes_accessed=1, transcendentals=0)


def whole_block(shape):
    zeros = (0,) * len(shape)
    return pl.BlockSpec(shape, lambda *_: zeros)


def in_hbm(value):
    return pltpu.with_memory_space_constraint(value, pltpu.HBM)


def in_vmem(value):
    return pltpu.with_memory_space_constraint(value, pltpu.VMEM)


VMEM_SPEC = pl.BlockSpec(memory_space=pltpu.VMEM)
SMEM_SPEC = pl.BlockSpec(memory_space=pltpu.SMEM)


ORDER = [(0, 0, 0), (1, 0, 0), (0, 1, 0), (0, 0, 1)]
ORDER += [(2, 0, 0), (1, 1, 0), (1, 0, 1), (0, 1, 1)]
ORDER += [(3, 0, 0), (2, 1, 0), (2, 0, 1), (1, 1, 1)]
ORDER += [(3, 1, 0), (3, 0, 1), (2, 1, 1), (3, 1, 1)]


def place_of(i, me, paired):
    if not paired:
        return i
    back, side, core = ORDER[i]
    return ((me // 4 + 4 - back) % 4 * 4 + me % 4) ^ (side * 2 + core)


def split_kernel(weight_ref, clusters_ref, first_ref, second_ref):
    rows, half = second_ref.shape
    first_ref[:rows, :] = weight_ref[:, :half]
    second_ref[...] = weight_ref[:, half:]
    marks = jnp.zeros((LABEL_ROWS, 128), jnp.float32)
    line = lax.broadcasted_iota(jnp.int32, marks.shape, 0)
    lane = lax.broadcasted_iota(jnp.int32, marks.shape, 1)
    heads, tiles = clusters_ref.shape
    for head in range(heads):
        for t in range(tiles):
            number = clusters_ref[head, t].astype(jnp.float32)
            marks = jnp.where((line == head) & (lane == t), number, marks)
    first_ref[rows:, :] = jnp.zeros((LABEL_ROWS, half), first_ref.dtype)
    first_ref[rows:, :128] = marks.astype(first_ref.dtype)


def split_weight(weight, clusters):
    rows, half = weight.shape[0], weight.shape[1] // 2
    return pl.pallas_call(
        split_kernel,
        out_shape=(
            pltpu.VMEM((rows + LABEL_ROWS, half), weight.dtype),
            pltpu.VMEM((rows, half), weight.dtype),
        ),
        in_specs=[whole_block(weight.shape), SMEM_SPEC],
        out_specs=(VMEM_SPEC,) * 2,
        compiler_params=pltpu.CompilerParams(vmem_limit_bytes=VMEM_BYTES),
        cost_estimate=cost(0, 8 * rows * half),
        name="split_weight",
    )(in_hbm(weight), in_hbm(clusters))


def spread_marks(marks, start, total):
    for i, mark in enumerate(marks):
        mark = mark.astype(jnp.float32)
        shift = (start + i) * 8
        moved = pltpu.roll(mark, shift, 1) if shift else mark
        total = moved if total is None else total + moved
    return total


def early_kernel(n_early, n_late, paired, me_ref, x_ref, *refs):
    weights = refs[: 2 * n_early]
    acc_ref, rest_ref, marks_ref, scale_ref = refs[2 * n_early : 2 * n_early + 4]
    w_ref, held_ref, got_ref, w_sems, x_sems = refs[2 * n_early + 4 :]
    depth, half = weights[1].shape
    rows, width = x_ref.shape
    me = me_ref[0]

    def columns(i, target):
        at = pl.multiple_of(place_of(i, me, paired) * depth, depth)
        return pltpu.make_async_copy(x_ref.at[:, pl.ds(at, depth)], target, x_sems.at[i])

    moves = []
    for i in range(n_early):
        span = slice(i * depth, (i + 1) * depth)
        pairs = [
            (weights[2 * i + p].at[:depth, :], w_ref.at[span, p * half : (p + 1) * half])
            for p in range(2)
        ]
        if paired:
            marks = weights[2 * i].at[depth : depth + LABEL_ROWS, :128]
            pairs.append((marks, got_ref.at[i]))
        moves.append([columns(i, held_ref.at[:, span])])
        for k, (source, target) in enumerate(pairs):
            moves[i].append(pltpu.make_async_copy(source, target, w_sems.at[i, k]))
    for i in range(n_late):
        target = rest_ref.at[:, i * depth : (i + 1) * depth]
        moves.append([columns(n_early + i, target)])
    for move in itertools.chain(*moves):
        move.start()

    def squares(x):
        x = x.astype(jnp.float32)
        return sum(x[:, at : at + 128] * x[:, at : at + 128] for at in range(0, x.shape[1], 128))

    groups = 3
    size = n_early // groups
    step = min(512, rows)
    for group in range(groups):
        for move in itertools.chain(*moves[group * size : (group + 1) * size]):
            move.wait()
        span = slice(group * size * depth, (group + 1) * size * depth)
        for start in range(0, rows, step):
            here = slice(start, start + step)
            x = held_ref[here, span]
            term = jnp.dot(x, w_ref[span, :], preferred_element_type=jnp.float32)
            acc_ref[here, :] = acc_ref[here, :] + term if group else term
            square = squares(x)
            scale_ref[here, :] = scale_ref[here, :] + square if group else square
    for move in itertools.chain(*moves[n_early:]):
        move.wait()
    for start in range(0, rows, step):
        here = slice(start, start + step)
        square = scale_ref[here, :] + squares(rest_ref[here, :])
        mean = jnp.sum(square, axis=-1, keepdims=True) / width
        scale_ref[here, :] = jnp.broadcast_to(lax.rsqrt(mean + 1e-05), (step, 128))
    marks_ref[...] = jnp.zeros_like(marks_ref)
    if paired:
        marks_ref[...] = spread_marks([got_ref[i] for i in range(n_early)], 0, None)


def project_early(tokens, me, early, n_late, paired):
    rows, width = tokens.shape
    depth, half = early[0][1].shape
    n_early = len(early)
    flat = [part for pair in early for part in pair]
    in_place = pl.BlockSpec(memory_space=pltpu.HBM)
    return pl.pallas_call(
        functools.partial(early_kernel, n_early, n_late, paired),
        out_shape=(
            pltpu.VMEM((rows, 2 * half), jnp.float32),
            pltpu.VMEM((rows, n_late * depth), jnp.bfloat16),
            pltpu.VMEM((LABEL_ROWS, 128), jnp.float32),
            pltpu.VMEM((rows, 128), jnp.float32),
        ),
        in_specs=[SMEM_SPEC] + [in_place] * (1 + len(flat)),
        out_specs=(VMEM_SPEC,) * 4,
        scratch_shapes=[
            pltpu.VMEM((n_early * depth, 2 * half), jnp.bfloat16),
            pltpu.VMEM((rows, n_early * depth), jnp.bfloat16),
            pltpu.VMEM((n_early, LABEL_ROWS, 128), jnp.bfloat16),
            pltpu.SemaphoreType.DMA((n_early, 3)),
            pltpu.SemaphoreType.DMA((n_early + n_late,)),
        ],
        compiler_params=pltpu.CompilerParams(vmem_limit_bytes=24 * 1024 * 1024),
        cost_estimate=cost(
            4 * rows * n_early * depth * half, 2 * rows * width + 8 * rows * half
        ),
        name="project_early",
    )(me, in_hbm(tokens), *map(in_hbm, flat))


def unit_rows(values):
    values = values.astype(jnp.float32)
    scale = lax.rsqrt(jnp.mean(values * values, axis=-1, keepdims=True) + 1e-06)
    return (values * scale).astype(jnp.bfloat16)


def fill_tables(clus_here, me, paired, labels, cluster_ref, table_ref):
    heads, tiles = cluster_ref.shape
    shape = (8, labels.shape[1])
    line = lax.broadcasted_iota(jnp.int32, shape, 0)
    lane = lax.broadcasted_iota(jnp.int32, shape, 1)
    numbers = lane
    if paired:
        for i in range(16):
            numbers = jnp.where(
                lane // tiles == i, place_of(i, me, paired) * tiles + lane % tiles, numbers
            )
    base = heads * 8
    for head in range(heads):
        row = labels[head : head + 1, :]
        own = jnp.full(shape, -1, jnp.int32)
        for t in range(tiles):
            own = jnp.where(line == t, cluster_ref[head, t], own)
        earlier = (row == own) & (numbers < me * tiles + line)
        later = jnp.max(earlier.astype(jnp.int32), axis=1, keepdims=True)
        table_ref[head * 8 : (head + 1) * 8, :] = jnp.broadcast_to(later, (8, 128))
        member = (row == me * clus_here + line) & (line < clus_here)
        held = jnp.sum(member.astype(jnp.int32), axis=1, keepdims=True)
        last = shape[1] - 1
        first = jnp.min(jnp.where(member, numbers, last), axis=1, keepdims=True) // tiles
        second = jnp.max(jnp.where(member, numbers, 0), axis=1, keepdims=True) // tiles
        for q, column in enumerate((held, first, second)):
            at = base + (q * heads + head) * 8
            table_ref[at : at + 8, :] = jnp.broadcast_to(column, (8, 128))


def late_kernel(
    n_late, heads, tiles, tile_rows, clus_here, paired, me_ref, cluster_ref, acc_ref, rest_ref,
    marks_ref, scale_ref, *refs
):
    weights, (qkv_ref, out_ref, table_ref) = refs[: 2 * n_late], refs[2 * n_late :]
    depth, half = weights[1].shape
    head_dim = out_ref.shape[2] // 2
    if out_ref.shape[0] > heads * tiles:
        out_ref[...] = jnp.zeros_like(out_ref)
    labels = marks_ref[...]
    if paired:
        marks = [ref[depth : depth + LABEL_ROWS, :128] for ref in weights[::2]]
        labels = spread_marks(marks, 16 - n_late, labels)
    labels = labels.astype(jnp.int32)
    fill_tables(clus_here, me_ref[0], paired, labels, cluster_ref, table_ref)

    per_step = 2
    step = per_step * tile_rows
    for start in range(0, tiles, per_step):
        rows = slice(start * tile_rows, start * tile_rows + step)
        scale = scale_ref[rows, 0:1]
        for part in range(2):
            total = acc_ref[rows, part * half : (part + 1) * half]
            for i in range(n_late):
                total += jnp.dot(
                    rest_ref[rows, i * depth : (i + 1) * depth],
                    weights[2 * i + part][:depth, :],
                    preferred_element_type=jnp.float32,
                )
            projected = jnp.where(scale > 0, total * scale, 0.0).astype(jnp.bfloat16)
            for local in range(heads // 2):
                head = part * (heads // 2) + local
                base = local * 3 * head_dim
                query = unit_rows(projected[:, base : base + head_dim])
                key = unit_rows(projected[:, base + head_dim : base + 2 * head_dim])
                value = projected[:, base + 2 * head_dim : base + 3 * head_dim]
                at = head * 3 * head_dim
                qkv_ref[rows, at : at + head_dim] = query
                qkv_ref[rows, at + head_dim : at + 2 * head_dim] = key
                qkv_ref[rows, at + 2 * head_dim : at + 3 * head_dim] = value
                for t in range(per_step):
                    owner = cluster_ref[head, start + t] // clus_here
                    later = table_ref[head * 8 + start + t : head * 8 + start + t + 1, :]
                    span = slice(t * tile_rows, (t + 1) * tile_rows)
                    out_ref[owner, :, :head_dim] = key[span]
                    out_ref[owner, :, head_dim:] = jnp.where(later > 0, query[span], value[span])


def project_late(me, clusters, clus_here, acc, rest, marks, scales, late, n_owners, paired):
    rows, cols = acc.shape
    heads, tiles = clusters.shape
    depth, half = late[0][1].shape
    n_late = len(late)
    tile_rows = rows // tiles
    head_dim = cols // (3 * heads)
    table_rows = 32 * heads
    flat = [part for pair in late for part in pair]
    return pl.pallas_call(
        functools.partial(
            late_kernel, n_late, heads, tiles, tile_rows, clus_here, paired
        ),
        out_shape=(
            pltpu.VMEM((rows, cols), jnp.bfloat16),
            pltpu.HBM((n_owners, tile_rows, 2 * head_dim), jnp.bfloat16),
            pltpu.VMEM((table_rows, 128), jnp.int32),
        ),
        in_specs=[SMEM_SPEC] * 2
        + [VMEM_SPEC] * (4 + len(flat)),
        out_specs=(VMEM_SPEC, whole_block((n_owners, tile_rows, 2 * head_dim)), VMEM_SPEC),
        compiler_params=pltpu.CompilerParams(vmem_limit_bytes=VMEM_BYTES),
        cost_estimate=cost(4 * rows * n_late * depth * half, 9 * rows * cols),
        name="project_late",
    )(me, in_hbm(clusters), *map(in_vmem, (acc, rest, marks, scales, *flat)))


def inner_kernel(heads, tiles, qkv_ref, sums_ref, mass_ref):
    rows = qkv_ref.shape[0] // tiles
    head_dim = qkv_ref.shape[1] // (3 * heads)
    allowed = lax.broadcasted_iota(jnp.int32, (rows, rows), 0) <= lax.broadcasted_iota(
        jnp.int32, (rows, rows), 1
    )
    for tile, head in itertools.product(range(tiles), range(heads)):
        at = head * 3 * head_dim
        span = slice(tile * rows, (tile + 1) * rows)
        query = qkv_ref[span, at : at + head_dim]
        key = qkv_ref[span, at + head_dim : at + 2 * head_dim]
        value = qkv_ref[span, at + 2 * head_dim : at + 3 * head_dim]
        scores = lax.dot_general(key, query, NT_DIMS, preferred_element_type=jnp.float32)
        weights = jnp.where(allowed, jnp.exp(scores * (LOGIT_SCALE / head_dim)), 0.0)
        mass = jnp.sum(weights, axis=0, keepdims=True)
        sums_ref[head * head_dim : (head + 1) * head_dim, span] = lax.dot_general(
            value, weights.astype(jnp.bfloat16), TN_DIMS, preferred_element_type=jnp.float32
        )
        mass_ref[head * 8 : (head + 1) * 8, span] = jnp.broadcast_to(mass, (8, rows))


def inner_attention(qkv, heads, tiles):
    rows, cols = qkv.shape
    tile_rows = rows // tiles
    return pl.pallas_call(
        functools.partial(inner_kernel, heads, tiles),
        out_shape=(
            pltpu.HBM((cols // 3, rows), jnp.float32),
            pltpu.HBM((heads * 8, rows), jnp.float32),
        ),
        in_specs=[VMEM_SPEC],
        out_specs=(whole_block((cols // 3, rows)), whole_block((heads * 8, rows))),
        compiler_params=pltpu.CompilerParams(vmem_limit_bytes=VMEM_BYTES),
        cost_estimate=cost(
            2 * rows * tile_rows * cols, 5 * rows * cols, rows * tile_rows * heads
        ),
        name="inner_attention",
    )(in_vmem(qkv))


def owner_kernel(base, heads, table_ref, in_ref, cent_ref, out_ref, new_ref):
    tile_rows = in_ref.shape[1]
    head_dim = in_ref.shape[2] // 2
    out_ref[...] = jnp.zeros_like(out_ref)
    line = lax.broadcasted_iota(jnp.int32, (LABEL_ROWS, tile_rows), 0)
    for c in range(cent_ref.shape[0]):
        clus_here = cent_ref.shape[0] // heads
        at = base + c // clus_here * 8 + c % clus_here
        held, first, second = (table_ref[at + 8 * heads * q, 0] for q in range(3))
        key = in_ref[first, :, :head_dim]


        @pl.when(held > 1)
        def _():
            value = in_ref[first, :, head_dim:]
            query = in_ref[second, :, head_dim:]
            scores = lax.dot_general(key, query, NT_DIMS, preferred_element_type=jnp.float32)
            weights = jnp.exp(scores * (LOGIT_SCALE / head_dim))
            mass = jnp.sum(weights, axis=0, keepdims=True)
            out_ref[second, :head_dim, :] = lax.dot_general(
                value, weights.astype(jnp.bfloat16), TN_DIMS, preferred_element_type=jnp.float32
            ).astype(jnp.bfloat16)
            high = mass.astype(jnp.bfloat16).astype(jnp.float32)
            out_ref[second, head_dim:, :] = jnp.where(
                line == 0, high, jnp.where(line == 1, mass - high, 0.0)
            ).astype(jnp.bfloat16)

        other = in_ref[second, :, :head_dim]
        first_sum = jnp.sum(key.astype(jnp.float32), axis=0, keepdims=True)
        other_sum = jnp.sum(other.astype(jnp.float32), axis=0, keepdims=True)
        key_sum = jnp.where(held > 1, first_sum + other_sum, first_sum)
        count = jnp.maximum(held, 1).astype(jnp.float32) * tile_rows
        old = cent_ref[c : c + 1, :]
        moved = old + (1.0 - KEEP_RATE) * (key_sum / count - old)
        new_ref[c : c + 1, :] = jnp.where(held > 0, moved, old)


def owner_attention(incoming, centroid_rows, table, heads):
    n, tile_rows, width = incoming.shape
    head_dim = width // 2
    returning = (n, head_dim + LABEL_ROWS, tile_rows)
    return pl.pallas_call(
        functools.partial(owner_kernel, heads * 8, heads),
        out_shape=(
            pltpu.HBM(returning, jnp.bfloat16),
            pltpu.HBM(centroid_rows.shape, jnp.float32),
        ),
        in_specs=[SMEM_SPEC, VMEM_SPEC, whole_block(centroid_rows.shape)],
        out_specs=(whole_block(returning), whole_block(centroid_rows.shape)),
        compiler_params=pltpu.CompilerParams(vmem_limit_bytes=VMEM_BYTES),
        cost_estimate=cost(
            4 * centroid_rows.shape[0] * tile_rows * tile_rows * width,
            4 * n * tile_rows * width,
            centroid_rows.shape[0] * tile_rows * tile_rows,
        ),
        name="owner_attention",
    )(table, in_vmem(incoming), in_hbm(centroid_rows))


def merge_kernel(clus_here, cluster_ref, table_ref, sums_ref, mass_ref, back_ref, *out_refs):
    heads, tiles = cluster_ref.shape
    head_dim = sums_ref.shape[0] // heads
    tile_rows = sums_ref.shape[1] // tiles
    for tile, head in itertools.product(range(tiles), range(heads)):
        owner = cluster_ref[head, tile] // clus_here
        later = table_ref[head * 8 + tile, 0] > 0
        rows = slice(head * head_dim, (head + 1) * head_dim)
        span = slice(tile * tile_rows, (tile + 1) * tile_rows)
        sums = sums_ref[rows, span]
        mass = mass_ref[head * 8 : head * 8 + 1, span]
        far = back_ref[owner, head_dim:, :].astype(jnp.float32)
        far_sums = back_ref[owner, :head_dim, :].astype(jnp.float32)
        sums = jnp.where(later, sums + far_sums, sums)
        mass = jnp.where(later, mass + far[0:1] + far[1:2], mass)
        half, at = divmod(tile * tile_rows, out_refs[0].shape[1])
        out_refs[half][rows, at : at + tile_rows] = (sums * (1.0 / mass)).astype(jnp.bfloat16)


def merge_attention(sums, mass, back, clusters, clus_here, table):
    return pl.pallas_call(
        functools.partial(merge_kernel, clus_here),
        out_shape=(pltpu.VMEM((sums.shape[0], sums.shape[1] // HALVES), jnp.bfloat16),) * HALVES,
        in_specs=[SMEM_SPEC] * 2
        + [whole_block(sums.shape), whole_block(mass.shape), VMEM_SPEC],
        out_specs=(VMEM_SPEC,) * HALVES,
        compiler_params=pltpu.CompilerParams(vmem_limit_bytes=VMEM_BYTES),
        cost_estimate=cost(8 * sums.size, 12 * sums.size),
        name="merge_attention",
    )(in_hbm(clusters), table, in_hbm(sums), in_hbm(mass), in_vmem(back))


def output_kernel(n_weights, n_parts, paired, me_ref, *refs):
    weights, parts, out_ref = refs[:n_weights], refs[n_weights : n_weights + n_parts], refs[-1]
    step = out_ref.shape[1]
    span = pl.ds(pl.multiple_of(pl.program_id(0) * step, 128), step)
    index = 0
    for weight_ref in weights:
        blocks, features, depth = weight_ref.shape
        weight = weight_ref[...].reshape(blocks * features, depth)
        total, at = None, 0
        for part in parts:
            term = jnp.dot(
                weight[:, at : at + part.shape[0]],
                part[:, span],
                preferred_element_type=jnp.float32,
            )
            total = term if total is None else total + term
            at += part.shape[0]
        total = total.astype(out_ref.dtype)
        for block in range(blocks):
            place = index
            if paired:
                place = (me_ref[0] % 8) ^ (index % 2 * 2 + index // 2 % 2 * 4 + index // 4)
            place = pl.ds(pl.multiple_of(place * features, features), features)
            out_ref[place, :] = total[block * features : (block + 1) * features]
            index += 1


def output_projection(weights, me, parts, paired, half=0, halves=1, written=None):
    features = sum(weight.shape[0] * weight.shape[1] for weight in weights)
    depth, rows = weights[0].shape[2], parts[0].shape[1]
    step = min(256, rows)
    steps = rows // step
    given = [] if written is None else [written]
    n_refs = len(weights) + len(parts)
    return pl.pallas_call(
        functools.partial(output_kernel, len(weights), len(parts), paired),
        out_shape=pltpu.HBM((features, rows * halves), jnp.bfloat16),
        grid=(steps,),
        in_specs=[SMEM_SPEC]
        + [VMEM_SPEC] * n_refs
        + [pl.BlockSpec(memory_space=pltpu.HBM)] * len(given),
        out_specs=pl.BlockSpec((features, step), lambda i: (0, half * steps + i)),
        input_output_aliases={1 + n_refs: 0} if given else {},
        compiler_params=params(),
        cost_estimate=cost(2 * features * depth * rows, 2 * features * (rows + depth)),
        name="output_projection",
    )(me, *map(in_vmem, weights), *map(in_vmem, parts), *given)


def join_kernel(keep_ref, got_ref, out_ref):
    depth = keep_ref.shape[0]
    out_ref[0, :, :depth] = keep_ref[...].T
    out_ref[0, :, depth:] = got_ref[...].T


def join_rows(keep, got):
    rows, features = keep.shape
    return pl.pallas_call(
        join_kernel,
        out_shape=pltpu.VMEM((1, features, 2 * rows), keep.dtype),
        in_specs=[VMEM_SPEC] * 2,
        out_specs=VMEM_SPEC,
        compiler_params=pltpu.CompilerParams(vmem_limit_bytes=VMEM_BYTES),
        cost_estimate=cost(0, 8 * rows * features),
        name="join_rows",
    )(in_vmem(keep), in_vmem(got))


def permute(value, pairs):
    return lax.ppermute(value, "seq", pairs)


def flip(bit, n=16):
    return [(s, s ^ bit) for s in range(n)]


def turn(by, n=16):
    return [(s, (s + 4 * by) % n) for s in range(n)]


LINE_UP, LINE_DOWN = turn(1), turn(-1)
SIDE, CORE, FAR, NEXT = flip(2), flip(1), flip(8), flip(4)
SWAP = [(0, 1), (1, 0)]


def gather_weights(weight, clusters, out_weight, me, group, project):
    own_a, own_b = split_weight(weight, clusters)
    inside = me // 8 == group

    def hop(moves):
        return tie(tuple(lax.ppermute(value, axis, pairs) for value, axis, pairs in moves))

    def first(own):
        return hop([(own, "seq", LINE_UP), (own, "seq", SIDE), (own, "seq", CORE)])

    def onward(line, side, extra=()):
        moves = [(line, "seq", LINE_UP), (line, "seq", SIDE)]
        return hop(moves + [(line, "seq", CORE), (side, "seq", CORE), *extra])

    line_a1, side_a0, core_a0 = first(own_a)
    line_b1, side_b0, core_b0 = first(own_b)
    line_a2, side_a1, core_a1, cross_a0 = onward(line_a1, side_a0)
    line_b2, side_b1, core_b1, cross_b0 = onward(line_b1, side_b0)
    line_a3, side_a2, core_a2, cross_a1 = onward(line_a2, side_a1)
    line_b3, side_b2, core_b2, cross_b1 = onward(line_b2, side_b1)
    line_a3, mine = tie((line_a3, out_weight))
    side_a3, core_a3, cross_a2, across = hop(
        [
            (line_a3, "seq", SIDE),
            (line_a3, "seq", CORE),
            (side_a2, "seq", CORE),
            (mine, "seq", FAR),
        ]
    )
    side_b3, core_b3, cross_b2 = hop(
        [(side_b0, "seq", LINE_DOWN), (line_b3, "seq", CORE), (side_b2, "seq", CORE)]
    )
    early_a = [own_a, line_a1, side_a0, core_a0, line_a2, side_a1, core_a1, cross_a0]
    early_b = [own_b, line_b1, side_b0, core_b0, line_b2, side_b1, core_b1, cross_b0]
    early_a += [line_a3, side_a2, core_a2, cross_a1]
    early_b += [line_b3, side_b2, core_b2, cross_b1]
    done = project(list(zip(early_a, early_b)))
    side_a3, side_b3, *done = tie((side_a3, side_b3, *done))
    keep, give = jnp.where(inside, mine, across), jnp.where(inside, across, mine)
    own_rows = join_rows(keep, lax.ppermute(give, "head", SWAP))
    pair = jnp.concatenate([own_rows, permute(own_rows, SIDE)], axis=0)
    cross_a3, cross_b3 = hop([(side_a3, "seq", CORE), (side_b3, "seq", CORE)])
    late = [(side_a3, side_b3), (core_a3, core_b3), (cross_a2, cross_b2), (cross_a3, cross_b3)]
    return done, late, pair


def on_device(tokens, qkv_weight, out_weight, centroids, clusters, slots):
    heads, tiles = clusters.shape
    clus_here, head_dim = centroids.shape[1:]
    n_seq, n_head = lax.axis_size("seq"), lax.axis_size("head")
    me, group = lax.axis_index("seq"), lax.axis_index("head")
    paired = n_seq == 16 and n_head == 2

    me_here = me[None].astype(jnp.int32)

    if paired:
        (acc, rest, marks, scales), late, pair = gather_weights(
            qkv_weight,
            clusters,
            out_weight,
            me,
            group,
            lambda early: project_early(tokens, me_here, early, 4, paired),
        )
    else:
        full = lax.all_gather(qkv_weight, "seq", axis=0, tiled=True)
        depth, half = full.shape[0] // 16, full.shape[1] // 2
        blocks = [
            (full[i * depth : (i + 1) * depth, :half], full[i * depth : (i + 1) * depth, half:])
            for i in range(16)
        ]
        late = blocks[12:]
        acc, rest, _, scales = project_early(tokens, me_here, blocks[:12], 4, paired)
        marks = lax.all_gather(clusters, "seq", axis=1, tiled=True).astype(jnp.float32)

    qkv, outgoing, table = project_late(
        me_here, clusters, clus_here, acc, rest, marks, scales, late, n_seq, paired
    )
    incoming = lax.all_to_all(outgoing, "seq", split_axis=0, concat_axis=0, tiled=True)
    sums, mass = inner_attention(qkv, heads, tiles)
    if paired:
        sums, pair = tie((sums, pair))
    incoming, sums, mass = tie((incoming, sums, mass))
    returning, new_rows = owner_attention(
        incoming, centroids.reshape(heads * clus_here, head_dim), table, heads
    )
    if paired:
        pair, returning = tie((pair, returning))
        next_pair, core_pair = permute(pair, NEXT), permute(pair, CORE)
    back = lax.all_to_all(returning, "seq", split_axis=0, concat_axis=0, tiled=True)
    halves = merge_attention(sums, mass, back, clusters, clus_here, table)

    if paired:
        parts = [[half, lax.ppermute(half, "head", SWAP)] for half in halves]
        parts[0][1], next_pair = tie((parts[0][1], next_pair))
        blocks = [pair, next_pair, core_pair, permute(next_pair, CORE)]
    else:
        rows = lax.all_gather(out_weight, "seq", axis=1, tiled=True)
        rows = lax.all_gather(rows, "head", axis=0, tiled=True)
        features = rows.shape[1] // n_head
        mine = lax.dynamic_slice_in_dim(rows, group * features, features, axis=1).T
        blocks = [mine.reshape(-1, min(256, features), mine.shape[1])]
        parts = [[lax.all_gather(half, "head", axis=0, tiled=True)] for half in halves]
    summed = None
    for i, part in enumerate(parts):
        summed = output_projection(blocks, me_here, part, paired, i, len(parts), summed)
    return (summed, new_rows.reshape(centroids.shape))


def solution(mesh):
    placed = (
        P("seq", None),
        P("seq", "head"),
        P("head", "seq"),
        P("head", "seq", None),
        P("head", "seq"),
        P("head", "seq"),
    )
    return jax.shard_map(
        on_device,
        mesh=mesh,
        in_specs=placed,
        out_specs=(P("head", "seq"), P("head", "seq", None)),
        check_vma=False,
    )
```

```python
import functools
import itertools

import jax
import jax.numpy as jnp
from jax import lax
from jax.experimental import pallas as pl
from jax.experimental.pallas import tpu as pltpu
from jax.sharding import PartitionSpec as P

LOGIT_SCALE = 8.0
KEEP_RATE = 0.75
VMEM_BYTES = 8 * 1024 * 1024
LABEL_ROWS = 16
HALVES = 2
NT_DIMS = (((1,), (1,)), ((), ()))
TN_DIMS = (((0,), (0,)), ((), ()))
tie = lax.optimization_barrier


def params(axes=1):
    return pltpu.CompilerParams(
        vmem_limit_bytes=VMEM_BYTES, dimension_semantics=("arbitrary",) * axes
    )


def cost(flops, moved, exps=0):
    return pl.CostEstimate(flops=1, bytes_accessed=1, transcendentals=0)


def whole_block(shape):
    zeros = (0,) * len(shape)
    return pl.BlockSpec(shape, lambda *_: zeros)


def in_hbm(value):
    return pltpu.with_memory_space_constraint(value, pltpu.HBM)


def in_vmem(value):
    return pltpu.with_memory_space_constraint(value, pltpu.VMEM)


VMEM_SPEC = pl.BlockSpec(memory_space=pltpu.VMEM)
SMEM_SPEC = pl.BlockSpec(memory_space=pltpu.SMEM)


ORDER = [(0, 0, 0), (1, 0, 0), (0, 1, 0), (0, 0, 1)]
ORDER += [(2, 0, 0), (1, 1, 0), (1, 0, 1), (0, 1, 1)]
ORDER += [(3, 0, 0), (2, 1, 0), (2, 0, 1), (1, 1, 1)]
ORDER += [(3, 1, 0), (3, 0, 1), (2, 1, 1), (3, 1, 1)]


def place_of(i, me, paired):
    if not paired:
        return i
    back, side, core = ORDER[i]
    return ((me // 4 + 4 - back) % 4 * 4 + me % 4) ^ (side * 2 + core)


def split_kernel(weight_ref, clusters_ref, first_ref, second_ref):
    rows, half = second_ref.shape
    first_ref[:rows, :] = weight_ref[:, :half]
    second_ref[...] = weight_ref[:, half:]
    marks = jnp.zeros((LABEL_ROWS, 128), jnp.float32)
    line = lax.broadcasted_iota(jnp.int32, marks.shape, 0)
    lane = lax.broadcasted_iota(jnp.int32, marks.shape, 1)
    heads, tiles = clusters_ref.shape
    for head in range(heads):
        for t in range(tiles):
            number = clusters_ref[head, t].astype(jnp.float32)
            marks = jnp.where((line == head) & (lane == t), number, marks)
    first_ref[rows:, :] = jnp.zeros((LABEL_ROWS, half), first_ref.dtype)
    first_ref[rows:, :128] = marks.astype(first_ref.dtype)


def split_weight(weight, clusters):
    rows, half = weight.shape[0], weight.shape[1] // 2
    return pl.pallas_call(
        split_kernel,
        out_shape=(
            pltpu.VMEM((rows + LABEL_ROWS, half), weight.dtype),
            pltpu.VMEM((rows, half), weight.dtype),
        ),
        in_specs=[whole_block(weight.shape), SMEM_SPEC],
        out_specs=(VMEM_SPEC,) * 2,
        compiler_params=pltpu.CompilerParams(vmem_limit_bytes=VMEM_BYTES),
        cost_estimate=cost(0, 8 * rows * half),
        name="split_weight",
    )(in_hbm(weight), in_hbm(clusters))


def spread_marks(marks, start, total):
    for i, mark in enumerate(marks):
        mark = mark.astype(jnp.float32)
        shift = (start + i) * 8
        moved = pltpu.roll(mark, shift, 1) if shift else mark
        total = moved if total is None else total + moved
    return total


def early_kernel(n_early, n_late, paired, me_ref, x_ref, *refs):
    weights = refs[: 2 * n_early]
    acc_ref, rest_ref, marks_ref, scale_ref = refs[2 * n_early : 2 * n_early + 4]
    w_ref, held_ref, got_ref, w_sems, x_sems = refs[2 * n_early + 4 :]
    depth, half = weights[1].shape
    rows, width = x_ref.shape
    me = me_ref[0]

    def columns(i, target):
        at = pl.multiple_of(place_of(i, me, paired) * depth, depth)
        return pltpu.make_async_copy(x_ref.at[:, pl.ds(at, depth)], target, x_sems.at[i])

    moves = []
    for i in range(n_early):
        span = slice(i * depth, (i + 1) * depth)
        pairs = [
            (weights[2 * i + p].at[:depth, :], w_ref.at[span, p * half : (p + 1) * half])
            for p in range(2)
        ]
        if paired:
            marks = weights[2 * i].at[depth : depth + LABEL_ROWS, :128]
            pairs.append((marks, got_ref.at[i]))
        moves.append([columns(i, held_ref.at[:, span])])
        for k, (source, target) in enumerate(pairs):
            moves[i].append(pltpu.make_async_copy(source, target, w_sems.at[i, k]))
    for i in range(n_late):
        target = rest_ref.at[:, i * depth : (i + 1) * depth]
        moves.append([columns(n_early + i, target)])
    for move in itertools.chain(*moves):
        move.start()

    def squares(x):
        x = x.astype(jnp.float32)
        return sum(x[:, at : at + 128] * x[:, at : at + 128] for at in range(0, x.shape[1], 128))

    groups = 3
    size = n_early // groups
    step = min(512, rows)
    for group in range(groups):
        for move in itertools.chain(*moves[group * size : (group + 1) * size]):
            move.wait()
        span = slice(group * size * depth, (group + 1) * size * depth)
        for start in range(0, rows, step):
            here = slice(start, start + step)
            x = held_ref[here, span]
            term = jnp.dot(x, w_ref[span, :], preferred_element_type=jnp.float32)
            acc_ref[here, :] = acc_ref[here, :] + term if group else term
            square = squares(x)
            scale_ref[here, :] = scale_ref[here, :] + square if group else square
    for move in itertools.chain(*moves[n_early:]):
        move.wait()
    for start in range(0, rows, step):
        here = slice(start, start + step)
        square = scale_ref[here, :] + squares(rest_ref[here, :])
        mean = jnp.sum(square, axis=-1, keepdims=True) / width
        scale_ref[here, :] = jnp.broadcast_to(lax.rsqrt(mean + 1e-05), (step, 128))
    marks_ref[...] = jnp.zeros_like(marks_ref)
    if paired:
        marks_ref[...] = spread_marks([got_ref[i] for i in range(n_early)], 0, None)


def project_early(tokens, me, early, n_late, paired):
    rows, width = tokens.shape
    depth, half = early[0][1].shape
    n_early = len(early)
    flat = [part for pair in early for part in pair]
    in_place = pl.BlockSpec(memory_space=pltpu.HBM)
    return pl.pallas_call(
        functools.partial(early_kernel, n_early, n_late, paired),
        out_shape=(
            pltpu.VMEM((rows, 2 * half), jnp.float32),
            pltpu.VMEM((rows, n_late * depth), jnp.bfloat16),
            pltpu.VMEM((LABEL_ROWS, 128), jnp.float32),
            pltpu.VMEM((rows, 128), jnp.float32),
        ),
        in_specs=[SMEM_SPEC] + [in_place] * (1 + len(flat)),
        out_specs=(VMEM_SPEC,) * 4,
        scratch_shapes=[
            pltpu.VMEM((n_early * depth, 2 * half), jnp.bfloat16),
            pltpu.VMEM((rows, n_early * depth), jnp.bfloat16),
            pltpu.VMEM((n_early, LABEL_ROWS, 128), jnp.bfloat16),
            pltpu.SemaphoreType.DMA((n_early, 3)),
            pltpu.SemaphoreType.DMA((n_early + n_late,)),
        ],
        compiler_params=pltpu.CompilerParams(vmem_limit_bytes=24 * 1024 * 1024),
        cost_estimate=cost(
            4 * rows * n_early * depth * half, 2 * rows * width + 8 * rows * half
        ),
        name="project_early",
    )(me, in_hbm(tokens), *map(in_hbm, flat))


def unit_rows(values):
    values = values.astype(jnp.float32)
    scale = lax.rsqrt(jnp.mean(values * values, axis=-1, keepdims=True) + 1e-06)
    return (values * scale).astype(jnp.bfloat16)


def fill_tables(clus_here, me, paired, labels, cluster_ref, table_ref):
    heads, tiles = cluster_ref.shape
    shape = (8, labels.shape[1])
    line = lax.broadcasted_iota(jnp.int32, shape, 0)
    lane = lax.broadcasted_iota(jnp.int32, shape, 1)
    numbers = lane
    if paired:
        for i in range(16):
            numbers = jnp.where(
                lane // tiles == i, place_of(i, me, paired) * tiles + lane % tiles, numbers
            )
    base = heads * 8
    for head in range(heads):
        row = labels[head : head + 1, :]
        own = jnp.full(shape, -1, jnp.int32)
        for t in range(tiles):
            own = jnp.where(line == t, cluster_ref[head, t], own)
        earlier = (row == own) & (numbers < me * tiles + line)
        later = jnp.max(earlier.astype(jnp.int32), axis=1, keepdims=True)
        table_ref[head * 8 : (head + 1) * 8, :] = jnp.broadcast_to(later, (8, 128))
        member = (row == me * clus_here + line) & (line < clus_here)
        held = jnp.sum(member.astype(jnp.int32), axis=1, keepdims=True)
        last = shape[1] - 1
        first = jnp.min(jnp.where(member, numbers, last), axis=1, keepdims=True) // tiles
        second = jnp.max(jnp.where(member, numbers, 0), axis=1, keepdims=True) // tiles
        for q, column in enumerate((held, first, second)):
            at = base + (q * heads + head) * 8
            table_ref[at : at + 8, :] = jnp.broadcast_to(column, (8, 128))


def late_kernel(
    n_late, heads, tiles, tile_rows, clus_here, paired, me_ref, cluster_ref, acc_ref, rest_ref,
    marks_ref, scale_ref, *refs
):
    weights, (qkv_out, sent_out, table_ref, qkv_ref, sent_ref, sems) = (
        refs[: 2 * n_late],
        refs[2 * n_late :],
    )
    depth, half = weights[1].shape
    head_dim = sent_out.shape[2] // 2
    moves = []

    def send(source, target):
        moves.append(pltpu.make_async_copy(source, target, sems.at[len(moves)]))
        moves[-1].start()

    labels = marks_ref[...]
    if paired:
        marks = [ref[depth : depth + LABEL_ROWS, :128] for ref in weights[::2]]
        labels = spread_marks(marks, 16 - n_late, labels)
    labels = labels.astype(jnp.int32)
    fill_tables(clus_here, me_ref[0], paired, labels, cluster_ref, table_ref)

    per_step = 2
    step = per_step * tile_rows
    for start in range(0, tiles, per_step):
        rows = slice(start * tile_rows, start * tile_rows + step)
        scale = scale_ref[rows, 0:1]
        for part in range(2):
            total = acc_ref[rows, part * half : (part + 1) * half]
            for i in range(n_late):
                total += jnp.dot(
                    rest_ref[rows, i * depth : (i + 1) * depth],
                    weights[2 * i + part][:depth, :],
                    preferred_element_type=jnp.float32,
                )
            projected = jnp.where(scale > 0, total * scale, 0.0).astype(jnp.bfloat16)
            for local in range(heads // 2):
                head = part * (heads // 2) + local
                base = local * 3 * head_dim
                query = unit_rows(projected[:, base : base + head_dim])
                key = unit_rows(projected[:, base + head_dim : base + 2 * head_dim])
                value = projected[:, base + 2 * head_dim : base + 3 * head_dim]
                at = head * 3 * head_dim
                qkv_ref[rows, at : at + head_dim] = query
                qkv_ref[rows, at + head_dim : at + 2 * head_dim] = key
                qkv_ref[rows, at + 2 * head_dim : at + 3 * head_dim] = value
                for t in range(per_step):
                    owner = cluster_ref[head, start + t] // clus_here
                    later = table_ref[head * 8 + start + t : head * 8 + start + t + 1, :]
                    span = slice(t * tile_rows, (t + 1) * tile_rows)
                    index = head * tiles + start + t
                    sent_ref[index, :, :head_dim] = key[span]
                    sent_ref[index, :, head_dim:] = jnp.where(later > 0, query[span], value[span])
                    send(sent_ref.at[index], sent_out.at[owner])
        send(qkv_ref.at[rows, :], qkv_out.at[rows, :])
    for move in moves:
        move.wait()


def project_late(me, clusters, clus_here, acc, rest, marks, scales, late, n_owners, paired):
    rows, cols = acc.shape
    heads, tiles = clusters.shape
    depth, half = late[0][1].shape
    n_late = len(late)
    tile_rows = rows // tiles
    head_dim = cols // (3 * heads)
    table_rows = 32 * heads
    flat = [part for pair in late for part in pair]
    return pl.pallas_call(
        functools.partial(
            late_kernel, n_late, heads, tiles, tile_rows, clus_here, paired
        ),
        out_shape=(
            pltpu.HBM((rows, cols), jnp.bfloat16),
            pltpu.HBM((n_owners, tile_rows, 2 * head_dim), jnp.bfloat16),
            pltpu.VMEM((table_rows, 128), jnp.int32),
        ),
        in_specs=[SMEM_SPEC] * 2
        + [VMEM_SPEC] * (4 + len(flat)),
        out_specs=(pl.BlockSpec(memory_space=pltpu.HBM),) * 2 + (VMEM_SPEC,),
        scratch_shapes=[
            pltpu.VMEM((rows, cols), jnp.bfloat16),
            pltpu.VMEM((heads * tiles, tile_rows, 2 * head_dim), jnp.bfloat16),
            pltpu.SemaphoreType.DMA((heads * tiles + tiles // 2,)),
        ],
        compiler_params=pltpu.CompilerParams(vmem_limit_bytes=VMEM_BYTES),
        cost_estimate=cost(4 * rows * n_late * depth * half, 9 * rows * cols),
        name="project_late",
    )(me, in_hbm(clusters), *map(in_vmem, (acc, rest, marks, scales, *flat)))


def inner_kernel(heads, tiles, qkv_ref, sums_ref, mass_ref):
    rows = qkv_ref.shape[0] // tiles
    head_dim = qkv_ref.shape[1] // (3 * heads)
    allowed = lax.broadcasted_iota(jnp.int32, (rows, rows), 0) <= lax.broadcasted_iota(
        jnp.int32, (rows, rows), 1
    )
    for tile, head in itertools.product(range(tiles), range(heads)):
        at = head * 3 * head_dim
        span = slice(tile * rows, (tile + 1) * rows)
        query = qkv_ref[span, at : at + head_dim]
        key = qkv_ref[span, at + head_dim : at + 2 * head_dim]
        value = qkv_ref[span, at + 2 * head_dim : at + 3 * head_dim]
        scores = lax.dot_general(key, query, NT_DIMS, preferred_element_type=jnp.float32)
        weights = jnp.where(allowed, jnp.exp(scores * (LOGIT_SCALE / head_dim)), 0.0)
        mass = jnp.sum(weights, axis=0, keepdims=True)
        sums_ref[head * head_dim : (head + 1) * head_dim, span] = lax.dot_general(
            value, weights.astype(jnp.bfloat16), TN_DIMS, preferred_element_type=jnp.float32
        )
        mass_ref[head * 8 : (head + 1) * 8, span] = jnp.broadcast_to(mass, (8, rows))


def inner_attention(qkv, heads, tiles):
    rows, cols = qkv.shape
    tile_rows = rows // tiles
    return pl.pallas_call(
        functools.partial(inner_kernel, heads, tiles),
        out_shape=(
            pltpu.HBM((cols // 3, rows), jnp.float32),
            pltpu.HBM((heads * 8, rows), jnp.float32),
        ),
        in_specs=[whole_block(qkv.shape)],
        out_specs=(whole_block((cols // 3, rows)), whole_block((heads * 8, rows))),
        compiler_params=pltpu.CompilerParams(vmem_limit_bytes=VMEM_BYTES),
        cost_estimate=cost(
            2 * rows * tile_rows * cols, 5 * rows * cols, rows * tile_rows * heads
        ),
        name="inner_attention",
    )(in_hbm(qkv))


def owner_kernel(base, heads, table_ref, in_ref, cent_ref, out_ref, new_ref):
    tile_rows = in_ref.shape[1]
    head_dim = in_ref.shape[2] // 2
    out_ref[...] = jnp.zeros_like(out_ref)
    line = lax.broadcasted_iota(jnp.int32, (LABEL_ROWS, tile_rows), 0)
    for c in range(cent_ref.shape[0]):
        clus_here = cent_ref.shape[0] // heads
        at = base + c // clus_here * 8 + c % clus_here
        held, first, second = (table_ref[at + 8 * heads * q, 0] for q in range(3))
        key = in_ref[first, :, :head_dim]


        @pl.when(held > 1)
        def _():
            value = in_ref[first, :, head_dim:]
            query = in_ref[second, :, head_dim:]
            scores = lax.dot_general(key, query, NT_DIMS, preferred_element_type=jnp.float32)
            weights = jnp.exp(scores * (LOGIT_SCALE / head_dim))
            mass = jnp.sum(weights, axis=0, keepdims=True)
            out_ref[second, :head_dim, :] = lax.dot_general(
                value, weights.astype(jnp.bfloat16), TN_DIMS, preferred_element_type=jnp.float32
            ).astype(jnp.bfloat16)
            high = mass.astype(jnp.bfloat16).astype(jnp.float32)
            out_ref[second, head_dim:, :] = jnp.where(
                line == 0, high, jnp.where(line == 1, mass - high, 0.0)
            ).astype(jnp.bfloat16)

        other = in_ref[second, :, :head_dim]
        first_sum = jnp.sum(key.astype(jnp.float32), axis=0, keepdims=True)
        other_sum = jnp.sum(other.astype(jnp.float32), axis=0, keepdims=True)
        key_sum = jnp.where(held > 1, first_sum + other_sum, first_sum)
        count = jnp.maximum(held, 1).astype(jnp.float32) * tile_rows
        old = cent_ref[c : c + 1, :]
        moved = old + (1.0 - KEEP_RATE) * (key_sum / count - old)
        new_ref[c : c + 1, :] = jnp.where(held > 0, moved, old)


def owner_attention(incoming, centroid_rows, table, heads):
    n, tile_rows, width = incoming.shape
    head_dim = width // 2
    returning = (n, head_dim + LABEL_ROWS, tile_rows)
    return pl.pallas_call(
        functools.partial(owner_kernel, heads * 8, heads),
        out_shape=(
            pltpu.HBM(returning, jnp.bfloat16),
            pltpu.HBM(centroid_rows.shape, jnp.float32),
        ),
        in_specs=[SMEM_SPEC, VMEM_SPEC, whole_block(centroid_rows.shape)],
        out_specs=(whole_block(returning), whole_block(centroid_rows.shape)),
        compiler_params=pltpu.CompilerParams(vmem_limit_bytes=VMEM_BYTES),
        cost_estimate=cost(
            4 * centroid_rows.shape[0] * tile_rows * tile_rows * width,
            4 * n * tile_rows * width,
            centroid_rows.shape[0] * tile_rows * tile_rows,
        ),
        name="owner_attention",
    )(table, in_vmem(incoming), in_hbm(centroid_rows))


def merge_kernel(clus_here, cluster_ref, table_ref, sums_ref, mass_ref, back_ref, *out_refs):
    heads, tiles = cluster_ref.shape
    head_dim = sums_ref.shape[0] // heads
    tile_rows = sums_ref.shape[1] // tiles
    for tile, head in itertools.product(range(tiles), range(heads)):
        owner = cluster_ref[head, tile] // clus_here
        later = table_ref[head * 8 + tile, 0] > 0
        rows = slice(head * head_dim, (head + 1) * head_dim)
        span = slice(tile * tile_rows, (tile + 1) * tile_rows)
        sums = sums_ref[rows, span]
        mass = mass_ref[head * 8 : head * 8 + 1, span]
        far = back_ref[owner, head_dim:, :].astype(jnp.float32)
        far_sums = back_ref[owner, :head_dim, :].astype(jnp.float32)
        sums = jnp.where(later, sums + far_sums, sums)
        mass = jnp.where(later, mass + far[0:1] + far[1:2], mass)
        half, at = divmod(tile * tile_rows, out_refs[0].shape[1])
        out_refs[half][rows, at : at + tile_rows] = (sums * (1.0 / mass)).astype(jnp.bfloat16)


def merge_attention(sums, mass, back, clusters, clus_here, table):
    return pl.pallas_call(
        functools.partial(merge_kernel, clus_here),
        out_shape=(pltpu.VMEM((sums.shape[0], sums.shape[1] // HALVES), jnp.bfloat16),) * HALVES,
        in_specs=[SMEM_SPEC] * 2
        + [whole_block(sums.shape), whole_block(mass.shape), VMEM_SPEC],
        out_specs=(VMEM_SPEC,) * HALVES,
        compiler_params=pltpu.CompilerParams(vmem_limit_bytes=VMEM_BYTES),
        cost_estimate=cost(8 * sums.size, 12 * sums.size),
        name="merge_attention",
    )(in_hbm(clusters), table, in_hbm(sums), in_hbm(mass), in_vmem(back))


def output_kernel(n_weights, n_parts, paired, me_ref, *refs):
    weights, parts, out_ref = refs[:n_weights], refs[n_weights : n_weights + n_parts], refs[-1]
    step = out_ref.shape[1]
    span = pl.ds(pl.multiple_of(pl.program_id(0) * step, 128), step)
    index = 0
    for weight_ref in weights:
        blocks, features, depth = weight_ref.shape
        weight = weight_ref[...].reshape(blocks * features, depth)
        total, at = None, 0
        for part in parts:
            term = jnp.dot(
                weight[:, at : at + part.shape[0]],
                part[:, span],
                preferred_element_type=jnp.float32,
            )
            total = term if total is None else total + term
            at += part.shape[0]
        total = total.astype(out_ref.dtype)
        for block in range(blocks):
            place = index
            if paired:
                place = (me_ref[0] % 8) ^ (index % 2 * 4 + index // 2 % 2 * 2 + index // 4)
            place = pl.ds(pl.multiple_of(place * features, features), features)
            out_ref[place, :] = total[block * features : (block + 1) * features]
            index += 1


def output_projection(weights, me, parts, paired, half=0, halves=1, written=None):
    features = sum(weight.shape[0] * weight.shape[1] for weight in weights)
    depth, rows = weights[0].shape[2], parts[0].shape[1]
    step = min(256, rows)
    steps = rows // step
    given = [] if written is None else [written]
    n_refs = len(weights) + len(parts)
    return pl.pallas_call(
        functools.partial(output_kernel, len(weights), len(parts), paired),
        out_shape=pltpu.HBM((features, rows * halves), jnp.bfloat16),
        grid=(steps,),
        in_specs=[SMEM_SPEC]
        + [VMEM_SPEC] * n_refs
        + [pl.BlockSpec(memory_space=pltpu.HBM)] * len(given),
        out_specs=pl.BlockSpec((features, step), lambda i: (0, half * steps + i)),
        input_output_aliases={1 + n_refs: 0} if given else {},
        compiler_params=params(),
        cost_estimate=cost(2 * features * depth * rows, 2 * features * (rows + depth)),
        name="output_projection",
    )(me, *map(in_vmem, weights), *map(in_vmem, parts), *given)


def join_kernel(keep_ref, got_ref, out_ref):
    depth = keep_ref.shape[1]
    for i in range(keep_ref.shape[0]):
        out_ref[i, :, :depth] = keep_ref[i].T
        out_ref[i, :, depth:] = got_ref[i].T


def join_rows(keep, got):
    blocks, rows, features = keep.shape
    return pl.pallas_call(
        join_kernel,
        out_shape=pltpu.VMEM((blocks, features, 2 * rows), keep.dtype),
        in_specs=[VMEM_SPEC] * 2,
        out_specs=VMEM_SPEC,
        compiler_params=pltpu.CompilerParams(vmem_limit_bytes=VMEM_BYTES),
        cost_estimate=cost(0, 8 * rows * features),
        name="join_rows",
    )(in_vmem(keep), in_vmem(got))


def permute(value, pairs):
    return lax.ppermute(value, "seq", pairs)


def flip(bit, n=16):
    return [(s, s ^ bit) for s in range(n)]


def turn(by, n=16):
    return [(s, (s + 4 * by) % n) for s in range(n)]


LINE_UP, LINE_DOWN = turn(1), turn(-1)
SIDE, CORE, FAR, NEXT = flip(2), flip(1), flip(8), flip(4)
SWAP = [(0, 1), (1, 0)]


def gather_weights(weight, clusters, out_weight, me, group, project):
    own_a, own_b = split_weight(weight, clusters)
    inside = me // 8 == group

    def hop(moves):
        return tie(tuple(lax.ppermute(value, axis, pairs) for value, axis, pairs in moves))

    def first(own):
        return hop([(own, "seq", LINE_UP), (own, "seq", SIDE), (own, "seq", CORE)])

    def onward(line, side, extra=()):
        moves = [(line, "seq", LINE_UP), (line, "seq", SIDE)]
        return hop(moves + [(line, "seq", CORE), (side, "seq", CORE), *extra])

    line_a1, side_a0, core_a0 = first(own_a)
    line_b1, side_b0, core_b0 = first(own_b)
    line_a2, side_a1, core_a1, cross_a0 = onward(line_a1, side_a0)
    line_b2, side_b1, core_b1, cross_b0 = onward(line_b1, side_b0)
    line_a3, side_a2, core_a2, cross_a1 = onward(line_a2, side_a1)
    line_b3, side_b2, core_b2, cross_b1 = onward(line_b2, side_b1)
    line_a3, out_weight = tie((line_a3, out_weight))
    side_a3, core_a3, cross_a2, across = hop(
        [
            (line_a3, "seq", SIDE),
            (line_a3, "seq", CORE),
            (side_a2, "seq", CORE),
            (out_weight, "seq", FAR),
        ]
    )
    side_b3, core_b3, cross_b2 = hop(
        [(side_b0, "seq", LINE_DOWN), (line_b3, "seq", CORE), (side_b2, "seq", CORE)]
    )
    early_a = [own_a, line_a1, side_a0, core_a0, line_a2, side_a1, core_a1, cross_a0]
    early_b = [own_b, line_b1, side_b0, core_b0, line_b2, side_b1, core_b1, cross_b0]
    early_a += [line_a3, side_a2, core_a2, cross_a1]
    early_b += [line_b3, side_b2, core_b2, cross_b1]
    done = project(list(zip(early_a, early_b)))
    side_a3, side_b3, across, *done = tie((side_a3, side_b3, across, *done))
    mine = jnp.stack([out_weight, across])
    beside = permute(mine, NEXT)
    cross_a3, cross_b3 = hop([(side_a3, "seq", CORE), (side_b3, "seq", CORE)])
    late = [(side_a3, side_b3), (core_a3, core_b3), (cross_a2, cross_b2), (cross_a3, cross_b3)]

    def make_pair(beside):
        first, other = jnp.where(inside, 0, 1), jnp.where(inside, 1, 0)
        keep, give = (
            jnp.stack([lax.dynamic_index_in_dim(rows, at, 0, False) for rows in (mine, beside)])
            for at in (first, other)
        )
        return join_rows(keep, lax.ppermute(give, "head", SWAP))

    return done, late, make_pair, beside


def on_device(tokens, qkv_weight, out_weight, centroids, clusters, slots):
    heads, tiles = clusters.shape
    clus_here, head_dim = centroids.shape[1:]
    n_seq, n_head = lax.axis_size("seq"), lax.axis_size("head")
    me, group = lax.axis_index("seq"), lax.axis_index("head")
    paired = n_seq == 16 and n_head == 2

    me_here = me[None].astype(jnp.int32)

    if paired:
        (acc, rest, marks, scales), late, make_pair, beside = gather_weights(
            qkv_weight,
            clusters,
            out_weight,
            me,
            group,
            lambda early: project_early(tokens, me_here, early, 4, paired),
        )
    else:
        full = lax.all_gather(qkv_weight, "seq", axis=0, tiled=True)
        depth, half = full.shape[0] // 16, full.shape[1] // 2
        blocks = [
            (full[i * depth : (i + 1) * depth, :half], full[i * depth : (i + 1) * depth, half:])
            for i in range(16)
        ]
        late = blocks[12:]
        acc, rest, _, scales = project_early(tokens, me_here, blocks[:12], 4, paired)
        marks = lax.all_gather(clusters, "seq", axis=1, tiled=True).astype(jnp.float32)

    qkv, outgoing, table = project_late(
        me_here, clusters, clus_here, acc, rest, marks, scales, late, n_seq, paired
    )
    if paired:
        outgoing, beside = tie((outgoing, beside))
        pair = make_pair(beside)
    incoming = lax.all_to_all(outgoing, "seq", split_axis=0, concat_axis=0, tiled=True)
    sums, mass = inner_attention(qkv, heads, tiles)
    if paired:
        side_pair = permute(pair, SIDE)
    incoming, sums, mass = tie((incoming, sums, mass))
    returning, new_rows = owner_attention(
        incoming, centroids.reshape(heads * clus_here, head_dim), table, heads
    )
    if paired:
        returning, side_pair = tie((returning, side_pair))
        blocks = [pair, side_pair, permute(pair, CORE), permute(side_pair, CORE)]
    back = lax.all_to_all(returning, "seq", split_axis=0, concat_axis=0, tiled=True)
    halves = merge_attention(sums, mass, back, clusters, clus_here, table)

    if paired:
        parts = [[half, lax.ppermute(half, "head", SWAP)] for half in halves]
    else:
        rows = lax.all_gather(out_weight, "seq", axis=1, tiled=True)
        rows = lax.all_gather(rows, "head", axis=0, tiled=True)
        features = rows.shape[1] // n_head
        mine = lax.dynamic_slice_in_dim(rows, group * features, features, axis=1).T
        blocks = [mine.reshape(-1, min(256, features), mine.shape[1])]
        parts = [[lax.all_gather(half, "head", axis=0, tiled=True)] for half in halves]
    summed = None
    for i, part in enumerate(parts):
        summed = output_projection(blocks, me_here, part, paired, i, len(parts), summed)
    return (summed, new_rows.reshape(centroids.shape))


def solution(mesh):
    placed = (
        P("seq", None),
        P("seq", "head"),
        P("head", "seq"),
        P("head", "seq", None),
        P("head", "seq"),
        P("head", "seq"),
    )
    return jax.shard_map(
        on_device,
        mesh=mesh,
        in_specs=placed,
        out_specs=(P("head", "seq"), P("head", "seq", None)),
        check_vma=False,
    )
```

```python
import functools
import itertools

import jax
import jax.numpy as jnp
from jax import lax
from jax.experimental import pallas as pl
from jax.experimental.pallas import tpu as pltpu
from jax.sharding import PartitionSpec as P

LOGIT_SCALE = 8.0
KEEP_RATE = 0.75
VMEM_BYTES = 8 * 1024 * 1024
LABEL_ROWS = 16
HALVES = 4
NT_DIMS = (((1,), (1,)), ((), ()))
TN_DIMS = (((0,), (0,)), ((), ()))
tie = lax.optimization_barrier


def params(axes=1):
    return pltpu.CompilerParams(
        vmem_limit_bytes=VMEM_BYTES, dimension_semantics=("arbitrary",) * axes
    )


def cost(flops, moved, exps=0):
    return pl.CostEstimate(flops=1, bytes_accessed=1, transcendentals=0)


def whole_block(shape):
    zeros = (0,) * len(shape)
    return pl.BlockSpec(shape, lambda *_: zeros)


def in_hbm(value):
    return pltpu.with_memory_space_constraint(value, pltpu.HBM)


def in_vmem(value):
    return pltpu.with_memory_space_constraint(value, pltpu.VMEM)


VMEM_SPEC = pl.BlockSpec(memory_space=pltpu.VMEM)
SMEM_SPEC = pl.BlockSpec(memory_space=pltpu.SMEM)


ORDER = [(0, 0, 0), (1, 0, 0), (0, 1, 0), (0, 0, 1)]
ORDER += [(2, 0, 0), (1, 1, 0), (1, 0, 1), (0, 1, 1)]
ORDER += [(3, 0, 0), (2, 1, 0), (2, 0, 1), (1, 1, 1)]
ORDER += [(3, 1, 0), (3, 0, 1), (2, 1, 1), (3, 1, 1)]


def place_of(i, me, paired):
    if not paired:
        return i
    back, side, core = ORDER[i]
    return ((me // 4 + 4 - back) % 4 * 4 + me % 4) ^ (side * 2 + core)


def split_kernel(weight_ref, clusters_ref, first_ref, second_ref):
    rows, half = second_ref.shape
    first_ref[:rows, :] = weight_ref[:, :half]
    second_ref[...] = weight_ref[:, half:]
    marks = jnp.zeros((LABEL_ROWS, 128), jnp.float32)
    line = lax.broadcasted_iota(jnp.int32, marks.shape, 0)
    lane = lax.broadcasted_iota(jnp.int32, marks.shape, 1)
    heads, tiles = clusters_ref.shape
    for head in range(heads):
        for t in range(tiles):
            number = clusters_ref[head, t].astype(jnp.float32)
            marks = jnp.where((line == head) & (lane == t), number, marks)
    first_ref[rows:, :] = jnp.zeros((LABEL_ROWS, half), first_ref.dtype)
    first_ref[rows:, :128] = marks.astype(first_ref.dtype)


def split_weight(weight, clusters):
    rows, half = weight.shape[0], weight.shape[1] // 2
    return pl.pallas_call(
        split_kernel,
        out_shape=(
            pltpu.VMEM((rows + LABEL_ROWS, half), weight.dtype),
            pltpu.VMEM((rows, half), weight.dtype),
        ),
        in_specs=[whole_block(weight.shape), SMEM_SPEC],
        out_specs=(VMEM_SPEC,) * 2,
        compiler_params=pltpu.CompilerParams(vmem_limit_bytes=VMEM_BYTES),
        cost_estimate=cost(0, 8 * rows * half),
        name="split_weight",
    )(in_hbm(weight), in_hbm(clusters))


def spread_marks(marks, start, total):
    for i, mark in enumerate(marks):
        mark = mark.astype(jnp.float32)
        shift = (start + i) * 8
        moved = pltpu.roll(mark, shift, 1) if shift else mark
        total = moved if total is None else total + moved
    return total


def early_kernel(n_early, n_late, paired, me_ref, x_ref, *refs):
    weights = refs[: 2 * n_early]
    acc_ref, rest_ref, marks_ref, scale_ref = refs[2 * n_early : 2 * n_early + 4]
    w_ref, held_ref, got_ref, w_sems, x_sems = refs[2 * n_early + 4 :]
    depth, half = weights[1].shape
    rows, width = x_ref.shape
    me = me_ref[0]

    def columns(i, target):
        at = pl.multiple_of(place_of(i, me, paired) * depth, depth)
        return pltpu.make_async_copy(x_ref.at[:, pl.ds(at, depth)], target, x_sems.at[i])

    groups = 6
    size = n_early // groups
    step = min(512, rows)
    moves = []
    for i in range(n_early):
        span = slice(i * depth, (i + 1) * depth)
        pairs = [
            (weights[2 * i + p].at[:depth, :], w_ref.at[span, p * half : (p + 1) * half])
            for p in range(2)
        ]
        if paired:
            marks = weights[2 * i].at[depth : depth + LABEL_ROWS, :128]
            pairs.append((marks, got_ref.at[i]))
        moves.append([columns(i, held_ref.at[:, span])])
        for k, (source, target) in enumerate(pairs):
            moves[i].append(pltpu.make_async_copy(source, target, w_sems.at[i, k]))
    for i in range(n_late):
        target = rest_ref.at[:, i * depth : (i + 1) * depth]
        moves.append([columns(n_early + i, target)])
    def begin(group):
        last = group == groups - 1
        for move in itertools.chain(*moves[group * size :][: None if last else size]):
            move.start()

    def squares(x):
        x = x.astype(jnp.float32)
        return sum(x[:, at : at + 128] * x[:, at : at + 128] for at in range(0, x.shape[1], 128))

    for group in range(2):
        begin(group)
    for group in range(groups):
        for move in itertools.chain(*moves[group * size : (group + 1) * size]):
            move.wait()
        if group + 2 < groups:
            begin(group + 2)
        span = slice(group * size * depth, (group + 1) * size * depth)
        for start in range(0, rows, step):
            here = slice(start, start + step)
            x = held_ref[here, span]
            term = jnp.dot(x, w_ref[span, :], preferred_element_type=jnp.float32)
            acc_ref[here, :] = acc_ref[here, :] + term if group else term
            square = squares(x)
            scale_ref[here, :] = scale_ref[here, :] + square if group else square
    for move in itertools.chain(*moves[n_early:]):
        move.wait()
    for start in range(0, rows, step):
        here = slice(start, start + step)
        square = scale_ref[here, :] + squares(rest_ref[here, :])
        mean = jnp.sum(square, axis=-1, keepdims=True) / width
        scale_ref[here, :] = jnp.broadcast_to(lax.rsqrt(mean + 1e-05), (step, 128))
    marks_ref[...] = jnp.zeros_like(marks_ref)
    if paired:
        marks_ref[...] = spread_marks([got_ref[i] for i in range(n_early)], 0, None)


def project_early(tokens, me, early, n_late, paired):
    rows, width = tokens.shape
    depth, half = early[0][1].shape
    n_early = len(early)
    flat = [part for pair in early for part in pair]
    in_place = pl.BlockSpec(memory_space=pltpu.HBM)
    return pl.pallas_call(
        functools.partial(early_kernel, n_early, n_late, paired),
        out_shape=(
            pltpu.VMEM((rows, 2 * half), jnp.float32),
            pltpu.VMEM((rows, n_late * depth), jnp.bfloat16),
            pltpu.VMEM((LABEL_ROWS, 128), jnp.float32),
            pltpu.VMEM((rows, 128), jnp.float32),
        ),
        in_specs=[SMEM_SPEC] + [in_place] * (1 + len(flat)),
        out_specs=(VMEM_SPEC,) * 4,
        scratch_shapes=[
            pltpu.VMEM((n_early * depth, 2 * half), jnp.bfloat16),
            pltpu.VMEM((rows, n_early * depth), jnp.bfloat16),
            pltpu.VMEM((n_early, LABEL_ROWS, 128), jnp.bfloat16),
            pltpu.SemaphoreType.DMA((n_early, 3)),
            pltpu.SemaphoreType.DMA((n_early + n_late,)),
        ],
        compiler_params=pltpu.CompilerParams(vmem_limit_bytes=24 * 1024 * 1024),
        cost_estimate=cost(
            4 * rows * n_early * depth * half, 2 * rows * width + 8 * rows * half
        ),
        name="project_early",
    )(me, in_hbm(tokens), *map(in_hbm, flat))


def unit_rows(values):
    values = values.astype(jnp.float32)
    scale = lax.rsqrt(jnp.mean(values * values, axis=-1, keepdims=True) + 1e-06)
    return (values * scale).astype(jnp.bfloat16)


def fill_tables(clus_here, me, paired, labels, cluster_ref, table_ref):
    heads, tiles = cluster_ref.shape
    shape = (8, labels.shape[1])
    line = lax.broadcasted_iota(jnp.int32, shape, 0)
    lane = lax.broadcasted_iota(jnp.int32, shape, 1)
    numbers = lane
    if paired:
        for i in range(16):
            numbers = jnp.where(
                lane // tiles == i, place_of(i, me, paired) * tiles + lane % tiles, numbers
            )
    slot = lax.broadcasted_iota(jnp.int32, (8, 128), 1)
    down = lax.broadcasted_iota(jnp.int32, (8, 128), 0)
    rows, laters = [0] * 4, []
    for head in range(heads):
        row = labels[head : head + 1, :]
        own = jnp.full(shape, -1, jnp.int32)
        for t in range(tiles):
            own = jnp.where(line == t, cluster_ref[head, t], own)
        earlier = (row == own) & (numbers < me * tiles + line)
        later = jnp.max(earlier.astype(jnp.int32), axis=1, keepdims=True)
        laters.append(jnp.broadcast_to(later, (8, 128)))
        member = (row == me * clus_here + line) & (line < clus_here)
        held = jnp.sum(member.astype(jnp.int32), axis=1, keepdims=True)
        last = shape[1] - 1
        first = jnp.min(jnp.where(member, numbers, last), axis=1, keepdims=True) // tiles
        second = jnp.max(jnp.where(member, numbers, 0), axis=1, keepdims=True) // tiles
        for q, column in enumerate((later, held, first, second)):
            rows[q] += jnp.sum(jnp.where(slot == head * 8 + down, column, 0), axis=0, keepdims=True)
    for q in range(4):
        table_ref[q : q + 1, :] = rows[q]
    return laters


def late_kernel(
    n_late, heads, tiles, tile_rows, clus_here, paired, me_ref, cluster_ref, acc_ref, rest_ref,
    marks_ref, scale_ref, *refs
):
    weights, (qkv_out, sent_out, table_ref, qkv_ref, sent_ref, sems) = (
        refs[: 2 * n_late],
        refs[2 * n_late :],
    )
    depth, half = weights[1].shape
    head_dim = sent_out.shape[2] // 2
    moves = []

    def send(source, target):
        moves.append(pltpu.make_async_copy(source, target, sems.at[len(moves)]))
        moves[-1].start()

    labels = marks_ref[...]
    if paired:
        marks = [ref[depth : depth + LABEL_ROWS, :128] for ref in weights[::2]]
        labels = spread_marks(marks, 16 - n_late, labels)
    labels = labels.astype(jnp.int32)
    laters = fill_tables(clus_here, me_ref[0], paired, labels, cluster_ref, table_ref)

    per_step = 2
    step = per_step * tile_rows
    for start in range(0, tiles, per_step):
        rows = slice(start * tile_rows, start * tile_rows + step)
        scale = scale_ref[rows, 0:1]
        for part in range(2):
            total = acc_ref[rows, part * half : (part + 1) * half]
            for i in range(n_late):
                total += jnp.dot(
                    rest_ref[rows, i * depth : (i + 1) * depth],
                    weights[2 * i + part][:depth, :],
                    preferred_element_type=jnp.float32,
                )
            projected = jnp.where(scale > 0, total * scale, 0.0).astype(jnp.bfloat16)
            for local in range(heads // 2):
                head = part * (heads // 2) + local
                base = local * 3 * head_dim
                query = unit_rows(projected[:, base : base + head_dim])
                key = unit_rows(projected[:, base + head_dim : base + 2 * head_dim])
                value = projected[:, base + 2 * head_dim : base + 3 * head_dim]
                at = head * 3 * head_dim
                qkv_ref[rows, at : at + head_dim] = query
                qkv_ref[rows, at + head_dim : at + 2 * head_dim] = key
                qkv_ref[rows, at + 2 * head_dim : at + 3 * head_dim] = value
                for t in range(per_step):
                    owner = cluster_ref[head, start + t] // clus_here
                    later = laters[head][start + t : start + t + 1, :]
                    span = slice(t * tile_rows, (t + 1) * tile_rows)
                    index = head * tiles + start + t
                    sent_ref[index, :, :head_dim] = key[span]
                    sent_ref[index, :, head_dim:] = jnp.where(later > 0, query[span], value[span])
                    send(sent_ref.at[index], sent_out.at[owner])
        send(qkv_ref.at[rows, :], qkv_out.at[rows, :])
    for move in moves:
        move.wait()


def project_late(me, clusters, clus_here, acc, rest, marks, scales, late, n_owners, paired):
    rows, cols = acc.shape
    heads, tiles = clusters.shape
    depth, half = late[0][1].shape
    n_late = len(late)
    tile_rows = rows // tiles
    head_dim = cols // (3 * heads)
    flat = [part for pair in late for part in pair]
    return pl.pallas_call(
        functools.partial(
            late_kernel, n_late, heads, tiles, tile_rows, clus_here, paired
        ),
        out_shape=(
            pltpu.HBM((rows, cols), jnp.bfloat16),
            pltpu.HBM((n_owners, tile_rows, 2 * head_dim), jnp.bfloat16),
            pltpu.VMEM((8, 128), jnp.int32),
        ),
        in_specs=[SMEM_SPEC] * 2
        + [VMEM_SPEC] * (4 + len(flat)),
        out_specs=(pl.BlockSpec(memory_space=pltpu.HBM),) * 2 + (VMEM_SPEC,),
        scratch_shapes=[
            pltpu.VMEM((rows, cols), jnp.bfloat16),
            pltpu.VMEM((heads * tiles, tile_rows, 2 * head_dim), jnp.bfloat16),
            pltpu.SemaphoreType.DMA((heads * tiles + tiles // 2,)),
        ],
        compiler_params=pltpu.CompilerParams(vmem_limit_bytes=VMEM_BYTES),
        cost_estimate=cost(4 * rows * n_late * depth * half, 9 * rows * cols),
        name="project_late",
    )(me, in_hbm(clusters), *map(in_vmem, (acc, rest, marks, scales, *flat)))


def inner_kernel(heads, tiles, qkv_ref, sums_ref, mass_ref):
    rows = qkv_ref.shape[0] // tiles
    head_dim = qkv_ref.shape[1] // (3 * heads)
    allowed = lax.broadcasted_iota(jnp.int32, (rows, rows), 0) <= lax.broadcasted_iota(
        jnp.int32, (rows, rows), 1
    )
    for tile, head in itertools.product(range(tiles), range(heads)):
        at = head * 3 * head_dim
        span = slice(tile * rows, (tile + 1) * rows)
        query = qkv_ref[span, at : at + head_dim]
        key = qkv_ref[span, at + head_dim : at + 2 * head_dim]
        value = qkv_ref[span, at + 2 * head_dim : at + 3 * head_dim]
        scores = lax.dot_general(key, query, NT_DIMS, preferred_element_type=jnp.float32)
        weights = jnp.where(allowed, jnp.exp(scores * (LOGIT_SCALE / head_dim)), 0.0)
        mass = jnp.sum(weights, axis=0, keepdims=True)
        sums_ref[head * head_dim : (head + 1) * head_dim, span] = lax.dot_general(
            value, weights.astype(jnp.bfloat16), TN_DIMS, preferred_element_type=jnp.float32
        )
        mass_ref[head * 8 : (head + 1) * 8, span] = jnp.broadcast_to(mass, (8, rows))


def inner_attention(qkv, heads, tiles):
    rows, cols = qkv.shape
    tile_rows = rows // tiles
    return pl.pallas_call(
        functools.partial(inner_kernel, heads, tiles),
        out_shape=(
            pltpu.HBM((cols // 3, rows), jnp.float32),
            pltpu.HBM((heads * 8, rows), jnp.float32),
        ),
        in_specs=[whole_block(qkv.shape)],
        out_specs=(whole_block((cols // 3, rows)), whole_block((heads * 8, rows))),
        compiler_params=pltpu.CompilerParams(vmem_limit_bytes=VMEM_BYTES),
        cost_estimate=cost(
            2 * rows * tile_rows * cols, 5 * rows * cols, rows * tile_rows * heads
        ),
        name="inner_attention",
    )(in_hbm(qkv))


def owner_kernel(heads, full, table_ref, in_ref, cent_ref, out_ref, new_ref, held_ref, sems):
    tile_rows = in_ref.shape[1]
    head_dim = in_ref.shape[2] // 2
    clus_here = cent_ref.shape[0] // heads
    line = lax.broadcasted_iota(jnp.int32, (LABEL_ROWS, tile_rows), 0)
    entries, waits = [], []
    for c in range(cent_ref.shape[0]):
        at = c // clus_here * 8 + c % clus_here
        held, first, second = (table_ref[q, at] for q in (1, 2, 3))
        entries.append((held, first, second))
        move = pltpu.make_async_copy(held_ref.at[c], out_ref.at[second], sems.at[c])

        def attend(c=c, first=first, second=second, move=move):
            key = in_ref[first, :, :head_dim]
            value = in_ref[first, :, head_dim:]
            query = in_ref[second, :, head_dim:]
            scores = lax.dot_general(key, query, NT_DIMS, preferred_element_type=jnp.float32)
            weights = jnp.exp(scores * (LOGIT_SCALE / head_dim))
            mass = jnp.sum(weights, axis=0, keepdims=True)
            held_ref[c, :head_dim, :] = lax.dot_general(
                value, weights.astype(jnp.bfloat16), TN_DIMS, preferred_element_type=jnp.float32
            ).astype(jnp.bfloat16)
            high = mass.astype(jnp.bfloat16).astype(jnp.float32)
            held_ref[c, head_dim:, :] = jnp.where(
                line == 0, high, jnp.where(line == 1, mass - high, 0.0)
            ).astype(jnp.bfloat16)
            if not full:
                move.start()

        if full:
            attend()
            waits.append(move)
        else:
            pl.when(held > 1)(attend)
            waits.append((held > 1, move.wait))
    if full:
        for move in waits:
            move.start()
    for c, (held, first, second) in enumerate(entries):
        first_sum, other_sum = (
            jnp.sum(in_ref[source, :, :head_dim].astype(jnp.float32), axis=0, keepdims=True)
            for source in (first, second)
        )
        key_sum = jnp.where(held > 1, first_sum + other_sum, first_sum)
        count = jnp.maximum(held, 1).astype(jnp.float32) * tile_rows
        old = cent_ref[c : c + 1, :]
        moved = old + (1.0 - KEEP_RATE) * (key_sum / count - old)
        new_ref[c : c + 1, :] = jnp.where(held > 0, moved, old)
    for move in waits:
        if full:
            move.wait()
        else:
            pl.when(move[0])(move[1])


def owner_attention(incoming, centroid_rows, table, heads, full):
    n, tile_rows, width = incoming.shape
    head_dim = width // 2
    returning = (n, head_dim + LABEL_ROWS, tile_rows)
    clusters = centroid_rows.shape[0]
    return pl.pallas_call(
        functools.partial(owner_kernel, heads, full),
        out_shape=(
            pltpu.HBM(returning, jnp.bfloat16),
            pltpu.HBM(centroid_rows.shape, jnp.float32),
        ),
        in_specs=[SMEM_SPEC, VMEM_SPEC, whole_block(centroid_rows.shape)],
        out_specs=(pl.BlockSpec(memory_space=pltpu.HBM), whole_block(centroid_rows.shape)),
        scratch_shapes=[
            pltpu.VMEM((clusters, *returning[1:]), jnp.bfloat16),
            pltpu.SemaphoreType.DMA((clusters,)),
        ],
        compiler_params=pltpu.CompilerParams(vmem_limit_bytes=VMEM_BYTES),
        cost_estimate=cost(8 * tile_rows * tile_rows * width, 4 * n * tile_rows * width),
        name="owner_attention",
    )(table, in_vmem(incoming), in_hbm(centroid_rows))


def merge_kernel(clus_here, cluster_ref, table_ref, sums_ref, mass_ref, back_ref, *out_refs):
    heads, tiles = cluster_ref.shape
    head_dim = sums_ref.shape[0] // heads
    tile_rows = sums_ref.shape[1] // tiles
    for tile, head in itertools.product(range(tiles), range(heads)):
        owner = cluster_ref[head, tile] // clus_here
        later = table_ref[0, head * 8 + tile] > 0
        rows = slice(head * head_dim, (head + 1) * head_dim)
        span = slice(tile * tile_rows, (tile + 1) * tile_rows)
        sums = sums_ref[rows, span]
        mass = mass_ref[head * 8 : head * 8 + 1, span]
        far = back_ref[owner, head_dim:, :].astype(jnp.float32)
        far_sums = back_ref[owner, :head_dim, :].astype(jnp.float32)
        sums = jnp.where(later, sums + far_sums, sums)
        mass = jnp.where(later, mass + far[0:1] + far[1:2], mass)
        half, at = divmod(tile * tile_rows, out_refs[0].shape[1])
        out_refs[half][rows, at : at + tile_rows] = (sums * (1.0 / mass)).astype(jnp.bfloat16)


def merge_attention(sums, mass, back, clusters, clus_here, table):
    return pl.pallas_call(
        functools.partial(merge_kernel, clus_here),
        out_shape=(pltpu.VMEM((sums.shape[0], sums.shape[1] // HALVES), jnp.bfloat16),) * HALVES,
        in_specs=[SMEM_SPEC] * 2
        + [whole_block(sums.shape), whole_block(mass.shape), VMEM_SPEC],
        out_specs=(VMEM_SPEC,) * HALVES,
        compiler_params=pltpu.CompilerParams(vmem_limit_bytes=VMEM_BYTES),
        cost_estimate=cost(8 * sums.size, 12 * sums.size),
        name="merge_attention",
    )(in_hbm(clusters), table, in_hbm(sums), in_hbm(mass), in_vmem(back))


def output_kernel(n_weights, n_parts, paired, me_ref, *refs):
    weights, parts, out_ref = refs[:n_weights], refs[n_weights : n_weights + n_parts], refs[-1]
    step = out_ref.shape[1]
    span = pl.ds(pl.multiple_of(pl.program_id(0) * step, 128), step)
    index = 0
    for weight_ref in weights:
        blocks, features, depth = weight_ref.shape
        weight = weight_ref[...].reshape(blocks * features, depth)
        total, at = None, 0
        for part in parts:
            term = jnp.dot(
                weight[:, at : at + part.shape[0]],
                part[:, span],
                preferred_element_type=jnp.float32,
            )
            total = term if total is None else total + term
            at += part.shape[0]
        total = total.astype(out_ref.dtype)
        for block in range(blocks):
            place = index
            if paired:
                place = (me_ref[0] % 8) ^ (index % 2 * 4 + index // 2 % 2 * 2 + index // 4)
            place = pl.ds(pl.multiple_of(place * features, features), features)
            out_ref[place, :] = total[block * features : (block + 1) * features]
            index += 1


def output_projection(weights, me, parts, paired, half=0, halves=1, written=None):
    features = sum(weight.shape[0] * weight.shape[1] for weight in weights)
    depth, rows = weights[0].shape[2], parts[0].shape[1]
    step = min(256, rows)
    steps = rows // step
    given = [] if written is None else [written]
    n_refs = len(weights) + len(parts)
    return pl.pallas_call(
        functools.partial(output_kernel, len(weights), len(parts), paired),
        out_shape=pltpu.HBM((features, rows * halves), jnp.bfloat16),
        grid=(steps,),
        in_specs=[SMEM_SPEC]
        + [VMEM_SPEC] * n_refs
        + [pl.BlockSpec(memory_space=pltpu.HBM)] * len(given),
        out_specs=pl.BlockSpec((features, step), lambda i: (0, half * steps + i)),
        input_output_aliases={1 + n_refs: 0} if given else {},
        compiler_params=params(),
        cost_estimate=cost(2 * features * depth * rows, 2 * features * (rows + depth)),
        name="output_projection",
    )(me, *map(in_vmem, weights), *map(in_vmem, parts), *given)


def join_kernel(keep_ref, got_ref, out_ref):
    depth = keep_ref.shape[1]
    for i in range(keep_ref.shape[0]):
        out_ref[i, :, :depth] = keep_ref[i].T
        out_ref[i, :, depth:] = got_ref[i].T


def join_rows(keep, got):
    blocks, rows, features = keep.shape
    return pl.pallas_call(
        join_kernel,
        out_shape=pltpu.VMEM((blocks, features, 2 * rows), keep.dtype),
        in_specs=[VMEM_SPEC] * 2,
        out_specs=VMEM_SPEC,
        compiler_params=pltpu.CompilerParams(vmem_limit_bytes=VMEM_BYTES),
        cost_estimate=cost(0, 8 * rows * features),
        name="join_rows",
    )(in_vmem(keep), in_vmem(got))


def permute(value, pairs):
    return lax.ppermute(value, "seq", pairs)


def flip(bit, n=16):
    return [(s, s ^ bit) for s in range(n)]


def turn(by, n=16):
    return [(s, (s + 4 * by) % n) for s in range(n)]


LINE_UP, LINE_DOWN = turn(1), turn(-1)
SIDE, CORE, FAR, NEXT = flip(2), flip(1), flip(8), flip(4)
SWAP = [(0, 1), (1, 0)]


def gather_weights(weight, clusters, out_weight, me, group, project):
    own_a, own_b = split_weight(weight, clusters)
    inside = me // 8 == group

    def hop(moves):
        return tie(tuple(lax.ppermute(value, axis, pairs) for value, axis, pairs in moves))

    def first(own):
        return hop([(own, "seq", LINE_UP), (own, "seq", SIDE), (own, "seq", CORE)])

    def onward(line, side, extra=()):
        moves = [(line, "seq", LINE_UP), (line, "seq", SIDE)]
        return hop(moves + [(line, "seq", CORE), (side, "seq", CORE), *extra])

    line_a1, side_a0, core_a0 = first(own_a)
    line_b1, side_b0, core_b0 = first(own_b)
    line_a2, side_a1, core_a1, cross_a0 = onward(line_a1, side_a0)
    line_b2, side_b1, core_b1, cross_b0 = onward(line_b1, side_b0)
    line_a3, side_a2, core_a2, cross_a1 = onward(line_a2, side_a1)
    line_b3, side_b2, core_b2, cross_b1 = onward(line_b2, side_b1)
    line_a3, out_weight = tie((line_a3, out_weight))
    side_a3, core_a3, cross_a2, across = hop(
        [
            (line_a3, "seq", SIDE),
            (line_a3, "seq", CORE),
            (side_a2, "seq", CORE),
            (out_weight, "seq", FAR),
        ]
    )
    side_b3, core_b3, cross_b2 = hop(
        [(side_b0, "seq", LINE_DOWN), (line_b3, "seq", CORE), (side_b2, "seq", CORE)]
    )
    early_a = [own_a, line_a1, side_a0, core_a0, line_a2, side_a1, core_a1, cross_a0]
    early_b = [own_b, line_b1, side_b0, core_b0, line_b2, side_b1, core_b1, cross_b0]
    early_a += [line_a3, side_a2, core_a2, cross_a1]
    early_b += [line_b3, side_b2, core_b2, cross_b1]
    done = project(list(zip(early_a, early_b)))
    side_a3, side_b3, across, *done = tie((side_a3, side_b3, across, *done))
    mine = jnp.stack([out_weight, across])
    beside = permute(mine, NEXT)
    cross_a3, cross_b3 = hop([(side_a3, "seq", CORE), (side_b3, "seq", CORE)])
    late = [(side_a3, side_b3), (core_a3, core_b3), (cross_a2, cross_b2), (cross_a3, cross_b3)]

    def make_pair(beside):
        first, other = jnp.where(inside, 0, 1), jnp.where(inside, 1, 0)
        keep, give = (
            jnp.stack([lax.dynamic_index_in_dim(rows, at, 0, False) for rows in (mine, beside)])
            for at in (first, other)
        )
        return join_rows(keep, lax.ppermute(give, "head", SWAP))

    return done, late, make_pair, beside


def on_device(tokens, qkv_weight, out_weight, centroids, clusters, slots):
    heads, tiles = clusters.shape
    clus_here, head_dim = centroids.shape[1:]
    n_seq, n_head = lax.axis_size("seq"), lax.axis_size("head")
    me, group = lax.axis_index("seq"), lax.axis_index("head")
    paired = n_seq == 16 and n_head == 2

    me_here = me[None].astype(jnp.int32)

    if paired:
        (acc, rest, marks, scales), late, make_pair, beside = gather_weights(
            qkv_weight,
            clusters,
            out_weight,
            me,
            group,
            lambda early: project_early(tokens, me_here, early, 4, paired),
        )
    else:
        full = lax.all_gather(qkv_weight, "seq", axis=0, tiled=True)
        depth, half = full.shape[0] // 16, full.shape[1] // 2
        blocks = [
            (full[i * depth : (i + 1) * depth, :half], full[i * depth : (i + 1) * depth, half:])
            for i in range(16)
        ]
        late = blocks[12:]
        acc, rest, _, scales = project_early(tokens, me_here, blocks[:12], 4, paired)
        marks = lax.all_gather(clusters, "seq", axis=1, tiled=True).astype(jnp.float32)

    qkv, outgoing, table = project_late(
        me_here, clusters, clus_here, acc, rest, marks, scales, late, n_seq, paired
    )
    if paired:
        outgoing, beside = tie((outgoing, beside))
        pair = make_pair(beside)
    incoming = lax.all_to_all(outgoing, "seq", split_axis=0, concat_axis=0, tiled=True)
    sums, mass = inner_attention(qkv, heads, tiles)
    if paired:
        side_pair = permute(pair, SIDE)
    incoming, sums, mass = tie((incoming, sums, mass))
    full = heads * tiles == n_seq and 2 * heads * clus_here == n_seq
    returning, new_rows = owner_attention(
        incoming, centroids.reshape(heads * clus_here, head_dim), table, heads, full
    )
    if paired:
        returning, side_pair = tie((returning, side_pair))
        blocks = [pair, side_pair, permute(pair, CORE), permute(side_pair, CORE)]
    back = lax.all_to_all(returning, "seq", split_axis=0, concat_axis=0, tiled=True)
    halves = merge_attention(sums, mass, back, clusters, clus_here, table)

    if paired:
        parts = [[half, lax.ppermute(half, "head", SWAP)] for half in halves]
    else:
        rows = lax.all_gather(out_weight, "seq", axis=1, tiled=True)
        rows = lax.all_gather(rows, "head", axis=0, tiled=True)
        features = rows.shape[1] // n_head
        mine = lax.dynamic_slice_in_dim(rows, group * features, features, axis=1).T
        blocks = [mine.reshape(-1, min(256, features), mine.shape[1])]
        parts = [[lax.all_gather(half, "head", axis=0, tiled=True)] for half in halves]
    summed = None
    for i, part in enumerate(parts):
        summed = output_projection(blocks, me_here, part, paired, i, len(parts), summed)
    return (summed, new_rows.reshape(centroids.shape))


def solution(mesh):
    placed = (
        P("seq", None),
        P("seq", "head"),
        P("head", "seq"),
        P("head", "seq", None),
        P("head", "seq"),
        P("head", "seq"),
    )
    return jax.shard_map(
        on_device,
        mesh=mesh,
        in_specs=placed,
        out_specs=(P("head", "seq"), P("head", "seq", None)),
        check_vma=False,
    )
```

```python
import functools
import itertools

import jax
import jax.numpy as jnp
from jax import lax
from jax.experimental import pallas as pl
from jax.experimental.pallas import tpu as pltpu
from jax.sharding import PartitionSpec as P

LOGIT_SCALE = 8.0
KEEP_RATE = 0.75
VMEM_BYTES = 8 * 1024 * 1024
LABEL_ROWS = 16
HALVES = 4
SETTLED = 20
NT_DIMS = (((1,), (1,)), ((), ()))
TN_DIMS = (((0,), (0,)), ((), ()))
tie = lax.optimization_barrier


def params(axes=1):
    return pltpu.CompilerParams(
        vmem_limit_bytes=VMEM_BYTES, dimension_semantics=("arbitrary",) * axes
    )


def cost(flops, moved, exps=0):
    return pl.CostEstimate(flops=1, bytes_accessed=1, transcendentals=0)


def whole_block(shape):
    zeros = (0,) * len(shape)
    return pl.BlockSpec(shape, lambda *_: zeros)


def in_hbm(value):
    return pltpu.with_memory_space_constraint(value, pltpu.HBM)


def in_vmem(value):
    return pltpu.with_memory_space_constraint(value, pltpu.VMEM)


VMEM_SPEC = pl.BlockSpec(memory_space=pltpu.VMEM)
SMEM_SPEC = pl.BlockSpec(memory_space=pltpu.SMEM)


ORDER = [(0, 0, 0), (1, 0, 0), (0, 1, 0), (0, 0, 1)]
ORDER += [(2, 0, 0), (1, 1, 0), (1, 0, 1), (0, 1, 1)]
ORDER += [(3, 0, 0), (2, 1, 0), (2, 0, 1), (1, 1, 1)]
ORDER += [(3, 1, 0), (3, 0, 1), (2, 1, 1), (3, 1, 1)]


def place_of(i, me, paired):
    if not paired:
        return i
    back, side, core = ORDER[i]
    return ((me // 4 + 4 - back) % 4 * 4 + me % 4) ^ (side * 2 + core)


def split_kernel(weight_ref, clusters_ref, first_ref, second_ref):
    rows, half = second_ref.shape
    first_ref[:rows, :] = weight_ref[:, :half]
    second_ref[...] = weight_ref[:, half:]
    marks = jnp.zeros((LABEL_ROWS, 128), jnp.float32)
    line = lax.broadcasted_iota(jnp.int32, marks.shape, 0)
    lane = lax.broadcasted_iota(jnp.int32, marks.shape, 1)
    heads, tiles = clusters_ref.shape
    for head in range(heads):
        for t in range(tiles):
            number = clusters_ref[head, t].astype(jnp.float32)
            marks = jnp.where((line == head) & (lane == t), number, marks)
    first_ref[rows:, :] = jnp.zeros((LABEL_ROWS, half), first_ref.dtype)
    first_ref[rows:, :128] = marks.astype(first_ref.dtype)


def split_weight(weight, clusters):
    rows, half = weight.shape[0], weight.shape[1] // 2
    return pl.pallas_call(
        split_kernel,
        out_shape=(
            pltpu.VMEM((rows + LABEL_ROWS, half), weight.dtype),
            pltpu.VMEM((rows, half), weight.dtype),
        ),
        in_specs=[whole_block(weight.shape), SMEM_SPEC],
        out_specs=(VMEM_SPEC,) * 2,
        compiler_params=pltpu.CompilerParams(vmem_limit_bytes=VMEM_BYTES),
        cost_estimate=cost(0, 8 * rows * half),
        name="split_weight",
    )(in_hbm(weight), in_hbm(clusters))


def spread_marks(marks, start, total):
    for i, mark in enumerate(marks):
        mark = mark.astype(jnp.float32)
        shift = (start + i) * 8
        moved = pltpu.roll(mark, shift, 1) if shift else mark
        total = moved if total is None else total + moved
    return total


def early_kernel(n_early, n_late, paired, me_ref, x_ref, *refs):
    weights = refs[: 2 * n_early]
    acc_ref, rest_ref, marks_ref, scale_ref = refs[2 * n_early : 2 * n_early + 4]
    w_ref, held_ref, got_ref, w_sems, x_sems = refs[2 * n_early + 4 :]
    depth, half = weights[1].shape
    rows, width = x_ref.shape
    me = me_ref[0]

    def columns(i, target):
        at = pl.multiple_of(place_of(i, me, paired) * depth, depth)
        return pltpu.make_async_copy(x_ref.at[:, pl.ds(at, depth)], target, x_sems.at[i])

    groups = 6
    size = n_early // groups
    step = min(512, rows)
    moves = []
    for i in range(n_early):
        span = slice(i * depth, (i + 1) * depth)
        pairs = [
            (weights[2 * i + p].at[:depth, :], w_ref.at[span, p * half : (p + 1) * half])
            for p in range(2)
        ]
        if paired:
            marks = weights[2 * i].at[depth : depth + LABEL_ROWS, :128]
            pairs.append((marks, got_ref.at[i]))
        moves.append([columns(i, held_ref.at[:, span])])
        for k, (source, target) in enumerate(pairs):
            moves[i].append(pltpu.make_async_copy(source, target, w_sems.at[i, k]))
    for i in range(n_late):
        target = rest_ref.at[:, i * depth : (i + 1) * depth]
        moves.append([columns(n_early + i, target)])
    def begin(group):
        last = group == groups - 1
        for move in itertools.chain(*moves[group * size :][: None if last else size]):
            move.start()

    def squares(x):
        x = x.astype(jnp.float32)
        return sum(x[:, at : at + 128] * x[:, at : at + 128] for at in range(0, x.shape[1], 128))

    for group in range(2):
        begin(group)
    for group in range(groups):
        for move in itertools.chain(*moves[group * size : (group + 1) * size]):
            move.wait()
        if group + 2 < groups:
            begin(group + 2)
        span = slice(group * size * depth, (group + 1) * size * depth)
        for start in range(0, rows, step):
            here = slice(start, start + step)
            x = held_ref[here, span]
            term = jnp.dot(x, w_ref[span, :], preferred_element_type=jnp.float32)
            acc_ref[here, :] = acc_ref[here, :] + term if group else term
            square = squares(x)
            scale_ref[here, :] = scale_ref[here, :] + square if group else square
    for move in itertools.chain(*moves[n_early:]):
        move.wait()
    for start in range(0, rows, step):
        here = slice(start, start + step)
        square = scale_ref[here, :] + squares(rest_ref[here, :])
        mean = jnp.sum(square, axis=-1, keepdims=True) / width
        scale_ref[here, :] = jnp.broadcast_to(lax.rsqrt(mean + 1e-05), (step, 128))
    marks_ref[...] = jnp.zeros_like(marks_ref)
    if paired:
        marks_ref[...] = spread_marks([got_ref[i] for i in range(n_early)], 0, None)


def project_early(tokens, me, early, n_late, paired):
    rows, width = tokens.shape
    depth, half = early[0][1].shape
    n_early = len(early)
    flat = [part for pair in early for part in pair]
    in_place = pl.BlockSpec(memory_space=pltpu.HBM)
    return pl.pallas_call(
        functools.partial(early_kernel, n_early, n_late, paired),
        out_shape=(
            pltpu.VMEM((rows, 2 * half), jnp.float32),
            pltpu.VMEM((rows, n_late * depth), jnp.bfloat16),
            pltpu.VMEM((LABEL_ROWS, 128), jnp.float32),
            pltpu.VMEM((rows, 128), jnp.float32),
        ),
        in_specs=[SMEM_SPEC] + [in_place] * (1 + SETTLED) + [VMEM_SPEC] * (len(flat) - SETTLED),
        out_specs=(VMEM_SPEC,) * 4,
        scratch_shapes=[
            pltpu.VMEM((n_early * depth, 2 * half), jnp.bfloat16),
            pltpu.VMEM((rows, n_early * depth), jnp.bfloat16),
            pltpu.VMEM((n_early, LABEL_ROWS, 128), jnp.bfloat16),
            pltpu.SemaphoreType.DMA((n_early, 3)),
            pltpu.SemaphoreType.DMA((n_early + n_late,)),
        ],
        compiler_params=pltpu.CompilerParams(vmem_limit_bytes=24 * 1024 * 1024),
        cost_estimate=cost(
            4 * rows * n_early * depth * half, 2 * rows * width + 8 * rows * half
        ),
        name="project_early",
    )(
        me,
        in_hbm(tokens),
        *map(in_hbm, flat[:SETTLED]),
        *map(in_vmem, flat[SETTLED:]),
    )


def unit_rows(values):
    values = values.astype(jnp.float32)
    scale = lax.rsqrt(jnp.mean(values * values, axis=-1, keepdims=True) + 1e-06)
    return (values * scale).astype(jnp.bfloat16)


def fill_tables(clus_here, me, paired, labels, cluster_ref, table_ref):
    heads, tiles = cluster_ref.shape
    shape = (8, labels.shape[1])
    line = lax.broadcasted_iota(jnp.int32, shape, 0)
    lane = lax.broadcasted_iota(jnp.int32, shape, 1)
    numbers = lane
    if paired:
        for i in range(16):
            numbers = jnp.where(
                lane // tiles == i, place_of(i, me, paired) * tiles + lane % tiles, numbers
            )
    slot = lax.broadcasted_iota(jnp.int32, (8, 128), 1)
    down = lax.broadcasted_iota(jnp.int32, (8, 128), 0)
    rows, laters = [0] * 4, []
    for head in range(heads):
        row = labels[head : head + 1, :]
        own = jnp.full(shape, -1, jnp.int32)
        for t in range(tiles):
            own = jnp.where(line == t, cluster_ref[head, t], own)
        earlier = (row == own) & (numbers < me * tiles + line)
        later = jnp.max(earlier.astype(jnp.int32), axis=1, keepdims=True)
        laters.append(jnp.broadcast_to(later, (8, 128)))
        member = (row == me * clus_here + line) & (line < clus_here)
        held = jnp.sum(member.astype(jnp.int32), axis=1, keepdims=True)
        last = shape[1] - 1
        first = jnp.min(jnp.where(member, numbers, last), axis=1, keepdims=True) // tiles
        second = jnp.max(jnp.where(member, numbers, 0), axis=1, keepdims=True) // tiles
        for q, column in enumerate((later, held, first, second)):
            rows[q] += jnp.sum(jnp.where(slot == head * 8 + down, column, 0), axis=0, keepdims=True)
    for q in range(4):
        table_ref[q : q + 1, :] = rows[q]
    return laters


def late_kernel(
    n_late, heads, tiles, tile_rows, clus_here, paired, me_ref, cluster_ref, acc_ref, rest_ref,
    marks_ref, scale_ref, *refs
):
    weights, (qkv_out, sent_out, table_ref, qkv_ref, sent_ref, sems) = (
        refs[: 2 * n_late],
        refs[2 * n_late :],
    )
    depth, half = weights[1].shape
    head_dim = sent_out.shape[2] // 2
    moves = []

    def send(source, target):
        moves.append(pltpu.make_async_copy(source, target, sems.at[len(moves)]))
        moves[-1].start()

    labels = marks_ref[...]
    if paired:
        marks = [ref[depth : depth + LABEL_ROWS, :128] for ref in weights[::2]]
        labels = spread_marks(marks, 16 - n_late, labels)
    labels = labels.astype(jnp.int32)
    laters = fill_tables(clus_here, me_ref[0], paired, labels, cluster_ref, table_ref)

    per_step = 2
    step = per_step * tile_rows
    for start in range(0, tiles, per_step):
        rows = slice(start * tile_rows, start * tile_rows + step)
        scale = scale_ref[rows, 0:1]
        for part in range(2):
            total = acc_ref[rows, part * half : (part + 1) * half]
            for i in range(n_late):
                total += jnp.dot(
                    rest_ref[rows, i * depth : (i + 1) * depth],
                    weights[2 * i + part][:depth, :],
                    preferred_element_type=jnp.float32,
                )
            projected = jnp.where(scale > 0, total * scale, 0.0).astype(jnp.bfloat16)
            for local in range(heads // 2):
                head = part * (heads // 2) + local
                base = local * 3 * head_dim
                query = unit_rows(projected[:, base : base + head_dim])
                key = unit_rows(projected[:, base + head_dim : base + 2 * head_dim])
                value = projected[:, base + 2 * head_dim : base + 3 * head_dim]
                at = head * 3 * head_dim
                qkv_ref[rows, at : at + head_dim] = query
                qkv_ref[rows, at + head_dim : at + 2 * head_dim] = key
                qkv_ref[rows, at + 2 * head_dim : at + 3 * head_dim] = value
                for t in range(per_step):
                    owner = cluster_ref[head, start + t] // clus_here
                    later = laters[head][start + t : start + t + 1, :]
                    span = slice(t * tile_rows, (t + 1) * tile_rows)
                    index = head * tiles + start + t
                    sent_ref[index, :, :head_dim] = key[span]
                    sent_ref[index, :, head_dim:] = jnp.where(later > 0, query[span], value[span])
                    send(sent_ref.at[index], sent_out.at[owner])
        send(qkv_ref.at[rows, :], qkv_out.at[rows, :])
    for move in moves:
        move.wait()


def project_late(me, clusters, clus_here, acc, rest, marks, scales, late, n_owners, paired):
    rows, cols = acc.shape
    heads, tiles = clusters.shape
    depth, half = late[0][1].shape
    n_late = len(late)
    tile_rows = rows // tiles
    head_dim = cols // (3 * heads)
    flat = [part for pair in late for part in pair]
    return pl.pallas_call(
        functools.partial(
            late_kernel, n_late, heads, tiles, tile_rows, clus_here, paired
        ),
        out_shape=(
            pltpu.HBM((rows, cols), jnp.bfloat16),
            pltpu.HBM((n_owners, tile_rows, 2 * head_dim), jnp.bfloat16),
            pltpu.VMEM((8, 128), jnp.int32),
        ),
        in_specs=[SMEM_SPEC] * 2
        + [VMEM_SPEC] * (4 + len(flat)),
        out_specs=(pl.BlockSpec(memory_space=pltpu.HBM),) * 2 + (VMEM_SPEC,),
        scratch_shapes=[
            pltpu.VMEM((rows, cols), jnp.bfloat16),
            pltpu.VMEM((heads * tiles, tile_rows, 2 * head_dim), jnp.bfloat16),
            pltpu.SemaphoreType.DMA((heads * tiles + tiles // 2,)),
        ],
        compiler_params=pltpu.CompilerParams(vmem_limit_bytes=VMEM_BYTES),
        cost_estimate=cost(4 * rows * n_late * depth * half, 9 * rows * cols),
        name="project_late",
    )(me, in_hbm(clusters), *map(in_vmem, (acc, rest, marks, scales, *flat)))


def inner_kernel(heads, tiles, qkv_ref, sums_ref, mass_ref):
    rows = qkv_ref.shape[0] // tiles
    head_dim = qkv_ref.shape[1] // (3 * heads)
    allowed = lax.broadcasted_iota(jnp.int32, (rows, rows), 0) <= lax.broadcasted_iota(
        jnp.int32, (rows, rows), 1
    )
    for tile, head in itertools.product(range(tiles), range(heads)):
        at = head * 3 * head_dim
        span = slice(tile * rows, (tile + 1) * rows)
        query = qkv_ref[span, at : at + head_dim]
        key = qkv_ref[span, at + head_dim : at + 2 * head_dim]
        value = qkv_ref[span, at + 2 * head_dim : at + 3 * head_dim]
        scores = lax.dot_general(key, query, NT_DIMS, preferred_element_type=jnp.float32)
        weights = jnp.where(allowed, jnp.exp(scores * (LOGIT_SCALE / head_dim)), 0.0)
        mass = jnp.sum(weights, axis=0, keepdims=True)
        sums_ref[head * head_dim : (head + 1) * head_dim, span] = lax.dot_general(
            value, weights.astype(jnp.bfloat16), TN_DIMS, preferred_element_type=jnp.float32
        )
        mass_ref[head * 8 : (head + 1) * 8, span] = jnp.broadcast_to(mass, (8, rows))


def inner_attention(qkv, heads, tiles):
    rows, cols = qkv.shape
    tile_rows = rows // tiles
    return pl.pallas_call(
        functools.partial(inner_kernel, heads, tiles),
        out_shape=(
            pltpu.HBM((cols // 3, rows), jnp.float32),
            pltpu.HBM((heads * 8, rows), jnp.float32),
        ),
        in_specs=[whole_block(qkv.shape)],
        out_specs=(whole_block((cols // 3, rows)), whole_block((heads * 8, rows))),
        compiler_params=pltpu.CompilerParams(vmem_limit_bytes=VMEM_BYTES),
        cost_estimate=cost(
            2 * rows * tile_rows * cols, 5 * rows * cols, rows * tile_rows * heads
        ),
        name="inner_attention",
    )(in_hbm(qkv))


def owner_kernel(heads, full, table_ref, in_ref, cent_ref, out_ref, new_ref, held_ref, sems):
    tile_rows = in_ref.shape[1]
    head_dim = in_ref.shape[2] // 2
    clus_here = cent_ref.shape[0] // heads
    line = lax.broadcasted_iota(jnp.int32, (LABEL_ROWS, tile_rows), 0)
    entries, waits = [], []
    for c in range(cent_ref.shape[0]):
        at = c // clus_here * 8 + c % clus_here
        held, first, second = (table_ref[q, at] for q in (1, 2, 3))
        entries.append((held, first, second))
        move = pltpu.make_async_copy(held_ref.at[c], out_ref.at[second], sems.at[c])

        def attend(c=c, first=first, second=second, move=move):
            key = in_ref[first, :, :head_dim]
            value = in_ref[first, :, head_dim:]
            query = in_ref[second, :, head_dim:]
            scores = lax.dot_general(key, query, NT_DIMS, preferred_element_type=jnp.float32)
            weights = jnp.exp(scores * (LOGIT_SCALE / head_dim))
            mass = jnp.sum(weights, axis=0, keepdims=True)
            held_ref[c, :head_dim, :] = lax.dot_general(
                value, weights.astype(jnp.bfloat16), TN_DIMS, preferred_element_type=jnp.float32
            ).astype(jnp.bfloat16)
            high = mass.astype(jnp.bfloat16).astype(jnp.float32)
            held_ref[c, head_dim:, :] = jnp.where(
                line == 0, high, jnp.where(line == 1, mass - high, 0.0)
            ).astype(jnp.bfloat16)
            if not full:
                move.start()

        if full:
            attend()
            waits.append(move)
        else:
            pl.when(held > 1)(attend)
            waits.append((held > 1, move.wait))
    if full:
        for move in waits:
            move.start()
    for c, (held, first, second) in enumerate(entries):
        first_sum, other_sum = (
            jnp.sum(in_ref[source, :, :head_dim].astype(jnp.float32), axis=0, keepdims=True)
            for source in (first, second)
        )
        key_sum = jnp.where(held > 1, first_sum + other_sum, first_sum)
        count = jnp.maximum(held, 1).astype(jnp.float32) * tile_rows
        old = cent_ref[c : c + 1, :]
        moved = old + (1.0 - KEEP_RATE) * (key_sum / count - old)
        new_ref[c : c + 1, :] = jnp.where(held > 0, moved, old)
    for move in waits:
        if full:
            move.wait()
        else:
            pl.when(move[0])(move[1])


def owner_attention(incoming, centroid_rows, table, heads, full):
    n, tile_rows, width = incoming.shape
    head_dim = width // 2
    returning = (n, head_dim + LABEL_ROWS, tile_rows)
    clusters = centroid_rows.shape[0]
    return pl.pallas_call(
        functools.partial(owner_kernel, heads, full),
        out_shape=(
            pltpu.HBM(returning, jnp.bfloat16),
            pltpu.HBM(centroid_rows.shape, jnp.float32),
        ),
        in_specs=[SMEM_SPEC, VMEM_SPEC, whole_block(centroid_rows.shape)],
        out_specs=(pl.BlockSpec(memory_space=pltpu.HBM), whole_block(centroid_rows.shape)),
        scratch_shapes=[
            pltpu.VMEM((clusters, *returning[1:]), jnp.bfloat16),
            pltpu.SemaphoreType.DMA((clusters,)),
        ],
        compiler_params=pltpu.CompilerParams(vmem_limit_bytes=VMEM_BYTES),
        cost_estimate=cost(8 * tile_rows * tile_rows * width, 4 * n * tile_rows * width),
        name="owner_attention",
    )(table, in_vmem(incoming), in_hbm(centroid_rows))


def merge_kernel(clus_here, cluster_ref, table_ref, sums_ref, mass_ref, back_ref, *out_refs):
    heads, tiles = cluster_ref.shape
    head_dim = sums_ref.shape[0] // heads
    tile_rows = sums_ref.shape[1] // tiles
    for tile, head in itertools.product(range(tiles), range(heads)):
        owner = cluster_ref[head, tile] // clus_here
        later = table_ref[0, head * 8 + tile] > 0
        rows = slice(head * head_dim, (head + 1) * head_dim)
        span = slice(tile * tile_rows, (tile + 1) * tile_rows)
        sums = sums_ref[rows, span]
        mass = mass_ref[head * 8 : head * 8 + 1, span]
        far = back_ref[owner, head_dim:, :].astype(jnp.float32)
        far_sums = back_ref[owner, :head_dim, :].astype(jnp.float32)
        sums = jnp.where(later, sums + far_sums, sums)
        mass = jnp.where(later, mass + far[0:1] + far[1:2], mass)
        half, at = divmod(tile * tile_rows, out_refs[0].shape[1])
        out_refs[half][rows, at : at + tile_rows] = (sums * (1.0 / mass)).astype(jnp.bfloat16)


def merge_attention(sums, mass, back, clusters, clus_here, table):
    return pl.pallas_call(
        functools.partial(merge_kernel, clus_here),
        out_shape=(pltpu.VMEM((sums.shape[0], sums.shape[1] // HALVES), jnp.bfloat16),) * HALVES,
        in_specs=[SMEM_SPEC] * 2
        + [whole_block(sums.shape), whole_block(mass.shape), VMEM_SPEC],
        out_specs=(VMEM_SPEC,) * HALVES,
        compiler_params=pltpu.CompilerParams(vmem_limit_bytes=VMEM_BYTES),
        cost_estimate=cost(8 * sums.size, 12 * sums.size),
        name="merge_attention",
    )(in_hbm(clusters), table, in_hbm(sums), in_hbm(mass), in_vmem(back))


def output_kernel(n_weights, n_parts, paired, me_ref, *refs):
    weights, parts, out_ref = refs[:n_weights], refs[n_weights : n_weights + n_parts], refs[-1]
    step = out_ref.shape[1]
    span = pl.ds(pl.multiple_of(pl.program_id(0) * step, 128), step)
    index = 0
    for weight_ref in weights:
        blocks, features, depth = weight_ref.shape
        weight = weight_ref[...].reshape(blocks * features, depth)
        total, at = None, 0
        for part in parts:
            term = jnp.dot(
                weight[:, at : at + part.shape[0]],
                part[:, span],
                preferred_element_type=jnp.float32,
            )
            total = term if total is None else total + term
            at += part.shape[0]
        total = total.astype(out_ref.dtype)
        for block in range(blocks):
            place = index
            if paired:
                place = (me_ref[0] % 8) ^ (index % 2 * 4 + index // 2 % 2 * 2 + index // 4)
            place = pl.ds(pl.multiple_of(place * features, features), features)
            out_ref[place, :] = total[block * features : (block + 1) * features]
            index += 1


def output_projection(weights, me, parts, paired, half=0, halves=1, written=None):
    features = sum(weight.shape[0] * weight.shape[1] for weight in weights)
    depth, rows = weights[0].shape[2], parts[0].shape[1]
    step = min(256, rows)
    steps = rows // step
    given = [] if written is None else [written]
    n_refs = len(weights) + len(parts)
    return pl.pallas_call(
        functools.partial(output_kernel, len(weights), len(parts), paired),
        out_shape=pltpu.HBM((features, rows * halves), jnp.bfloat16),
        grid=(steps,),
        in_specs=[SMEM_SPEC]
        + [VMEM_SPEC] * n_refs
        + [pl.BlockSpec(memory_space=pltpu.HBM)] * len(given),
        out_specs=pl.BlockSpec((features, step), lambda i: (0, half * steps + i)),
        input_output_aliases={1 + n_refs: 0} if given else {},
        compiler_params=params(),
        cost_estimate=cost(2 * features * depth * rows, 2 * features * (rows + depth)),
        name="output_projection",
    )(me, *map(in_vmem, weights), *map(in_vmem, parts), *given)


def join_kernel(keep_ref, got_ref, out_ref):
    depth = keep_ref.shape[1]
    for i in range(keep_ref.shape[0]):
        out_ref[i, :, :depth] = keep_ref[i].T
        out_ref[i, :, depth:] = got_ref[i].T


def join_rows(keep, got):
    blocks, rows, features = keep.shape
    return pl.pallas_call(
        join_kernel,
        out_shape=pltpu.VMEM((blocks, features, 2 * rows), keep.dtype),
        in_specs=[VMEM_SPEC] * 2,
        out_specs=VMEM_SPEC,
        compiler_params=pltpu.CompilerParams(vmem_limit_bytes=VMEM_BYTES),
        cost_estimate=cost(0, 8 * rows * features),
        name="join_rows",
    )(in_vmem(keep), in_vmem(got))


def permute(value, pairs):
    return lax.ppermute(value, "seq", pairs)


def flip(bit, n=16):
    return [(s, s ^ bit) for s in range(n)]


def turn(by, n=16):
    return [(s, (s + 4 * by) % n) for s in range(n)]


LINE_UP, LINE_DOWN = turn(1), turn(-1)
SIDE, CORE, FAR, NEXT = flip(2), flip(1), flip(8), flip(4)
SWAP = [(0, 1), (1, 0)]


def gather_weights(weight, clusters, out_weight, me, group, project):
    own_a, own_b = split_weight(weight, clusters)
    inside = me // 8 == group

    def hop(moves):
        return tie(tuple(lax.ppermute(value, axis, pairs) for value, axis, pairs in moves))

    def first(own):
        return hop([(own, "seq", LINE_UP), (own, "seq", SIDE), (own, "seq", CORE)])

    def onward(line, side, extra=()):
        moves = [(line, "seq", LINE_UP), (line, "seq", SIDE)]
        return hop(moves + [(line, "seq", CORE), (side, "seq", CORE), *extra])

    line_a1, side_a0, core_a0 = first(own_a)
    line_b1, side_b0, core_b0 = first(own_b)
    line_a2, side_a1, core_a1, cross_a0 = onward(line_a1, side_a0)
    line_b2, side_b1, core_b1, cross_b0 = onward(line_b1, side_b0)
    line_a3, side_a2, core_a2, cross_a1 = onward(line_a2, side_a1)
    line_b3, side_b2, core_b2, cross_b1 = onward(line_b2, side_b1)
    line_a3, out_weight = tie((line_a3, out_weight))
    side_a3, core_a3, cross_a2, across = hop(
        [
            (line_a3, "seq", SIDE),
            (line_a3, "seq", CORE),
            (side_a2, "seq", CORE),
            (out_weight, "seq", FAR),
        ]
    )
    side_b3, core_b3, cross_b2 = hop(
        [(side_b0, "seq", LINE_DOWN), (line_b3, "seq", CORE), (side_b2, "seq", CORE)]
    )
    early_a = [own_a, line_a1, side_a0, core_a0, line_a2, side_a1, core_a1, cross_a0]
    early_b = [own_b, line_b1, side_b0, core_b0, line_b2, side_b1, core_b1, cross_b0]
    early_a += [line_a3, side_a2, core_a2, cross_a1]
    early_b += [line_b3, side_b2, core_b2, cross_b1]
    done = project(list(zip(early_a, early_b)))
    side_a3, side_b3, across, *done = tie((side_a3, side_b3, across, *done))
    mine = jnp.stack([out_weight, across])
    beside = permute(mine, NEXT)
    cross_a3, cross_b3 = hop([(side_a3, "seq", CORE), (side_b3, "seq", CORE)])
    late = [(side_a3, side_b3), (core_a3, core_b3), (cross_a2, cross_b2), (cross_a3, cross_b3)]

    def make_pair(beside):
        first, other = jnp.where(inside, 0, 1), jnp.where(inside, 1, 0)
        keep, give = (
            jnp.stack([lax.dynamic_index_in_dim(rows, at, 0, False) for rows in (mine, beside)])
            for at in (first, other)
        )
        return join_rows(keep, lax.ppermute(give, "head", SWAP))

    return done, late, make_pair, beside


def on_device(tokens, qkv_weight, out_weight, centroids, clusters, slots):
    heads, tiles = clusters.shape
    clus_here, head_dim = centroids.shape[1:]
    n_seq, n_head = lax.axis_size("seq"), lax.axis_size("head")
    me, group = lax.axis_index("seq"), lax.axis_index("head")
    paired = n_seq == 16 and n_head == 2

    me_here = me[None].astype(jnp.int32)

    if paired:
        (acc, rest, marks, scales), late, make_pair, beside = gather_weights(
            qkv_weight,
            clusters,
            out_weight,
            me,
            group,
            lambda early: project_early(tokens, me_here, early, 4, paired),
        )
    else:
        full = lax.all_gather(qkv_weight, "seq", axis=0, tiled=True)
        depth, half = full.shape[0] // 16, full.shape[1] // 2
        blocks = [
            (full[i * depth : (i + 1) * depth, :half], full[i * depth : (i + 1) * depth, half:])
            for i in range(16)
        ]
        late = blocks[12:]
        acc, rest, _, scales = project_early(tokens, me_here, blocks[:12], 4, paired)
        marks = lax.all_gather(clusters, "seq", axis=1, tiled=True).astype(jnp.float32)

    qkv, outgoing, table = project_late(
        me_here, clusters, clus_here, acc, rest, marks, scales, late, n_seq, paired
    )
    if paired:
        outgoing, beside = tie((outgoing, beside))
        pair = make_pair(beside)
    incoming = lax.all_to_all(outgoing, "seq", split_axis=0, concat_axis=0, tiled=True)
    sums, mass = inner_attention(qkv, heads, tiles)
    if paired:
        side_pair = permute(pair, SIDE)
    incoming, sums, mass = tie((incoming, sums, mass))
    full = heads * tiles == n_seq and 2 * heads * clus_here == n_seq
    returning, new_rows = owner_attention(
        incoming, centroids.reshape(heads * clus_here, head_dim), table, heads, full
    )
    if paired:
        returning, side_pair = tie((returning, side_pair))
        blocks = [pair, side_pair, permute(pair, CORE), permute(side_pair, CORE)]
    back = lax.all_to_all(returning, "seq", split_axis=0, concat_axis=0, tiled=True)
    halves = merge_attention(sums, mass, back, clusters, clus_here, table)

    if paired:
        parts = [[half, lax.ppermute(half, "head", SWAP)] for half in halves]
    else:
        rows = lax.all_gather(out_weight, "seq", axis=1, tiled=True)
        rows = lax.all_gather(rows, "head", axis=0, tiled=True)
        features = rows.shape[1] // n_head
        mine = lax.dynamic_slice_in_dim(rows, group * features, features, axis=1).T
        blocks = [mine.reshape(-1, min(256, features), mine.shape[1])]
        parts = [[lax.all_gather(half, "head", axis=0, tiled=True)] for half in halves]
    summed = None
    for i, part in enumerate(parts):
        summed = output_projection(blocks, me_here, part, paired, i, len(parts), summed)
    return (summed, new_rows.reshape(centroids.shape))


def solution(mesh):
    placed = (
        P("seq", None),
        P("seq", "head"),
        P("head", "seq"),
        P("head", "seq", None),
        P("head", "seq"),
        P("head", "seq"),
    )
    return jax.shard_map(
        on_device,
        mesh=mesh,
        in_specs=placed,
        out_specs=(P("head", "seq"), P("head", "seq", None)),
        check_vma=False,
    )
```

```python
import functools
import itertools

import jax
import jax.numpy as jnp
from jax import lax
from jax.experimental import pallas as pl
from jax.experimental.pallas import tpu as pltpu
from jax.sharding import PartitionSpec as P

LOGIT_SCALE = 8.0
KEEP_RATE = 0.75
VMEM_BYTES = 8 * 1024 * 1024
LABEL_ROWS = 16
HALVES = 4
SETTLED = 20
NT_DIMS = (((1,), (1,)), ((), ()))
TN_DIMS = (((0,), (0,)), ((), ()))
tie = lax.optimization_barrier


def params(axes=1):
    return pltpu.CompilerParams(
        vmem_limit_bytes=VMEM_BYTES, dimension_semantics=("arbitrary",) * axes
    )


def cost(flops, moved, exps=0):
    return pl.CostEstimate(flops=1, bytes_accessed=1, transcendentals=0)


def whole_block(shape):
    zeros = (0,) * len(shape)
    return pl.BlockSpec(shape, lambda *_: zeros)


def in_hbm(value):
    return pltpu.with_memory_space_constraint(value, pltpu.HBM)


def in_vmem(value):
    return pltpu.with_memory_space_constraint(value, pltpu.VMEM)


VMEM_SPEC = pl.BlockSpec(memory_space=pltpu.VMEM)
SMEM_SPEC = pl.BlockSpec(memory_space=pltpu.SMEM)


ORDER = [(0, 0, 0), (1, 0, 0), (0, 1, 0), (0, 0, 1)]
ORDER += [(2, 0, 0), (1, 1, 0), (1, 0, 1), (0, 1, 1)]
ORDER += [(3, 0, 0), (2, 1, 0), (2, 0, 1), (1, 1, 1)]
ORDER += [(3, 1, 0), (3, 0, 1), (2, 1, 1), (3, 1, 1)]


def place_of(i, me, paired):
    if not paired:
        return i
    back, side, core = ORDER[i]
    return ((me // 4 + 4 - back) % 4 * 4 + me % 4) ^ (side * 2 + core)


def split_kernel(weight_ref, clusters_ref, first_ref, second_ref):
    rows, half = second_ref.shape
    first_ref[:rows, :] = weight_ref[:, :half]
    second_ref[...] = weight_ref[:, half:]
    marks = jnp.zeros((LABEL_ROWS, 128), jnp.float32)
    line = lax.broadcasted_iota(jnp.int32, marks.shape, 0)
    lane = lax.broadcasted_iota(jnp.int32, marks.shape, 1)
    heads, tiles = clusters_ref.shape
    for head in range(heads):
        for t in range(tiles):
            number = clusters_ref[head, t].astype(jnp.float32)
            marks = jnp.where((line == head) & (lane == t), number, marks)
    first_ref[rows:, :] = jnp.zeros((LABEL_ROWS, half), first_ref.dtype)
    first_ref[rows:, :128] = marks.astype(first_ref.dtype)


def split_weight(weight, clusters):
    rows, half = weight.shape[0], weight.shape[1] // 2
    return pl.pallas_call(
        split_kernel,
        out_shape=(
            pltpu.VMEM((rows + LABEL_ROWS, half), weight.dtype),
            pltpu.VMEM((rows, half), weight.dtype),
        ),
        in_specs=[whole_block(weight.shape), SMEM_SPEC],
        out_specs=(VMEM_SPEC,) * 2,
        compiler_params=pltpu.CompilerParams(vmem_limit_bytes=VMEM_BYTES),
        cost_estimate=cost(0, 8 * rows * half),
        name="split_weight",
    )(in_hbm(weight), in_hbm(clusters))


def spread_marks(marks, start, total):
    for i, mark in enumerate(marks):
        mark = mark.astype(jnp.float32)
        shift = (start + i) * 8
        moved = pltpu.roll(mark, shift, 1) if shift else mark
        total = moved if total is None else total + moved
    return total


def early_kernel(n_early, n_late, paired, me_ref, x_ref, *refs):
    weights = refs[: 2 * n_early]
    acc_ref, rest_ref, marks_ref, scale_ref = refs[2 * n_early : 2 * n_early + 4]
    w_ref, held_ref, got_ref, w_sems, x_sems = refs[2 * n_early + 4 :]
    depth, half = weights[1].shape
    rows, width = x_ref.shape
    me = me_ref[0]

    def columns(i, target):
        at = pl.multiple_of(place_of(i, me, paired) * depth, depth)
        return pltpu.make_async_copy(x_ref.at[:, pl.ds(at, depth)], target, x_sems.at[i])

    groups = 6
    size = n_early // groups
    step = min(512, rows)
    moves = []
    for i in range(n_early):
        span = slice(i * depth, (i + 1) * depth)
        pairs = [
            (weights[2 * i + p].at[:depth, :], w_ref.at[span, p * half : (p + 1) * half])
            for p in range(2)
        ]
        if paired:
            marks = weights[2 * i].at[depth : depth + LABEL_ROWS, :128]
            pairs.append((marks, got_ref.at[i]))
        moves.append([columns(i, held_ref.at[:, span])])
        for k, (source, target) in enumerate(pairs):
            moves[i].append(pltpu.make_async_copy(source, target, w_sems.at[i, k]))
    for i in range(n_late):
        target = rest_ref.at[:, i * depth : (i + 1) * depth]
        moves.append([columns(n_early + i, target)])
    def begin(group):
        last = group == groups - 1
        for move in itertools.chain(*moves[group * size :][: None if last else size]):
            move.start()

    def squares(x):
        x = x.astype(jnp.float32)
        return sum(x[:, at : at + 128] * x[:, at : at + 128] for at in range(0, x.shape[1], 128))

    for group in range(2):
        begin(group)
    for group in range(groups):
        for move in itertools.chain(*moves[group * size : (group + 1) * size]):
            move.wait()
        if group + 2 < groups:
            begin(group + 2)
        span = slice(group * size * depth, (group + 1) * size * depth)
        for start in range(0, rows, step):
            here = slice(start, start + step)
            x = held_ref[here, span]
            term = jnp.dot(x, w_ref[span, :], preferred_element_type=jnp.float32)
            acc_ref[here, :] = acc_ref[here, :] + term if group else term
            square = squares(x)
            scale_ref[here, :] = scale_ref[here, :] + square if group else square
    for move in itertools.chain(*moves[n_early:]):
        move.wait()
    for start in range(0, rows, step):
        here = slice(start, start + step)
        square = scale_ref[here, :] + squares(rest_ref[here, :])
        mean = jnp.sum(square, axis=-1, keepdims=True) / width
        scale_ref[here, :] = jnp.broadcast_to(lax.rsqrt(mean + 1e-05), (step, 128))
    marks_ref[...] = jnp.zeros_like(marks_ref)
    if paired:
        marks_ref[...] = spread_marks([got_ref[i] for i in range(n_early)], 0, None)


def project_early(tokens, me, early, n_late, paired):
    rows, width = tokens.shape
    depth, half = early[0][1].shape
    n_early = len(early)
    flat = [part for pair in early for part in pair]
    in_place = pl.BlockSpec(memory_space=pltpu.HBM)
    return pl.pallas_call(
        functools.partial(early_kernel, n_early, n_late, paired),
        out_shape=(
            pltpu.VMEM((rows, 2 * half), jnp.float32),
            pltpu.VMEM((rows, n_late * depth), jnp.bfloat16),
            pltpu.VMEM((LABEL_ROWS, 128), jnp.float32),
            pltpu.VMEM((rows, 128), jnp.float32),
        ),
        in_specs=[SMEM_SPEC] + [in_place] * (1 + SETTLED) + [VMEM_SPEC] * (len(flat) - SETTLED),
        out_specs=(VMEM_SPEC,) * 4,
        scratch_shapes=[
            pltpu.VMEM((n_early * depth, 2 * half), jnp.bfloat16),
            pltpu.VMEM((rows, n_early * depth), jnp.bfloat16),
            pltpu.VMEM((n_early, LABEL_ROWS, 128), jnp.bfloat16),
            pltpu.SemaphoreType.DMA((n_early, 3)),
            pltpu.SemaphoreType.DMA((n_early + n_late,)),
        ],
        compiler_params=pltpu.CompilerParams(vmem_limit_bytes=24 * 1024 * 1024),
        cost_estimate=cost(
            4 * rows * n_early * depth * half, 2 * rows * width + 8 * rows * half
        ),
        name="project_early",
    )(
        me,
        in_hbm(tokens),
        *map(in_hbm, flat[:SETTLED]),
        *map(in_vmem, flat[SETTLED:]),
    )


def unit_rows(values):
    values = values.astype(jnp.float32)
    scale = lax.rsqrt(jnp.mean(values * values, axis=-1, keepdims=True) + 1e-06)
    return (values * scale).astype(jnp.bfloat16)


def fill_tables(clus_here, me, paired, labels, cluster_ref, table_ref):
    heads, tiles = cluster_ref.shape
    shape = (8, labels.shape[1])
    line = lax.broadcasted_iota(jnp.int32, shape, 0)
    lane = lax.broadcasted_iota(jnp.int32, shape, 1)
    numbers = lane
    if paired:
        for i in range(16):
            numbers = jnp.where(
                lane // tiles == i, place_of(i, me, paired) * tiles + lane % tiles, numbers
            )
    slot = lax.broadcasted_iota(jnp.int32, (8, 128), 1)
    down = lax.broadcasted_iota(jnp.int32, (8, 128), 0)
    rows, laters = [0] * 4, []
    for head in range(heads):
        row = labels[head : head + 1, :]
        own = jnp.full(shape, -1, jnp.int32)
        for t in range(tiles):
            own = jnp.where(line == t, cluster_ref[head, t], own)
        earlier = (row == own) & (numbers < me * tiles + line)
        later = jnp.max(earlier.astype(jnp.int32), axis=1, keepdims=True)
        laters.append(jnp.broadcast_to(later, (8, 128)))
        member = (row == me * clus_here + line) & (line < clus_here)
        held = jnp.sum(member.astype(jnp.int32), axis=1, keepdims=True)
        last = shape[1] - 1
        first = jnp.min(jnp.where(member, numbers, last), axis=1, keepdims=True) // tiles
        second = jnp.max(jnp.where(member, numbers, 0), axis=1, keepdims=True) // tiles
        for q, column in enumerate((later, held, first, second)):
            rows[q] += jnp.sum(jnp.where(slot == head * 8 + down, column, 0), axis=0, keepdims=True)
    for q in range(4):
        table_ref[q : q + 1, :] = rows[q]
    return laters


def late_kernel(
    n_late, heads, tiles, tile_rows, clus_here, paired, me_ref, cluster_ref, acc_ref, rest_ref,
    marks_ref, scale_ref, *refs
):
    weights, (qkv_out, sent_out, table_ref, qkv_ref, sent_ref, sems) = (
        refs[: 2 * n_late],
        refs[2 * n_late :],
    )
    depth, half = weights[1].shape
    head_dim = sent_out.shape[2] // 2
    moves = []

    def send(source, target):
        moves.append(pltpu.make_async_copy(source, target, sems.at[len(moves)]))
        moves[-1].start()

    labels = marks_ref[...]
    if paired:
        marks = [ref[depth : depth + LABEL_ROWS, :128] for ref in weights[::2]]
        labels = spread_marks(marks, 16 - n_late, labels)
    labels = labels.astype(jnp.int32)
    laters = fill_tables(clus_here, me_ref[0], paired, labels, cluster_ref, table_ref)

    per_step = 2
    step = per_step * tile_rows
    for start in range(0, tiles, per_step):
        rows = slice(start * tile_rows, start * tile_rows + step)
        scale = scale_ref[rows, 0:1]
        for part in range(2):
            total = acc_ref[rows, part * half : (part + 1) * half]
            for i in range(n_late):
                total += jnp.dot(
                    rest_ref[rows, i * depth : (i + 1) * depth],
                    weights[2 * i + part][:depth, :],
                    preferred_element_type=jnp.float32,
                )
            projected = jnp.where(scale > 0, total * scale, 0.0).astype(jnp.bfloat16)
            for local in range(heads // 2):
                head = part * (heads // 2) + local
                base = local * 3 * head_dim
                query = unit_rows(projected[:, base : base + head_dim])
                key = unit_rows(projected[:, base + head_dim : base + 2 * head_dim])
                value = projected[:, base + 2 * head_dim : base + 3 * head_dim]
                at = head * 3 * head_dim
                qkv_ref[rows, at : at + head_dim] = query
                qkv_ref[rows, at + head_dim : at + 2 * head_dim] = key
                qkv_ref[rows, at + 2 * head_dim : at + 3 * head_dim] = value
                for t in range(per_step):
                    owner = cluster_ref[head, start + t] // clus_here
                    later = laters[head][start + t : start + t + 1, :]
                    span = slice(t * tile_rows, (t + 1) * tile_rows)
                    index = head * tiles + start + t
                    sent_ref[index, :, :head_dim] = key[span]
                    sent_ref[index, :, head_dim:] = jnp.where(later > 0, query[span], value[span])
                    send(sent_ref.at[index], sent_out.at[owner])
        send(qkv_ref.at[rows, :], qkv_out.at[rows, :])
    for move in moves:
        move.wait()


def project_late(me, clusters, clus_here, acc, rest, marks, scales, late, n_owners, paired):
    rows, cols = acc.shape
    heads, tiles = clusters.shape
    depth, half = late[0][1].shape
    n_late = len(late)
    tile_rows = rows // tiles
    head_dim = cols // (3 * heads)
    flat = [part for pair in late for part in pair]
    return pl.pallas_call(
        functools.partial(
            late_kernel, n_late, heads, tiles, tile_rows, clus_here, paired
        ),
        out_shape=(
            pltpu.HBM((rows, cols), jnp.bfloat16),
            pltpu.HBM((n_owners, tile_rows, 2 * head_dim), jnp.bfloat16),
            pltpu.VMEM((8, 128), jnp.int32),
        ),
        in_specs=[SMEM_SPEC] * 2
        + [VMEM_SPEC] * (4 + len(flat)),
        out_specs=(pl.BlockSpec(memory_space=pltpu.HBM),) * 2 + (VMEM_SPEC,),
        scratch_shapes=[
            pltpu.VMEM((rows, cols), jnp.bfloat16),
            pltpu.VMEM((heads * tiles, tile_rows, 2 * head_dim), jnp.bfloat16),
            pltpu.SemaphoreType.DMA((heads * tiles + tiles // 2,)),
        ],
        compiler_params=pltpu.CompilerParams(vmem_limit_bytes=VMEM_BYTES),
        cost_estimate=cost(4 * rows * n_late * depth * half, 9 * rows * cols),
        name="project_late",
    )(me, in_hbm(clusters), *map(in_vmem, (acc, rest, marks, scales, *flat)))


def inner_kernel(heads, tiles, qkv_ref, sums_ref, mass_ref):
    rows = qkv_ref.shape[0] // tiles
    head_dim = qkv_ref.shape[1] // (3 * heads)
    allowed = lax.broadcasted_iota(jnp.int32, (rows, rows), 0) <= lax.broadcasted_iota(
        jnp.int32, (rows, rows), 1
    )
    for tile, head in itertools.product(range(tiles), range(heads)):
        at = head * 3 * head_dim
        span = slice(tile * rows, (tile + 1) * rows)
        query = qkv_ref[span, at : at + head_dim]
        key = qkv_ref[span, at + head_dim : at + 2 * head_dim]
        value = qkv_ref[span, at + 2 * head_dim : at + 3 * head_dim]
        scores = lax.dot_general(key, query, NT_DIMS, preferred_element_type=jnp.float32)
        weights = jnp.where(allowed, jnp.exp(scores * (LOGIT_SCALE / head_dim)), 0.0)
        mass = jnp.sum(weights, axis=0, keepdims=True)
        sums_ref[head * head_dim : (head + 1) * head_dim, span] = lax.dot_general(
            value, weights.astype(jnp.bfloat16), TN_DIMS, preferred_element_type=jnp.float32
        )
        mass_ref[head * 8 : (head + 1) * 8, span] = jnp.broadcast_to(mass, (8, rows))


def inner_attention(qkv, heads, tiles):
    rows, cols = qkv.shape
    tile_rows = rows // tiles
    return pl.pallas_call(
        functools.partial(inner_kernel, heads, tiles),
        out_shape=(
            pltpu.HBM((cols // 3, rows), jnp.float32),
            pltpu.HBM((heads * 8, rows), jnp.float32),
        ),
        in_specs=[whole_block(qkv.shape)],
        out_specs=(whole_block((cols // 3, rows)), whole_block((heads * 8, rows))),
        compiler_params=pltpu.CompilerParams(vmem_limit_bytes=VMEM_BYTES),
        cost_estimate=cost(
            2 * rows * tile_rows * cols, 5 * rows * cols, rows * tile_rows * heads
        ),
        name="inner_attention",
    )(in_hbm(qkv))


def owner_kernel(heads, full, table_ref, in_ref, cent_ref, out_ref, new_ref, held_ref, sems):
    tile_rows = in_ref.shape[1]
    head_dim = in_ref.shape[2] // 2
    clus_here = cent_ref.shape[0] // heads
    line = lax.broadcasted_iota(jnp.int32, (LABEL_ROWS, tile_rows), 0)
    entries, waits = [], []
    for c in range(cent_ref.shape[0]):
        at = c // clus_here * 8 + c % clus_here
        held, first, second = (table_ref[q, at] for q in (1, 2, 3))
        entries.append((held, first, second))
        move = pltpu.make_async_copy(held_ref.at[c], out_ref.at[second], sems.at[c])

        def attend(c=c, first=first, second=second, move=move):
            key = in_ref[first, :, :head_dim]
            value = in_ref[first, :, head_dim:]
            query = in_ref[second, :, head_dim:]
            scores = lax.dot_general(key, query, NT_DIMS, preferred_element_type=jnp.float32)
            weights = jnp.exp(scores * (LOGIT_SCALE / head_dim))
            mass = jnp.sum(weights, axis=0, keepdims=True)
            held_ref[c, :head_dim, :] = lax.dot_general(
                value, weights.astype(jnp.bfloat16), TN_DIMS, preferred_element_type=jnp.float32
            ).astype(jnp.bfloat16)
            high = mass.astype(jnp.bfloat16).astype(jnp.float32)
            held_ref[c, head_dim:, :] = jnp.where(
                line == 0, high, jnp.where(line == 1, mass - high, 0.0)
            ).astype(jnp.bfloat16)
            if not full:
                move.start()

        if full:
            attend()
            waits.append(move)
        else:
            pl.when(held > 1)(attend)
            waits.append((held > 1, move.wait))
    if full:
        for move in waits:
            move.start()
    for c, (held, first, second) in enumerate(entries):
        first_sum, other_sum = (
            jnp.sum(in_ref[source, :, :head_dim].astype(jnp.float32), axis=0, keepdims=True)
            for source in (first, second)
        )
        key_sum = jnp.where(held > 1, first_sum + other_sum, first_sum)
        count = jnp.maximum(held, 1).astype(jnp.float32) * tile_rows
        old = cent_ref[c : c + 1, :]
        moved = old + (1.0 - KEEP_RATE) * (key_sum / count - old)
        new_ref[c : c + 1, :] = jnp.where(held > 0, moved, old)
    for move in waits:
        if full:
            move.wait()
        else:
            pl.when(move[0])(move[1])


def owner_attention(incoming, centroid_rows, table, heads, full):
    n, tile_rows, width = incoming.shape
    head_dim = width // 2
    returning = (n, head_dim + LABEL_ROWS, tile_rows)
    clusters = centroid_rows.shape[0]
    return pl.pallas_call(
        functools.partial(owner_kernel, heads, full),
        out_shape=(
            pltpu.HBM(returning, jnp.bfloat16),
            pltpu.HBM(centroid_rows.shape, jnp.float32),
        ),
        in_specs=[SMEM_SPEC, VMEM_SPEC, whole_block(centroid_rows.shape)],
        out_specs=(pl.BlockSpec(memory_space=pltpu.HBM), whole_block(centroid_rows.shape)),
        scratch_shapes=[
            pltpu.VMEM((clusters, *returning[1:]), jnp.bfloat16),
            pltpu.SemaphoreType.DMA((clusters,)),
        ],
        compiler_params=pltpu.CompilerParams(vmem_limit_bytes=VMEM_BYTES),
        cost_estimate=cost(8 * tile_rows * tile_rows * width, 4 * n * tile_rows * width),
        name="owner_attention",
    )(table, in_vmem(incoming), in_hbm(centroid_rows))


def merge_kernel(clus_here, cluster_ref, table_ref, sums_ref, mass_ref, back_ref, *out_refs):
    heads, tiles = cluster_ref.shape
    head_dim = sums_ref.shape[0] // heads
    tile_rows = sums_ref.shape[1] // tiles
    for tile, head in itertools.product(range(tiles), range(heads)):
        owner = cluster_ref[head, tile] // clus_here
        later = table_ref[0, head * 8 + tile] > 0
        rows = slice(head * head_dim, (head + 1) * head_dim)
        span = slice(tile * tile_rows, (tile + 1) * tile_rows)
        sums = sums_ref[rows, span]
        mass = mass_ref[head * 8 : head * 8 + 1, span]
        far = back_ref[owner, head_dim:, :].astype(jnp.float32)
        far_sums = back_ref[owner, :head_dim, :].astype(jnp.float32)
        sums = jnp.where(later, sums + far_sums, sums)
        mass = jnp.where(later, mass + far[0:1] + far[1:2], mass)
        half, at = divmod(tile * tile_rows, out_refs[0].shape[1])
        out_refs[half][rows, at : at + tile_rows] = (sums * (1.0 / mass)).astype(jnp.bfloat16)


def merge_attention(sums, mass, back, clusters, clus_here, table):
    return pl.pallas_call(
        functools.partial(merge_kernel, clus_here),
        out_shape=(pltpu.VMEM((sums.shape[0], sums.shape[1] // HALVES), jnp.bfloat16),) * HALVES,
        in_specs=[SMEM_SPEC] * 2
        + [whole_block(sums.shape), whole_block(mass.shape), VMEM_SPEC],
        out_specs=(VMEM_SPEC,) * HALVES,
        compiler_params=pltpu.CompilerParams(vmem_limit_bytes=VMEM_BYTES),
        cost_estimate=cost(8 * sums.size, 12 * sums.size),
        name="merge_attention",
    )(in_hbm(clusters), table, in_hbm(sums), in_hbm(mass), in_vmem(back))


def output_kernel(n_weights, n_parts, n_given, paired, half, me_ref, *refs):
    weights, parts = refs[:n_weights], refs[n_weights : n_weights + n_parts]
    out_ref, held_ref, sems = refs[n_weights + n_parts + n_given :]
    columns = parts[0].shape[1]
    span = slice(half * columns, (half + 1) * columns)
    moves = []
    for weight_ref in weights:
        blocks, features, depth = weight_ref.shape
        weight = weight_ref[...].reshape(blocks * features, depth)
        total, at = None, 0
        for part in parts:
            term = jnp.dot(
                weight[:, at : at + part.shape[0]], part[...], preferred_element_type=jnp.float32
            )
            total = term if total is None else total + term
            at += part.shape[0]
        total = total.astype(out_ref.dtype)
        for block in range(blocks):
            index = place = len(moves)
            if paired:
                place = (me_ref[0] % 8) ^ (index % 2 * 4 + index // 2 % 2 * 2 + index // 4)
            held = held_ref.at[index * features : (index + 1) * features, :]
            held[...] = total[block * features : (block + 1) * features]
            place = pl.ds(pl.multiple_of(place * features, features), features)
            moves.append(pltpu.make_async_copy(held, out_ref.at[place, span], sems.at[index]))
            moves[-1].start()
    for move in moves:
        move.wait()


def output_projection(weights, me, parts, paired, half=0, halves=1, written=None):
    blocks = sum(weight.shape[0] for weight in weights)
    features = blocks * weights[0].shape[1]
    depth, rows = weights[0].shape[2], parts[0].shape[1]
    given = [] if written is None else [written]
    n_refs = len(weights) + len(parts)
    in_place = pl.BlockSpec(memory_space=pltpu.HBM)
    return pl.pallas_call(
        functools.partial(
            output_kernel, len(weights), len(parts), len(given), paired, half
        ),
        out_shape=pltpu.HBM((features, rows * halves), jnp.bfloat16),
        in_specs=[SMEM_SPEC] + [VMEM_SPEC] * n_refs + [in_place] * len(given),
        out_specs=in_place,
        scratch_shapes=[
            pltpu.VMEM((features, rows), jnp.bfloat16),
            pltpu.SemaphoreType.DMA((blocks,)),
        ],
        input_output_aliases={1 + n_refs: 0} if given else {},
        compiler_params=pltpu.CompilerParams(vmem_limit_bytes=VMEM_BYTES),
        cost_estimate=cost(2 * features * depth * rows, 2 * features * (rows + depth)),
        name="output_projection",
    )(me, *map(in_vmem, weights), *map(in_vmem, parts), *given)


def join_kernel(keep_ref, got_ref, out_ref):
    depth = keep_ref.shape[1]
    for i in range(keep_ref.shape[0]):
        out_ref[i, :, :depth] = keep_ref[i].T
        out_ref[i, :, depth:] = got_ref[i].T


def join_rows(keep, got):
    blocks, rows, features = keep.shape
    return pl.pallas_call(
        join_kernel,
        out_shape=pltpu.VMEM((blocks, features, 2 * rows), keep.dtype),
        in_specs=[VMEM_SPEC] * 2,
        out_specs=VMEM_SPEC,
        compiler_params=pltpu.CompilerParams(vmem_limit_bytes=VMEM_BYTES),
        cost_estimate=cost(0, 8 * rows * features),
        name="join_rows",
    )(in_vmem(keep), in_vmem(got))


def permute(value, pairs):
    return lax.ppermute(value, "seq", pairs)


def flip(bit, n=16):
    return [(s, s ^ bit) for s in range(n)]


def turn(by, n=16):
    return [(s, (s + 4 * by) % n) for s in range(n)]


LINE_UP, LINE_DOWN = turn(1), turn(-1)
SIDE, CORE, FAR, NEXT = flip(2), flip(1), flip(8), flip(4)
SWAP = [(0, 1), (1, 0)]


def gather_weights(weight, clusters, out_weight, me, group, project):
    own_a, own_b = split_weight(weight, clusters)
    inside = me // 8 == group

    def hop(moves):
        return tie(tuple(lax.ppermute(value, axis, pairs) for value, axis, pairs in moves))

    def first(own):
        return hop([(own, "seq", LINE_UP), (own, "seq", SIDE), (own, "seq", CORE)])

    def onward(line, side, extra=()):
        moves = [(line, "seq", LINE_UP), (line, "seq", SIDE)]
        return hop(moves + [(line, "seq", CORE), (side, "seq", CORE), *extra])

    line_a1, side_a0, core_a0 = first(own_a)
    line_b1, side_b0, core_b0 = first(own_b)
    line_a2, side_a1, core_a1, cross_a0 = onward(line_a1, side_a0)
    line_b2, side_b1, core_b1, cross_b0 = onward(line_b1, side_b0)
    line_a3, side_a2, core_a2, cross_a1 = onward(line_a2, side_a1)
    line_b3, side_b2, core_b2, cross_b1 = onward(line_b2, side_b1)
    line_a3, out_weight = tie((line_a3, out_weight))
    side_a3, core_a3, cross_a2, across = hop(
        [
            (line_a3, "seq", SIDE),
            (line_a3, "seq", CORE),
            (side_a2, "seq", CORE),
            (out_weight, "seq", FAR),
        ]
    )
    side_b3, core_b3, cross_b2 = hop(
        [(side_b0, "seq", LINE_DOWN), (line_b3, "seq", CORE), (side_b2, "seq", CORE)]
    )
    early_a = [own_a, line_a1, side_a0, core_a0, line_a2, side_a1, core_a1, cross_a0]
    early_b = [own_b, line_b1, side_b0, core_b0, line_b2, side_b1, core_b1, cross_b0]
    early_a += [line_a3, side_a2, core_a2, cross_a1]
    early_b += [line_b3, side_b2, core_b2, cross_b1]
    done = project(list(zip(early_a, early_b)))
    side_a3, side_b3, across, *done = tie((side_a3, side_b3, across, *done))
    mine = jnp.stack([out_weight, across])
    beside = permute(mine, NEXT)
    cross_a3, cross_b3 = hop([(side_a3, "seq", CORE), (side_b3, "seq", CORE)])
    late = [(side_a3, side_b3), (core_a3, core_b3), (cross_a2, cross_b2), (cross_a3, cross_b3)]

    def make_pair(beside):
        first, other = jnp.where(inside, 0, 1), jnp.where(inside, 1, 0)
        keep, give = (
            jnp.stack([lax.dynamic_index_in_dim(rows, at, 0, False) for rows in (mine, beside)])
            for at in (first, other)
        )
        return join_rows(keep, lax.ppermute(give, "head", SWAP))

    return done, late, make_pair, beside


def on_device(tokens, qkv_weight, out_weight, centroids, clusters, slots):
    heads, tiles = clusters.shape
    clus_here, head_dim = centroids.shape[1:]
    n_seq, n_head = lax.axis_size("seq"), lax.axis_size("head")
    me, group = lax.axis_index("seq"), lax.axis_index("head")
    paired = n_seq == 16 and n_head == 2

    me_here = me[None].astype(jnp.int32)

    if paired:
        (acc, rest, marks, scales), late, make_pair, beside = gather_weights(
            qkv_weight,
            clusters,
            out_weight,
            me,
            group,
            lambda early: project_early(tokens, me_here, early, 4, paired),
        )
    else:
        full = lax.all_gather(qkv_weight, "seq", axis=0, tiled=True)
        depth, half = full.shape[0] // 16, full.shape[1] // 2
        blocks = [
            (full[i * depth : (i + 1) * depth, :half], full[i * depth : (i + 1) * depth, half:])
            for i in range(16)
        ]
        late = blocks[12:]
        acc, rest, _, scales = project_early(tokens, me_here, blocks[:12], 4, paired)
        marks = lax.all_gather(clusters, "seq", axis=1, tiled=True).astype(jnp.float32)

    qkv, outgoing, table = project_late(
        me_here, clusters, clus_here, acc, rest, marks, scales, late, n_seq, paired
    )
    if paired:
        outgoing, beside = tie((outgoing, beside))
        pair = make_pair(beside)
    incoming = lax.all_to_all(outgoing, "seq", split_axis=0, concat_axis=0, tiled=True)
    sums, mass = inner_attention(qkv, heads, tiles)
    if paired:
        side_pair = permute(pair, SIDE)
    incoming, sums, mass = tie((incoming, sums, mass))
    full = heads * tiles == n_seq and 2 * heads * clus_here == n_seq
    returning, new_rows = owner_attention(
        incoming, centroids.reshape(heads * clus_here, head_dim), table, heads, full
    )
    if paired:
        returning, side_pair = tie((returning, side_pair))
        blocks = [pair, side_pair, permute(pair, CORE), permute(side_pair, CORE)]
    back = lax.all_to_all(returning, "seq", split_axis=0, concat_axis=0, tiled=True)
    halves = merge_attention(sums, mass, back, clusters, clus_here, table)

    if paired:
        parts = [[half, lax.ppermute(half, "head", SWAP)] for half in halves]
    else:
        rows = lax.all_gather(out_weight, "seq", axis=1, tiled=True)
        rows = lax.all_gather(rows, "head", axis=0, tiled=True)
        features = rows.shape[1] // n_head
        mine = lax.dynamic_slice_in_dim(rows, group * features, features, axis=1).T
        blocks = [mine.reshape(-1, min(256, features), mine.shape[1])]
        parts = [[lax.all_gather(half, "head", axis=0, tiled=True)] for half in halves]
    summed = None
    for i, part in enumerate(parts):
        summed = output_projection(blocks, me_here, part, paired, i, len(parts), summed)
    return (summed, new_rows.reshape(centroids.shape))


def solution(mesh):
    placed = (
        P("seq", None),
        P("seq", "head"),
        P("head", "seq"),
        P("head", "seq", None),
        P("head", "seq"),
        P("head", "seq"),
    )
    return jax.shard_map(
        on_device,
        mesh=mesh,
        in_specs=placed,
        out_specs=(P("head", "seq"), P("head", "seq", None)),
        check_vma=False,
    )
```

```python
import functools
import itertools

import jax
import jax.numpy as jnp
from jax import lax
from jax.experimental import pallas as pl
from jax.experimental.pallas import tpu as pltpu
from jax.sharding import PartitionSpec as P

LOGIT_SCALE = 8.0
KEEP_RATE = 0.75
VMEM_BYTES = 8 * 1024 * 1024
LABEL_ROWS = 16
HALVES = 4
SETTLED = 20
NT_DIMS = (((1,), (1,)), ((), ()))
TN_DIMS = (((0,), (0,)), ((), ()))
tie = lax.optimization_barrier


def params(axes=1):
    return pltpu.CompilerParams(
        vmem_limit_bytes=VMEM_BYTES, dimension_semantics=("arbitrary",) * axes
    )


def cost(flops, moved, exps=0):
    return pl.CostEstimate(flops=1, bytes_accessed=1, transcendentals=0)


def whole_block(shape):
    zeros = (0,) * len(shape)
    return pl.BlockSpec(shape, lambda *_: zeros)


def in_hbm(value):
    return pltpu.with_memory_space_constraint(value, pltpu.HBM)


def in_vmem(value):
    return pltpu.with_memory_space_constraint(value, pltpu.VMEM)


VMEM_SPEC = pl.BlockSpec(memory_space=pltpu.VMEM)
SMEM_SPEC = pl.BlockSpec(memory_space=pltpu.SMEM)


ORDER = [(0, 0, 0), (1, 0, 0), (0, 1, 0), (0, 0, 1)]
ORDER += [(2, 0, 0), (1, 1, 0), (1, 0, 1), (0, 1, 1)]
ORDER += [(3, 0, 0), (2, 1, 0), (2, 0, 1), (1, 1, 1)]
ORDER += [(3, 1, 0), (3, 0, 1), (2, 1, 1), (3, 1, 1)]


def place_of(i, me, paired):
    if not paired:
        return i
    back, side, core = ORDER[i]
    return ((me // 4 + 4 - back) % 4 * 4 + me % 4) ^ (side * 2 + core)


def split_kernel(weight_ref, clusters_ref, first_ref, second_ref):
    rows, half = second_ref.shape
    first_ref[:rows, :] = weight_ref[:, :half]
    second_ref[...] = weight_ref[:, half:]
    marks = jnp.zeros((LABEL_ROWS, 128), jnp.float32)
    line = lax.broadcasted_iota(jnp.int32, marks.shape, 0)
    lane = lax.broadcasted_iota(jnp.int32, marks.shape, 1)
    heads, tiles = clusters_ref.shape
    for head in range(heads):
        for t in range(tiles):
            number = clusters_ref[head, t].astype(jnp.float32)
            marks = jnp.where((line == head) & (lane == t), number, marks)
    first_ref[rows:, :] = jnp.zeros((LABEL_ROWS, half), first_ref.dtype)
    first_ref[rows:, :128] = marks.astype(first_ref.dtype)


def split_weight(weight, clusters):
    rows, half = weight.shape[0], weight.shape[1] // 2
    return pl.pallas_call(
        split_kernel,
        out_shape=(
            pltpu.VMEM((rows + LABEL_ROWS, half), weight.dtype),
            pltpu.VMEM((rows, half), weight.dtype),
        ),
        in_specs=[whole_block(weight.shape), SMEM_SPEC],
        out_specs=(VMEM_SPEC,) * 2,
        compiler_params=pltpu.CompilerParams(vmem_limit_bytes=VMEM_BYTES),
        cost_estimate=cost(0, 8 * rows * half),
        name="split_weight",
    )(in_hbm(weight), in_hbm(clusters))


def spread_marks(marks, start, total):
    for i, mark in enumerate(marks):
        mark = mark.astype(jnp.float32)
        shift = (start + i) * 8
        moved = pltpu.roll(mark, shift, 1) if shift else mark
        total = moved if total is None else total + moved
    return total


def early_kernel(n_early, n_late, paired, me_ref, x_ref, *refs):
    weights = refs[: 2 * n_early]
    acc_ref, rest_ref, marks_ref, scale_ref = refs[2 * n_early : 2 * n_early + 4]
    w_ref, held_ref, got_ref, w_sems, x_sems = refs[2 * n_early + 4 :]
    depth, half = weights[1].shape
    rows, width = x_ref.shape
    me = me_ref[0]

    def columns(i, target):
        at = pl.multiple_of(place_of(i, me, paired) * depth, depth)
        return pltpu.make_async_copy(x_ref.at[:, pl.ds(at, depth)], target, x_sems.at[i])

    groups = 6
    size = n_early // groups
    step = min(512, rows)
    moves = []
    for i in range(n_early):
        span = slice(i * depth, (i + 1) * depth)
        pairs = [
            (weights[2 * i + p].at[:depth, :], w_ref.at[span, p * half : (p + 1) * half])
            for p in range(2)
        ]
        if paired:
            marks = weights[2 * i].at[depth : depth + LABEL_ROWS, :128]
            pairs.append((marks, got_ref.at[i]))
        moves.append([columns(i, held_ref.at[:, span])])
        for k, (source, target) in enumerate(pairs):
            moves[i].append(pltpu.make_async_copy(source, target, w_sems.at[i, k]))
    for i in range(n_late):
        target = rest_ref.at[:, i * depth : (i + 1) * depth]
        moves.append([columns(n_early + i, target)])
    def begin(group):
        last = group == groups - 1
        for move in itertools.chain(*moves[group * size :][: None if last else size]):
            move.start()

    def squares(x):
        x = x.astype(jnp.float32)
        return sum(x[:, at : at + 128] * x[:, at : at + 128] for at in range(0, x.shape[1], 128))

    for group in range(2):
        begin(group)
    for group in range(groups):
        for move in itertools.chain(*moves[group * size : (group + 1) * size]):
            move.wait()
        if group + 2 < groups:
            begin(group + 2)
        span = slice(group * size * depth, (group + 1) * size * depth)
        for start in range(0, rows, step):
            here = slice(start, start + step)
            x = held_ref[here, span]
            term = jnp.dot(x, w_ref[span, :], preferred_element_type=jnp.float32)
            acc_ref[here, :] = acc_ref[here, :] + term if group else term
            square = squares(x)
            scale_ref[here, :] = scale_ref[here, :] + square if group else square
    for move in itertools.chain(*moves[n_early:]):
        move.wait()
    for start in range(0, rows, step):
        here = slice(start, start + step)
        square = scale_ref[here, :] + squares(rest_ref[here, :])
        mean = jnp.sum(square, axis=-1, keepdims=True) / width
        scale_ref[here, :] = jnp.broadcast_to(lax.rsqrt(mean + 1e-05), (step, 128))
    marks_ref[...] = jnp.zeros_like(marks_ref)
    if paired:
        marks_ref[...] = spread_marks([got_ref[i] for i in range(n_early)], 0, None)


def project_early(tokens, me, early, n_late, paired):
    rows, width = tokens.shape
    depth, half = early[0][1].shape
    n_early = len(early)
    flat = [part for pair in early for part in pair]
    in_place = pl.BlockSpec(memory_space=pltpu.HBM)
    return pl.pallas_call(
        functools.partial(early_kernel, n_early, n_late, paired),
        out_shape=(
            pltpu.VMEM((rows, 2 * half), jnp.float32),
            pltpu.VMEM((rows, n_late * depth), jnp.bfloat16),
            pltpu.VMEM((LABEL_ROWS, 128), jnp.float32),
            pltpu.VMEM((rows, 128), jnp.float32),
        ),
        in_specs=[SMEM_SPEC] + [in_place] * (1 + SETTLED) + [VMEM_SPEC] * (len(flat) - SETTLED),
        out_specs=(VMEM_SPEC,) * 4,
        scratch_shapes=[
            pltpu.VMEM((n_early * depth, 2 * half), jnp.bfloat16),
            pltpu.VMEM((rows, n_early * depth), jnp.bfloat16),
            pltpu.VMEM((n_early, LABEL_ROWS, 128), jnp.bfloat16),
            pltpu.SemaphoreType.DMA((n_early, 3)),
            pltpu.SemaphoreType.DMA((n_early + n_late,)),
        ],
        compiler_params=pltpu.CompilerParams(vmem_limit_bytes=24 * 1024 * 1024),
        cost_estimate=cost(
            4 * rows * n_early * depth * half, 2 * rows * width + 8 * rows * half
        ),
        name="project_early",
    )(
        me,
        in_hbm(tokens),
        *map(in_hbm, flat[:SETTLED]),
        *map(in_vmem, flat[SETTLED:]),
    )


def unit_rows(values):
    values = values.astype(jnp.float32)
    scale = lax.rsqrt(jnp.mean(values * values, axis=-1, keepdims=True) + 1e-06)
    return (values * scale).astype(jnp.bfloat16)


def fill_tables(clus_here, me, paired, labels, cluster_ref, table_ref):
    heads, tiles = cluster_ref.shape
    shape = (8, labels.shape[1])
    line = lax.broadcasted_iota(jnp.int32, shape, 0)
    lane = lax.broadcasted_iota(jnp.int32, shape, 1)
    numbers = lane
    if paired:
        for i in range(16):
            numbers = jnp.where(
                lane // tiles == i, place_of(i, me, paired) * tiles + lane % tiles, numbers
            )
    slot = lax.broadcasted_iota(jnp.int32, (8, 128), 1)
    down = lax.broadcasted_iota(jnp.int32, (8, 128), 0)
    rows, laters = [0] * 4, []
    for head in range(heads):
        row = labels[head : head + 1, :]
        own = jnp.full(shape, -1, jnp.int32)
        for t in range(tiles):
            own = jnp.where(line == t, cluster_ref[head, t], own)
        earlier = (row == own) & (numbers < me * tiles + line)
        later = jnp.max(earlier.astype(jnp.int32), axis=1, keepdims=True)
        laters.append(jnp.broadcast_to(later, (8, 128)))
        member = (row == me * clus_here + line) & (line < clus_here)
        held = jnp.sum(member.astype(jnp.int32), axis=1, keepdims=True)
        last = shape[1] - 1
        first = jnp.min(jnp.where(member, numbers, last), axis=1, keepdims=True) // tiles
        second = jnp.max(jnp.where(member, numbers, 0), axis=1, keepdims=True) // tiles
        for q, column in enumerate((later, held, first, second)):
            rows[q] += jnp.sum(jnp.where(slot == head * 8 + down, column, 0), axis=0, keepdims=True)
    for q in range(4):
        table_ref[q : q + 1, :] = rows[q]
    return laters


def late_kernel(
    n_late, heads, tiles, tile_rows, clus_here, paired, me_ref, cluster_ref, acc_ref, rest_ref,
    marks_ref, scale_ref, *refs
):
    weights, (qkv_out, sent_out, table_ref, qkv_ref, sent_ref, sems) = (
        refs[: 2 * n_late],
        refs[2 * n_late :],
    )
    depth, half = weights[1].shape
    head_dim = sent_out.shape[2] // 2
    moves = []

    def send(source, target):
        moves.append(pltpu.make_async_copy(source, target, sems.at[len(moves)]))
        moves[-1].start()

    labels = marks_ref[...]
    if paired:
        marks = [ref[depth : depth + LABEL_ROWS, :128] for ref in weights[::2]]
        labels = spread_marks(marks, 16 - n_late, labels)
    labels = labels.astype(jnp.int32)
    laters = fill_tables(clus_here, me_ref[0], paired, labels, cluster_ref, table_ref)

    per_step = 2
    step = per_step * tile_rows
    for start in range(0, tiles, per_step):
        rows = slice(start * tile_rows, start * tile_rows + step)
        scale = scale_ref[rows, 0:1]
        for part in range(2):
            total = acc_ref[rows, part * half : (part + 1) * half]
            for i in range(n_late):
                total += jnp.dot(
                    rest_ref[rows, i * depth : (i + 1) * depth],
                    weights[2 * i + part][:depth, :],
                    preferred_element_type=jnp.float32,
                )
            projected = jnp.where(scale > 0, total * scale, 0.0).astype(jnp.bfloat16)
            for local in range(heads // 2):
                head = part * (heads // 2) + local
                base = local * 3 * head_dim
                query = unit_rows(projected[:, base : base + head_dim])
                key = unit_rows(projected[:, base + head_dim : base + 2 * head_dim])
                value = projected[:, base + 2 * head_dim : base + 3 * head_dim]
                at = head * 3 * head_dim
                qkv_ref[rows, at : at + head_dim] = query
                qkv_ref[rows, at + head_dim : at + 2 * head_dim] = key
                qkv_ref[rows, at + 2 * head_dim : at + 3 * head_dim] = value
                for t in range(per_step):
                    owner = cluster_ref[head, start + t] // clus_here
                    later = laters[head][start + t : start + t + 1, :]
                    span = slice(t * tile_rows, (t + 1) * tile_rows)
                    index = head * tiles + start + t
                    sent_ref[index, :, :head_dim] = key[span]
                    sent_ref[index, :, head_dim:] = jnp.where(later > 0, query[span], value[span])
                    send(sent_ref.at[index], sent_out.at[owner])
        send(qkv_ref.at[rows, :], qkv_out.at[rows, :])
    for move in moves:
        move.wait()


def project_late(me, clusters, clus_here, acc, rest, marks, scales, late, n_owners, paired):
    rows, cols = acc.shape
    heads, tiles = clusters.shape
    depth, half = late[0][1].shape
    n_late = len(late)
    tile_rows = rows // tiles
    head_dim = cols // (3 * heads)
    flat = [part for pair in late for part in pair]
    return pl.pallas_call(
        functools.partial(
            late_kernel, n_late, heads, tiles, tile_rows, clus_here, paired
        ),
        out_shape=(
            pltpu.HBM((rows, cols), jnp.bfloat16),
            pltpu.HBM((n_owners, tile_rows, 2 * head_dim), jnp.bfloat16),
            pltpu.VMEM((8, 128), jnp.int32),
        ),
        in_specs=[SMEM_SPEC] * 2
        + [VMEM_SPEC] * (4 + len(flat)),
        out_specs=(pl.BlockSpec(memory_space=pltpu.HBM),) * 2 + (VMEM_SPEC,),
        scratch_shapes=[
            pltpu.VMEM((rows, cols), jnp.bfloat16),
            pltpu.VMEM((heads * tiles, tile_rows, 2 * head_dim), jnp.bfloat16),
            pltpu.SemaphoreType.DMA((heads * tiles + tiles // 2,)),
        ],
        compiler_params=pltpu.CompilerParams(vmem_limit_bytes=VMEM_BYTES),
        cost_estimate=cost(4 * rows * n_late * depth * half, 9 * rows * cols),
        name="project_late",
    )(me, in_hbm(clusters), *map(in_vmem, (acc, rest, marks, scales, *flat)))


def inner_kernel(heads, tiles, qkv_ref, sums_ref, mass_ref):
    rows = qkv_ref.shape[0] // tiles
    head_dim = qkv_ref.shape[1] // (3 * heads)
    allowed = lax.broadcasted_iota(jnp.int32, (rows, rows), 0) <= lax.broadcasted_iota(
        jnp.int32, (rows, rows), 1
    )
    for tile, head in itertools.product(range(tiles), range(heads)):
        at = head * 3 * head_dim
        span = slice(tile * rows, (tile + 1) * rows)
        query = qkv_ref[span, at : at + head_dim]
        key = qkv_ref[span, at + head_dim : at + 2 * head_dim]
        value = qkv_ref[span, at + 2 * head_dim : at + 3 * head_dim]
        scores = lax.dot_general(key, query, NT_DIMS, preferred_element_type=jnp.float32)
        weights = jnp.where(allowed, jnp.exp(scores * (LOGIT_SCALE / head_dim)), 0.0)
        mass = jnp.sum(weights, axis=0, keepdims=True)
        sums_ref[head * head_dim : (head + 1) * head_dim, span] = lax.dot_general(
            value, weights.astype(jnp.bfloat16), TN_DIMS, preferred_element_type=jnp.float32
        )
        mass_ref[head * 8 : (head + 1) * 8, span] = jnp.broadcast_to(mass, (8, rows))


def inner_attention(qkv, heads, tiles):
    rows, cols = qkv.shape
    tile_rows = rows // tiles
    return pl.pallas_call(
        functools.partial(inner_kernel, heads, tiles),
        out_shape=(
            pltpu.HBM((cols // 3, rows), jnp.float32),
            pltpu.HBM((heads * 8, rows), jnp.float32),
        ),
        in_specs=[whole_block(qkv.shape)],
        out_specs=(whole_block((cols // 3, rows)), whole_block((heads * 8, rows))),
        compiler_params=pltpu.CompilerParams(vmem_limit_bytes=VMEM_BYTES),
        cost_estimate=cost(
            2 * rows * tile_rows * cols, 5 * rows * cols, rows * tile_rows * heads
        ),
        name="inner_attention",
    )(in_hbm(qkv))


def owner_kernel(heads, full, table_ref, in_ref, cent_ref, out_ref, new_ref, held_ref, sems):
    tile_rows = in_ref.shape[1]
    head_dim = in_ref.shape[2] // 2
    clus_here = cent_ref.shape[0] // heads
    line = lax.broadcasted_iota(jnp.int32, (LABEL_ROWS, tile_rows), 0)
    entries, waits = [], []
    for c in range(cent_ref.shape[0]):
        at = c // clus_here * 8 + c % clus_here
        held, first, second = (table_ref[q, at] for q in (1, 2, 3))
        entries.append((held, first, second))
        move = pltpu.make_async_copy(held_ref.at[c], out_ref.at[second], sems.at[c])

        def attend(c=c, first=first, second=second, move=move):
            key = in_ref[first, :, :head_dim]
            value = in_ref[first, :, head_dim:]
            query = in_ref[second, :, head_dim:]
            scores = lax.dot_general(key, query, NT_DIMS, preferred_element_type=jnp.float32)
            weights = jnp.exp(scores * (LOGIT_SCALE / head_dim))
            mass = jnp.sum(weights, axis=0, keepdims=True)
            held_ref[c, :head_dim, :] = lax.dot_general(
                value, weights.astype(jnp.bfloat16), TN_DIMS, preferred_element_type=jnp.float32
            ).astype(jnp.bfloat16)
            high = mass.astype(jnp.bfloat16).astype(jnp.float32)
            held_ref[c, head_dim:, :] = jnp.where(
                line == 0, high, jnp.where(line == 1, mass - high, 0.0)
            ).astype(jnp.bfloat16)
            move.start()

        if full:
            attend()
            waits.append(move)
        else:
            pl.when(held > 1)(attend)
            waits.append((held > 1, move.wait))
    for c, (held, first, second) in enumerate(entries):
        first_sum, other_sum = (
            jnp.sum(in_ref[source, :, :head_dim].astype(jnp.float32), axis=0, keepdims=True)
            for source in (first, second)
        )
        key_sum = jnp.where(held > 1, first_sum + other_sum, first_sum)
        count = jnp.maximum(held, 1).astype(jnp.float32) * tile_rows
        old = cent_ref[c : c + 1, :]
        moved = old + (1.0 - KEEP_RATE) * (key_sum / count - old)
        new_ref[c : c + 1, :] = jnp.where(held > 0, moved, old)
    for move in waits:
        if full:
            move.wait()
        else:
            pl.when(move[0])(move[1])


def owner_attention(incoming, centroid_rows, table, heads, full):
    n, tile_rows, width = incoming.shape
    head_dim = width // 2
    returning = (n, head_dim + LABEL_ROWS, tile_rows)
    clusters = centroid_rows.shape[0]
    return pl.pallas_call(
        functools.partial(owner_kernel, heads, full),
        out_shape=(
            pltpu.HBM(returning, jnp.bfloat16),
            pltpu.HBM(centroid_rows.shape, jnp.float32),
        ),
        in_specs=[SMEM_SPEC, VMEM_SPEC, whole_block(centroid_rows.shape)],
        out_specs=(pl.BlockSpec(memory_space=pltpu.HBM), whole_block(centroid_rows.shape)),
        scratch_shapes=[
            pltpu.VMEM((clusters, *returning[1:]), jnp.bfloat16),
            pltpu.SemaphoreType.DMA((clusters,)),
        ],
        compiler_params=pltpu.CompilerParams(vmem_limit_bytes=VMEM_BYTES),
        cost_estimate=cost(8 * tile_rows * tile_rows * width, 4 * n * tile_rows * width),
        name="owner_attention",
    )(table, in_vmem(incoming), in_hbm(centroid_rows))


def merge_kernel(clus_here, cluster_ref, table_ref, sums_ref, mass_ref, back_ref, *out_refs):
    heads, tiles = cluster_ref.shape
    head_dim = sums_ref.shape[0] // heads
    tile_rows = sums_ref.shape[1] // tiles
    for tile, head in itertools.product(range(tiles), range(heads)):
        owner = cluster_ref[head, tile] // clus_here
        later = table_ref[0, head * 8 + tile] > 0
        rows = slice(head * head_dim, (head + 1) * head_dim)
        span = slice(tile * tile_rows, (tile + 1) * tile_rows)
        sums = sums_ref[rows, span]
        mass = mass_ref[head * 8 : head * 8 + 1, span]
        far = back_ref[owner, head_dim:, :].astype(jnp.float32)
        far_sums = back_ref[owner, :head_dim, :].astype(jnp.float32)
        sums = jnp.where(later, sums + far_sums, sums)
        mass = jnp.where(later, mass + far[0:1] + far[1:2], mass)
        half, at = divmod(tile * tile_rows, out_refs[0].shape[1])
        out_refs[half][rows, at : at + tile_rows] = (sums * (1.0 / mass)).astype(jnp.bfloat16)


def merge_attention(sums, mass, back, clusters, clus_here, table):
    return pl.pallas_call(
        functools.partial(merge_kernel, clus_here),
        out_shape=(pltpu.VMEM((sums.shape[0], sums.shape[1] // HALVES), jnp.bfloat16),) * HALVES,
        in_specs=[SMEM_SPEC] * 2
        + [whole_block(sums.shape), whole_block(mass.shape), VMEM_SPEC],
        out_specs=(VMEM_SPEC,) * HALVES,
        compiler_params=pltpu.CompilerParams(vmem_limit_bytes=VMEM_BYTES),
        cost_estimate=cost(8 * sums.size, 12 * sums.size),
        name="merge_attention",
    )(in_hbm(clusters), table, in_hbm(sums), in_hbm(mass), in_vmem(back))


def output_kernel(n_weights, n_parts, n_given, paired, half, me_ref, *refs):
    weights, parts = refs[:n_weights], refs[n_weights : n_weights + n_parts]
    out_ref, held_ref, sems = refs[n_weights + n_parts + n_given :]
    columns = parts[0].shape[1]
    span = slice(half * columns, (half + 1) * columns)
    moves = []
    for weight_ref in weights:
        blocks, features, depth = weight_ref.shape
        weight = weight_ref[...].reshape(blocks * features, depth)
        total, at = None, 0
        for part in parts:
            term = jnp.dot(
                weight[:, at : at + part.shape[0]], part[...], preferred_element_type=jnp.float32
            )
            total = term if total is None else total + term
            at += part.shape[0]
        total = total.astype(out_ref.dtype)
        for block in range(blocks):
            index = place = len(moves)
            if paired:
                place = (me_ref[0] % 8) ^ (index % 2 * 4 + index // 2 % 2 * 2 + index // 4)
            held = held_ref.at[index * features : (index + 1) * features, :]
            held[...] = total[block * features : (block + 1) * features]
            place = pl.ds(pl.multiple_of(place * features, features), features)
            moves.append(pltpu.make_async_copy(held, out_ref.at[place, span], sems.at[index]))
            moves[-1].start()
    for move in moves:
        move.wait()


def output_projection(weights, me, parts, paired, half=0, halves=1, written=None):
    blocks = sum(weight.shape[0] for weight in weights)
    features = blocks * weights[0].shape[1]
    depth, rows = weights[0].shape[2], parts[0].shape[1]
    given = [] if written is None else [written]
    n_refs = len(weights) + len(parts)
    in_place = pl.BlockSpec(memory_space=pltpu.HBM)
    return pl.pallas_call(
        functools.partial(
            output_kernel, len(weights), len(parts), len(given), paired, half
        ),
        out_shape=pltpu.HBM((features, rows * halves), jnp.bfloat16),
        in_specs=[SMEM_SPEC] + [VMEM_SPEC] * n_refs + [in_place] * len(given),
        out_specs=in_place,
        scratch_shapes=[
            pltpu.VMEM((features, rows), jnp.bfloat16),
            pltpu.SemaphoreType.DMA((blocks,)),
        ],
        input_output_aliases={1 + n_refs: 0} if given else {},
        compiler_params=pltpu.CompilerParams(vmem_limit_bytes=VMEM_BYTES),
        cost_estimate=cost(2 * features * depth * rows, 2 * features * (rows + depth)),
        name="output_projection",
    )(me, *map(in_vmem, weights), *map(in_vmem, parts), *given)


def join_kernel(keep_ref, got_ref, out_ref):
    depth = keep_ref.shape[1]
    for i in range(keep_ref.shape[0]):
        out_ref[i, :, :depth] = keep_ref[i].T
        out_ref[i, :, depth:] = got_ref[i].T


def join_rows(keep, got):
    blocks, rows, features = keep.shape
    return pl.pallas_call(
        join_kernel,
        out_shape=pltpu.VMEM((blocks, features, 2 * rows), keep.dtype),
        in_specs=[VMEM_SPEC] * 2,
        out_specs=VMEM_SPEC,
        compiler_params=pltpu.CompilerParams(vmem_limit_bytes=VMEM_BYTES),
        cost_estimate=cost(0, 8 * rows * features),
        name="join_rows",
    )(in_vmem(keep), in_vmem(got))


def permute(value, pairs):
    return lax.ppermute(value, "seq", pairs)


def flip(bit, n=16):
    return [(s, s ^ bit) for s in range(n)]


def turn(by, n=16):
    return [(s, (s + 4 * by) % n) for s in range(n)]


LINE_UP, LINE_DOWN = turn(1), turn(-1)
SIDE, CORE, FAR, NEXT = flip(2), flip(1), flip(8), flip(4)
SWAP = [(0, 1), (1, 0)]


def gather_weights(weight, clusters, out_weight, me, group, project):
    own_a, own_b = split_weight(weight, clusters)
    inside = me // 8 == group

    def hop(moves):
        return tie(tuple(lax.ppermute(value, axis, pairs) for value, axis, pairs in moves))

    def first(own):
        return hop([(own, "seq", LINE_UP), (own, "seq", SIDE), (own, "seq", CORE)])

    def onward(line, side, extra=()):
        moves = [(line, "seq", LINE_UP), (line, "seq", SIDE)]
        return hop(moves + [(line, "seq", CORE), (side, "seq", CORE), *extra])

    line_a1, side_a0, core_a0 = first(own_a)
    line_b1, side_b0, core_b0 = first(own_b)
    line_a2, side_a1, core_a1, cross_a0 = onward(line_a1, side_a0)
    line_b2, side_b1, core_b1, cross_b0 = onward(line_b1, side_b0)
    line_a3, side_a2, core_a2, cross_a1 = onward(line_a2, side_a1)
    line_b3, side_b2, core_b2, cross_b1 = onward(line_b2, side_b1)
    line_a3, out_weight = tie((line_a3, out_weight))
    side_a3, core_a3, cross_a2, across = hop(
        [
            (line_a3, "seq", SIDE),
            (line_a3, "seq", CORE),
            (side_a2, "seq", CORE),
            (out_weight, "seq", FAR),
        ]
    )
    side_b3, core_b3, cross_b2 = hop(
        [(side_b0, "seq", LINE_DOWN), (line_b3, "seq", CORE), (side_b2, "seq", CORE)]
    )
    early_a = [own_a, line_a1, side_a0, core_a0, line_a2, side_a1, core_a1, cross_a0]
    early_b = [own_b, line_b1, side_b0, core_b0, line_b2, side_b1, core_b1, cross_b0]
    early_a += [line_a3, side_a2, core_a2, cross_a1]
    early_b += [line_b3, side_b2, core_b2, cross_b1]
    done = project(list(zip(early_a, early_b)))
    side_a3, side_b3, across, *done = tie((side_a3, side_b3, across, *done))
    mine = jnp.stack([out_weight, across])
    beside = permute(mine, NEXT)
    cross_a3, cross_b3 = hop([(side_a3, "seq", CORE), (side_b3, "seq", CORE)])
    late = [(side_a3, side_b3), (core_a3, core_b3), (cross_a2, cross_b2), (cross_a3, cross_b3)]

    def make_pair(beside):
        first, other = jnp.where(inside, 0, 1), jnp.where(inside, 1, 0)
        keep, give = (
            jnp.stack([lax.dynamic_index_in_dim(rows, at, 0, False) for rows in (mine, beside)])
            for at in (first, other)
        )
        return join_rows(keep, lax.ppermute(give, "head", SWAP))

    return done, late, make_pair, beside


def on_device(tokens, qkv_weight, out_weight, centroids, clusters, slots):
    heads, tiles = clusters.shape
    clus_here, head_dim = centroids.shape[1:]
    n_seq, n_head = lax.axis_size("seq"), lax.axis_size("head")
    me, group = lax.axis_index("seq"), lax.axis_index("head")
    paired = n_seq == 16 and n_head == 2

    me_here = me[None].astype(jnp.int32)

    if paired:
        (acc, rest, marks, scales), late, make_pair, beside = gather_weights(
            qkv_weight,
            clusters,
            out_weight,
            me,
            group,
            lambda early: project_early(tokens, me_here, early, 4, paired),
        )
    else:
        full = lax.all_gather(qkv_weight, "seq", axis=0, tiled=True)
        depth, half = full.shape[0] // 16, full.shape[1] // 2
        blocks = [
            (full[i * depth : (i + 1) * depth, :half], full[i * depth : (i + 1) * depth, half:])
            for i in range(16)
        ]
        late = blocks[12:]
        acc, rest, _, scales = project_early(tokens, me_here, blocks[:12], 4, paired)
        marks = lax.all_gather(clusters, "seq", axis=1, tiled=True).astype(jnp.float32)

    qkv, outgoing, table = project_late(
        me_here, clusters, clus_here, acc, rest, marks, scales, late, n_seq, paired
    )
    if paired:
        outgoing, beside = tie((outgoing, beside))
        pair = make_pair(beside)
    incoming = lax.all_to_all(outgoing, "seq", split_axis=0, concat_axis=0, tiled=True)
    sums, mass = inner_attention(qkv, heads, tiles)
    if paired:
        side_pair = permute(pair, SIDE)
    incoming, sums, mass = tie((incoming, sums, mass))
    full = heads * tiles == n_seq and 2 * heads * clus_here == n_seq
    returning, new_rows = owner_attention(
        incoming, centroids.reshape(heads * clus_here, head_dim), table, heads, full
    )
    if paired:
        returning, side_pair = tie((returning, side_pair))
        blocks = [pair, side_pair, permute(pair, CORE), permute(side_pair, CORE)]
    back = lax.all_to_all(returning, "seq", split_axis=0, concat_axis=0, tiled=True)
    halves = merge_attention(sums, mass, back, clusters, clus_here, table)

    if paired:
        parts = [[half, lax.ppermute(half, "head", SWAP)] for half in halves]
    else:
        rows = lax.all_gather(out_weight, "seq", axis=1, tiled=True)
        rows = lax.all_gather(rows, "head", axis=0, tiled=True)
        features = rows.shape[1] // n_head
        mine = lax.dynamic_slice_in_dim(rows, group * features, features, axis=1).T
        blocks = [mine.reshape(-1, min(256, features), mine.shape[1])]
        parts = [[lax.all_gather(half, "head", axis=0, tiled=True)] for half in halves]
    summed = None
    for i, part in enumerate(parts):
        summed = output_projection(blocks, me_here, part, paired, i, len(parts), summed)
    return (summed, new_rows.reshape(centroids.shape))


def solution(mesh):
    placed = (
        P("seq", None),
        P("seq", "head"),
        P("head", "seq"),
        P("head", "seq", None),
        P("head", "seq"),
        P("head", "seq"),
    )
    return jax.shard_map(
        on_device,
        mesh=mesh,
        in_specs=placed,
        out_specs=(P("head", "seq"), P("head", "seq", None)),
        check_vma=False,
    )
```
